32 devices in a mesh: ctx: 4 (over y, x), fsdp: 8 (over z, core).
Axes of the slice: x: 2, y: 2, z: 4, core: 2. Of those that a mesh axis runs over, the one named last changes fastest.
Arguments:
- tokens: bfloat16 [1024, 16, 768], P('ctx', 'fsdp'), may hold values from -6 to 6
- norm1_gain: bfloat16 [768], P('fsdp'), may hold values from 0.5 to 1.5
- norm1_bias: bfloat16 [768], P('fsdp'), may hold values from -4 to 4
- norm2_gain: bfloat16 [768], P('fsdp'), may hold values from 0.5 to 1.5
- norm2_bias: bfloat16 [768], P('fsdp'), may hold values from -4 to 4
- qkv_weight: bfloat16 [768, 2304], P('fsdp'), may hold values from -0.3125 to 0.3125
- qkv_bias: bfloat16 [2304], P('fsdp'), may hold values from -6 to 6
- out_weight: bfloat16 [768, 768], P('fsdp'), may hold values from -0.4375 to 0.4375
- out_bias: bfloat16 [768], P('fsdp'), may hold values from -6 to 6
- up_weight: bfloat16 [768, 3072], P('fsdp'), may hold values from -0.21875 to 0.21875
- up_bias: bfloat16 [3072], P('fsdp'), may hold values from -6 to 6
- down_weight: bfloat16 [3072, 768], P('fsdp'), may hold values from -0.15625 to 0.15625
- down_bias: bfloat16 [768], P('fsdp'), may hold values from -6 to 6
- cotangent: bfloat16 [1024, 16, 768], P('ctx', 'fsdp'), may hold values from -6 to 6
Outputs:
- layer_out: bfloat16 [1024, 16, 768], P('ctx', 'fsdp')
- tokens_grad: bfloat16 [1024, 16, 768], P('ctx', 'fsdp')
- norm1_gain_grad: float32 [768], P('fsdp')
- norm1_bias_grad: float32 [768], P('fsdp')
- norm2_gain_grad: float32 [768], P('fsdp')
- norm2_bias_grad: float32 [768], P('fsdp')
- qkv_weight_grad: float32 [768, 2304], P('fsdp')
- qkv_bias_grad: float32 [2304], P('fsdp')
- out_weight_grad: float32 [768, 768], P('fsdp')
- out_bias_grad: float32 [768], P('fsdp')
- up_weight_grad: float32 [768, 3072], P('fsdp')
- up_bias_grad: float32 [3072], P('fsdp')
- down_weight_grad: float32 [3072, 768], P('fsdp')
- down_bias_grad: float32 [768], P('fsdp')
The draws below stay inside these ranges and needn't reach their ends.
All inputs are finite; a program needn't handle non-finite values.
Results may differ from the reference program's by a relative error of at most 0.012.
The reference program's roundings to bfloat16 on the way count: a program that leaves them out, or rounds other values in their place, can miss the bound.
Values may be sent and summed in bfloat16 or wider, within the bound.
No kernel may reach another device: no remote copies, remote signals or barrier semaphores. Data moves between devices by JAX's collectives and lax.ppermute only.
A program may use at most 256 MiB of HBM per device.

```python
import jax
import jax.numpy as jnp
from jax import lax

D = 768
H = 12
HD = 64
ROT = 16
FF = 3072
BLK = 256
SEQ_LEN = 1024
SEQS = 16


def level_of(stream_key, extent, cuts, low, top_value):
    def one(axis_at, shards_of):
        steps = jax.random.uniform(jax.random.fold_in(jax.random.fold_in(stream_key, 6), axis_at), (shards_of,), jnp.float32, low / len(cuts), top_value / len(cuts))
        return jnp.repeat(jnp.exp(steps), extent[axis_at] // shards_of).reshape((-1,) + (1,) * (len(extent) - axis_at - 1))

    level = one(*cuts[0])
    for cut in cuts[1:]:
        level = level * one(*cut)
    return level


def gaussian(rng, dims, scale, limit, cuts=(), held_as=jnp.bfloat16):
    gain = level_of(rng, dims, cuts, -0.22, 0.18) if cuts else 1.0
    entries = jax.random.normal(rng, dims, jnp.float32) * scale * gain
    return jnp.minimum(jnp.maximum(entries, -limit), limit).astype(held_as)


def setup_inputs(seed: int = 0) -> dict:
    splits = jax.random.split(jax.random.key(seed), 15)
    return {
        "tokens": gaussian(splits[0], (SEQ_LEN, SEQS, D), 1.0, 6.0, ((0, 4), (1, 8))),
        "norm1_gain": jnp.clip(1.0 + 0.1 * jax.random.normal(splits[1], (D,), jnp.float32), 0.5, 1.5).astype(jnp.bfloat16),
        "norm1_bias": gaussian(splits[2], (D,), 0.3, 4.0, ((0, 8),)),
        "norm2_gain": jnp.clip(1.0 + 0.1 * jax.random.normal(splits[3], (D,), jnp.float32), 0.5, 1.5).astype(jnp.bfloat16),
        "norm2_bias": gaussian(splits[4], (D,), 0.3, 4.0, ((0, 8),)),
        "qkv_weight": gaussian(splits[5], (D, 3 * D), (D // 2) ** -0.5, 0.3125, ((0, 8),)),
        "qkv_bias": gaussian(splits[6], (3 * D,), 0.5, 6.0, ((0, 8),)),
        "out_weight": gaussian(splits[7], (D, D), (D // 4) ** -0.5, 0.4375, ((0, 8),)),
        "out_bias": gaussian(splits[8], (D,), 0.5, 6.0, ((0, 8),)),
        "up_weight": gaussian(splits[9], (D, FF), D ** -0.5, 0.21875, ((0, 8),)),
        "up_bias": gaussian(splits[10], (FF,), 0.5, 6.0, ((0, 8),)),
        "down_weight": gaussian(splits[11], (FF, D), (FF // 2) ** -0.5, 0.15625, ((0, 8),)),
        "down_bias": gaussian(splits[12], (D,), 0.5, 6.0, ((0, 8),)),
        "cotangent": gaussian(splits[13], (SEQ_LEN, SEQS, D), 1.0, 6.0, ((0, 4), (1, 8))),
    }


@jax.custom_vjp
def low(v):
    return lax.optimization_barrier(v.astype(jnp.bfloat16)).astype(jnp.float32)

@jax.custom_vjp
def low_back(v):
    return v

def low_keep(v):
    return (low(v), None)

def low_pass(kept, grad):
    return (grad,)

def back_keep(v):
    return (v, None)

def back_low(kept, grad):
    return (low(grad),)
low.defvjp(low_keep, low_pass)
low_back.defvjp(back_keep, back_low)
epsilon = 1e-05
masked_score = -1e+30

def layer_norm(inputs, gain_vec, bias_vec):
    center = inputs - lax.optimization_barrier(jnp.mean(inputs, axis=-1, keepdims=True))
    spread = lax.optimization_barrier(jnp.mean(center * center, axis=-1, keepdims=True))
    return center * lax.rsqrt(spread + epsilon) * gain_vec + bias_vec

def exact_gelu(values_in):
    return jax.nn.gelu(values_in, approximate=False)

def angles(positions):
    inverse = 10000.0 ** (-jnp.arange(0, ROT, 2, dtype=jnp.float32) / ROT)
    phase = positions[:, None] * inverse[None, :]
    phase = jnp.concatenate([phase, phase], axis=-1)
    return (jnp.cos(phase), jnp.sin(phase))

def rotate(values_in, cosine_table, sine_table):
    half_rot = ROT // 2
    part = values_in[..., :ROT]
    turned = jnp.concatenate([-part[..., half_rot:], part[..., :half_rot]], axis=-1)
    return jnp.concatenate([part * cosine_table + turned * sine_table, values_in[..., ROT:]], axis=-1)

def matmul(left, right):
    return jnp.dot(left, right, precision=lax.Precision.HIGHEST)

def attention(query_rot, key_rot, value_low):
    length = query_rot.shape[0]
    pieces = length // BLK
    score_scale = HD ** (-0.5)
    positions = jnp.arange(length, dtype=jnp.int32)

    def one_block(block_args):
        query_blk, query_pos = block_args
        scores = low_back(jnp.einsum('qhd,khd->hqk', query_blk, key_rot, precision=lax.Precision.HIGHEST) * score_scale)
        allowed = positions[None, :] <= query_pos[:, None]
        scores = jnp.where(allowed[None], scores, masked_score)
        top_score = lax.optimization_barrier(jnp.max(scores, axis=-1, keepdims=True))
        log_total = top_score + jnp.log(lax.optimization_barrier(jnp.sum(jnp.exp(scores - top_score), axis=-1, keepdims=True)))
        probs = low(jnp.exp(scores - log_total))
        return jnp.einsum('hqk,khd->qhd', probs, value_low, precision=lax.Precision.HIGHEST)
    blocks = lax.map(jax.checkpoint(one_block), (query_rot.reshape(pieces, BLK, H, HD), positions.reshape(pieces, BLK)))
    return blocks.reshape(length, H, HD)

def layer(sequence, params):
    gain_one, bias_one, gain_two, bias_two, weight_qkv, bias_qkv, weight_out, bias_out, weight_up, bias_up, weight_down, bias_down = params
    length = sequence.shape[0]
    normed_one = low(layer_norm(sequence, gain_one, bias_one))
    normed_two = low(layer_norm(sequence, gain_two, bias_two))
    projected = low_back(matmul(normed_one, weight_qkv) + bias_qkv)
    split = projected.reshape(length, 3, H, HD)
    cosine_table, sine_table = angles(jnp.arange(length, dtype=jnp.float32))
    cosine_table = cosine_table[:, None, :]
    sine_table = sine_table[:, None, :]
    query_rot = low(rotate(split[:, 0], cosine_table, sine_table))
    key_rot = low(rotate(split[:, 1], cosine_table, sine_table))
    value_low = low(split[:, 2])
    mixed_heads = low_back(low(attention(query_rot, key_rot, value_low).reshape(length, D)))
    attn_branch = matmul(mixed_heads, weight_out) + bias_out
    hidden_pre = low_back(matmul(normed_two, weight_up) + bias_up)
    activated = low(exact_gelu(hidden_pre))
    mlp_branch = matmul(activated, weight_down) + bias_down
    return sequence + attn_branch + mlp_branch

def add_pair(first_val, second_val):
    return first_val + second_val

def reference(tokens, norm1_gain, norm1_bias, norm2_gain, norm2_bias, qkv_weight, qkv_bias, out_weight, out_bias, up_weight, up_bias, down_weight, down_bias, cotangent):
    params = tuple((single.astype(jnp.float32) for single in (norm1_gain, norm1_bias, norm2_gain, norm2_bias, qkv_weight, qkv_bias, out_weight, out_bias, up_weight, up_bias, down_weight, down_bias)))
    seq_first = tokens.astype(jnp.float32).transpose(1, 0, 2)
    cot_first = cotangent.astype(jnp.float32).transpose(1, 0, 2)

    def per_sequence(totals, seq_args):
        sequence, seq_cot = seq_args
        result, pull_back = jax.vjp(layer, sequence, params)
        grad_seq, grad_params = pull_back(seq_cot)
        totals = jax.tree.map(add_pair, totals, grad_params)
        return (totals, (result.astype(jnp.bfloat16), grad_seq.astype(jnp.bfloat16)))
    initial = tuple((jnp.zeros_like(single) for single in params))
    totals, (results, grad_tokens) = lax.scan(per_sequence, initial, (seq_first, cot_first))
    return (results.transpose(1, 0, 2), grad_tokens.transpose(1, 0, 2), totals[0], totals[1], totals[2], totals[3], totals[4], totals[5], totals[6], totals[7], totals[8], totals[9], totals[10], totals[11])
```

```python
import functools

import jax
import jax.numpy as jnp
import numpy as np
from jax import lax
from jax.experimental import pallas as pl
from jax.experimental.pallas import tpu as pltpu
from jax.sharding import PartitionSpec as P

H = 12
HD = 64
ROT = 16
LANES = 128
EPS = 1e-05
MASKED = -1e30
VMEM = 56 * 1024 * 1024
BF = jnp.bfloat16
F32 = jnp.float32


def dot(left, right, dims=((1,), (0,))):
    return lax.dot_general(left, right, (dims, ((), ())), preferred_element_type=F32)


def back_dot(left, right):
    return dot(left, right, ((1,), (1,)))


def outer_sum(left, right):
    return dot(left, right, ((0,), (0,)))


def layer_norm(inputs, gain_vec, bias_vec):
    center = inputs - jnp.mean(inputs, axis=-1, keepdims=True)
    spread = jnp.mean(center * center, axis=-1, keepdims=True)
    return center * lax.rsqrt(spread + EPS) * gain_vec + bias_vec


def rotary_tables(length):
    half = ROT // 2
    inverse = np.float32(10000.0) ** (-np.arange(0, ROT, 2, dtype=np.float32) / np.float32(ROT))
    phase = np.arange(length, dtype=np.float32)[:, None] * inverse[None, :].astype(np.float32)
    cosine, sine = np.cos(phase), np.sin(phase)
    c = np.ones((length, HD), np.float32)
    s1 = np.zeros((length, HD), np.float32)
    s2 = np.zeros((length, HD), np.float32)
    c[:, :half] = cosine
    c[:, half:ROT] = cosine
    s1[:, :half] = -sine
    s2[:, half:ROT] = sine
    return tuple(np.concatenate([t, t], axis=1) for t in (c, s1, s2))


def turn(values, c, s1, s2):
    half = ROT // 2
    return (
        values * c
        + pltpu.roll(values, LANES - half, 1) * s1
        + pltpu.roll(values, half, 1) * s2
    )


def project_kernel(
    me, normed, cot, w_qkv, b_qkv, w_out, c_ref, s1_ref, s2_ref, out
):
    kind = pl.program_id(0)
    width = out.shape[-1]

    @pl.when(kind < 2)
    def _():
        full = dot(normed[...], w_qkv[...]) + b_qkv[...]
        c, s1, s2 = c_ref[...], s1_ref[...], s2_ref[...]
        for j in range(width // LANES):
            cols = slice(j * LANES, (j + 1) * LANES)
            out[0, :, cols] = turn(full[:, cols], c, s1, s2).astype(BF)

    @pl.when(kind == 2)
    def _():
        out[0] = (dot(normed[...], w_qkv[...]) + b_qkv[...]).astype(BF)

    @pl.when(kind == 3)
    def _():
        out[0] = back_dot(cot[...], w_out[...]).astype(BF)


def project(shift, me, normed, cot, w_qkv, b_qkv, w_out, tables, block_len, width, used):
    model = normed.shape[1]
    per = model // width

    def group(me_ref):
        return jnp.minimum(me_ref[0] ^ shift, used - 1)

    def rows(kind, me_ref):
        return (group(me_ref) // per, 0)

    def qkv_cols(kind, me_ref):
        return (0, jnp.minimum(kind, 2) * per + group(me_ref) % per)

    def own(kind, me_ref):
        return (0, 0)

    flops = 2 * 4 * block_len * model * width
    return pl.pallas_call(
        project_kernel,
        grid_spec=pltpu.PrefetchScalarGridSpec(
            num_scalar_prefetch=1,
            grid=(4,),
            in_specs=[
                pl.BlockSpec((block_len, model), rows),
                pl.BlockSpec((block_len, model), rows),
                pl.BlockSpec((model, width), qkv_cols),
                pl.BlockSpec((1, width), qkv_cols),
                pl.BlockSpec((width, model), lambda kind, me_ref: (group(me_ref) % per, 0)),
                pl.BlockSpec((block_len, LANES), own),
                pl.BlockSpec((block_len, LANES), own),
                pl.BlockSpec((block_len, LANES), own),
            ],
            out_specs=pl.BlockSpec((1, block_len, width), lambda kind, me_ref: (kind, 0, 0)),
        ),
        out_shape=jax.ShapeDtypeStruct((4, block_len, width), BF),
        compiler_params=pltpu.CompilerParams(vmem_limit_bytes=VMEM),
        cost_estimate=pl.CostEstimate(
            flops=flops, bytes_accessed=2 * (4 * model * width + 8 * block_len * width), transcendentals=0
        ),
        name="project",
    )(me, normed, cot, w_qkv, b_qkv, w_out, *tables)


def attend_kernel(n, block, me, *refs):
    ins = refs[:n]
    c_ref, s1_ref, s2_ref = refs[n : n + 3]
    outs = refs[n + 3 : 2 * n + 3]
    (q_s, k_s, v_s, g_s, qt_s, kt_s, vt_s, gt_s, sc, pb, dk, dv, o_s, dq_s) = refs[2 * n + 3 :]
    two = 2 * block
    scale = HD**-0.5

    for shift in range(n):
        at = ins[shift]
        place = me[0] ^ shift
        for kind, plain, flipped in ((0, q_s, qt_s), (1, k_s, kt_s), (2, v_s, vt_s), (3, g_s, gt_s)):
            piece = at[kind].astype(F32)
            if kind == 0:
                piece = piece * scale
            plain[place] = piece.astype(BF)
            flipped[place] = piece.T.astype(BF)

    lane = lax.broadcasted_iota(jnp.int32, (block, LANES), 1) < HD
    row = lax.broadcasted_iota(jnp.int32, (LANES, block), 0) < HD
    key_at = lax.broadcasted_iota(jnp.int32, (block, two), 0)
    query_at = lax.broadcasted_iota(jnp.int32, (block, two), 1)
    query_at = jnp.where(query_at >= block, query_at - block, query_at)
    allowed = key_at <= query_at

    def beside(flipped):
        zero = jnp.zeros_like(flipped)
        return jnp.concatenate([jnp.where(row, flipped, zero), jnp.where(row, zero, flipped)], axis=1)

    def below(plain):
        zero = jnp.zeros_like(plain)
        return jnp.concatenate([jnp.where(lane, plain, zero), jnp.where(lane, zero, plain)], axis=0)

    def loop(upto, body, init):
        if isinstance(upto, int):
            for j in range(upto):
                init = body(j, init)
            return init
        return lax.fori_loop(0, upto, body, init)

    def query_block(i, _):
        queries_t = beside(qt_s[i].astype(F32)).astype(BF)
        grads_t = beside(gt_s[i].astype(F32)).astype(BF)
        queries = below(q_s[i].astype(F32)).astype(BF)
        grads = below(g_s[i].astype(F32)).astype(BF)

        def score(j, top):
            found = dot(k_s[j], queries_t)
            sc[j] = found
            return jnp.maximum(top, jnp.max(found, axis=0, keepdims=True))

        diagonal = jnp.where(allowed, dot(k_s[i], queries_t), MASKED)
        sc[i] = diagonal
        top = loop(i, score, jnp.max(diagonal, axis=0, keepdims=True))

        def weigh(j, total):
            exps = jnp.exp(sc[j] - top)
            sc[j] = exps
            return total + jnp.sum(exps, axis=0, keepdims=True)

        total = loop(i + 1, weigh, jnp.zeros((1, two), F32))
        inverse = 1.0 / total

        def mix(j, heads):
            probs = sc[j] * inverse
            sc[j] = probs
            low = probs.astype(BF)
            pb[j] = low
            return tuple(
                heads[h] + dot(vt_s[j, h * HD : (h + 1) * HD], low[:, h * block : (h + 1) * block])
                for h in range(2)
            )

        none = jnp.zeros((HD, block), F32)
        heads = loop(i + 1, mix, (none, none))
        delta = jnp.concatenate(
            [
                jnp.sum(heads[h] * gt_s[i, h * HD : (h + 1) * HD].astype(F32), axis=0, keepdims=True)
                for h in range(2)
            ],
            axis=1,
        )
        o_s[i] = jnp.concatenate(heads, axis=0).T.astype(BF)

        def back(j, found, first):
            grad_scores = (sc[j] * (dot(v_s[j], grads_t) - delta)).astype(BF)
            key_part = dot(grad_scores, queries)
            value_part = dot(pb[j], grads)
            if first:
                dk[j] = key_part
                dv[j] = value_part
            else:
                dk[j] = dk[j] + key_part
                dv[j] = dv[j] + value_part
            return tuple(
                found[h]
                + dot(kt_s[j, h * HD : (h + 1) * HD], grad_scores[:, h * block : (h + 1) * block])
                for h in range(2)
            )

        found = back(i, (none, none), True)
        found = loop(i, lambda j, kept: back(j, kept, False), found)
        grad_query = jnp.concatenate(found, axis=0).T * scale
        dq_s[i] = turn(grad_query, c_ref[i], -s1_ref[i], -s2_ref[i]).astype(BF)
        return 0

    if n <= 4:
        for i in range(n):
            query_block(i, 0)
    else:
        lax.fori_loop(0, n, query_block, 0)

    for shift in range(n):
        place = me[0] ^ shift
        c, s1, s2 = c_ref[place], -s1_ref[place], -s2_ref[place]
        outs[shift][0] = o_s[place]
        outs[shift][1] = dq_s[place]
        outs[shift][2] = turn(dk[place], c, s1, s2).astype(BF)
        outs[shift][3] = dv[place].astype(BF)


def attend(n, me, pieces, tables):
    _, block, width = pieces[0].shape
    length = n * block
    spec = pl.BlockSpec((4, block, LANES), lambda j, me_ref: (0, 0, j))
    table_spec = pl.BlockSpec((n, block, LANES), lambda j, me_ref: (0, 0, 0))
    plain = pltpu.VMEM((n, block, LANES), BF)
    flipped = pltpu.VMEM((n, LANES, block), BF)
    total = pltpu.VMEM((n, block, LANES), F32)
    work = width // HD * length * (length + block) // 2
    return pl.pallas_call(
        functools.partial(attend_kernel, n, block),
        grid_spec=pltpu.PrefetchScalarGridSpec(
            num_scalar_prefetch=1,
            grid=(width // LANES,),
            in_specs=[spec] * n + [table_spec] * 3,
            out_specs=[spec] * n,
            scratch_shapes=[
                plain, plain, plain, plain,
                flipped, flipped, flipped, flipped,
                pltpu.VMEM((n, block, 2 * block), F32),
                pltpu.VMEM((n, block, 2 * block), BF),
                total, total, plain, plain,
            ],
        ),
        out_shape=[jax.ShapeDtypeStruct((4, block, width), BF)] * n,
        compiler_params=pltpu.CompilerParams(vmem_limit_bytes=VMEM),
        cost_estimate=pl.CostEstimate(
            flops=12 * work * 4 * HD, bytes_accessed=2 * 8 * length * width, transcendentals=work
        ),
        name="attend",
    )(me, *pieces, *(jnp.asarray(t).reshape(n, block, LANES) for t in tables))


def mlp_kernel(normed, cot, w_up, b_up, w_down, out, grad_in, grad_up, grad_down, grad_b):
    step = pl.program_id(0)
    hidden = dot(normed[...], w_up[...]) + b_up[...]
    share = 0.5 + 0.5 * lax.erf(hidden * (0.5**0.5))
    slope = share + hidden * (jnp.exp(-0.5 * hidden * hidden) * ((2.0 * np.pi) ** -0.5))
    active = (hidden * share).astype(BF)
    grad_hidden_f = back_dot(cot[...], w_down[...]) * slope
    grad_hidden = grad_hidden_f.astype(BF)
    grad_b[...] = jnp.sum(grad_hidden.astype(F32), axis=0, keepdims=True)
    mixed = dot(active, w_down[...])
    back = back_dot(grad_hidden, w_up[...])

    @pl.when(step == 0)
    def _():
        out[...] = mixed
        grad_in[...] = back

    @pl.when(step > 0)
    def _():
        out[...] = out[...] + mixed
        grad_in[...] = grad_in[...] + back

    grad_down[...] = outer_sum(active, cot[...]).astype(BF)
    grad_up[...] = outer_sum(normed[...], grad_hidden).astype(BF)


def mlp(normed, cot, w_up, b_up, w_down):
    rows, model = normed.shape
    hidden = w_up.shape[1]
    chunk = 384
    whole = pl.BlockSpec((rows, model), lambda j: (0, 0))
    tall = pl.BlockSpec((model, chunk), lambda j: (0, j))
    flat = pl.BlockSpec((chunk, model), lambda j: (j, 0))
    line = pl.BlockSpec((1, chunk), lambda j: (0, j))
    return pl.pallas_call(
        mlp_kernel,
        grid=(hidden // chunk,),
        in_specs=[whole, whole, tall, line, flat],
        out_specs=[whole, whole, tall, flat, line],
        out_shape=[
            jax.ShapeDtypeStruct((rows, model), F32),
            jax.ShapeDtypeStruct((rows, model), F32),
            jax.ShapeDtypeStruct((model, hidden), BF),
            jax.ShapeDtypeStruct((hidden, model), BF),
            jax.ShapeDtypeStruct((1, hidden), F32),
        ],
        compiler_params=pltpu.CompilerParams(vmem_limit_bytes=VMEM),
        cost_estimate=pl.CostEstimate(
            flops=12 * rows * model * hidden,
            bytes_accessed=8 * model * hidden + 12 * rows * model,
            transcendentals=2 * rows * hidden,
        ),
        name="mlp",
    )(normed, cot, w_up, b_up, w_down)


def swap(value, shift, n):
    return lax.ppermute(value, "ctx", [(i, i ^ shift) for i in range(n)])


def sum_over_ctx(shard, n):
    me = lax.axis_index("ctx")
    rows = shard.shape[0] // n
    parts = shard.reshape((n, rows) + shard.shape[1:])

    def part(at):
        return lax.dynamic_index_in_dim(parts, at, 0, keepdims=False)

    total = part(me).astype(F32)
    for shift in range(1, n):
        total = total + swap(part(me ^ shift), shift, n).astype(F32)
    own = total.astype(BF)
    gathered = jnp.stack([own] + [swap(own, shift, n) for shift in range(1, n)])
    return jnp.stack(
        [lax.dynamic_index_in_dim(gathered, me ^ at, 0, keepdims=False) for at in range(n)]
    ).reshape(shard.shape)


def body(
    tokens,
    norm1_gain,
    norm1_bias,
    norm2_gain,
    norm2_bias,
    qkv_weight,
    qkv_bias,
    out_weight,
    out_bias,
    up_weight,
    up_bias,
    down_weight,
    down_bias,
    cotangent,
):
    block_len, seq_count, model = tokens.shape
    n = lax.axis_size("ctx")
    shards = lax.axis_size("fsdp")
    rows = block_len * seq_count
    hidden = up_weight.shape[1]
    me = lax.axis_index("ctx")
    me_arr = me.astype(jnp.int32).reshape(1)
    width = -(-seq_count * model // (n * LANES)) * LANES
    used = seq_count * model // width
    per = model // width

    vectors = (
        norm1_gain, norm1_bias, norm2_gain, norm2_bias, qkv_bias, out_bias, up_bias, down_bias,
    )
    sizes = [v.shape[0] for v in vectors]
    packed = jnp.concatenate(vectors)
    lines = 16
    packed = jnp.pad(packed, (0, lines * model - packed.shape[0])).reshape(lines, model)
    own_rows = out_weight.shape[0]
    out_every = lax.all_gather(
        jnp.concatenate([out_weight, packed], axis=0), "fsdp", axis=0, tiled=False
    )
    w_qkv = lax.all_gather(qkv_weight, "fsdp", axis=0, tiled=True)
    w_up = lax.all_gather(up_weight, "fsdp", axis=0, tiled=True)
    w_down = lax.all_gather(down_weight, "fsdp", axis=0, tiled=True)
    w_out = out_every[:, :own_rows].reshape(model, model)
    flat = out_every[:, own_rows:].reshape(shards, lines * model)
    whole, start = [], 0
    for size in sizes:
        whole.append(flat[:, start : start + size].reshape(shards * size).astype(F32))
        start += size
    gain_one, bias_one, gain_two, bias_two, b_qkv, b_out, b_up, b_down = whole

    inputs_low = tokens.transpose(1, 0, 2).reshape(rows, model)
    inputs = inputs_low.astype(F32)
    cot = cotangent.transpose(1, 0, 2).reshape(rows, model)
    cot_f = cot.astype(F32)
    normed_one = layer_norm(inputs, gain_one, bias_one).astype(BF)
    normed_two = layer_norm(inputs, gain_two, bias_two).astype(BF)

    tables = rotary_tables(n * block_len)
    own_tables = tuple(
        lax.dynamic_slice_in_dim(jnp.asarray(t), me * block_len, block_len, 0) for t in tables
    )

    def made(shift):
        return project(
            shift, me_arr, normed_one, cot, w_qkv, b_qkv.reshape(1, -1), w_out, own_tables,
            block_len, width, used,
        )

    pieces = [None] * n
    for shift in list(range(1, n)) + [0]:
        pieces[shift] = made(shift) if shift == 0 else swap(made(shift), shift, n)
    answers = attend(n, me_arr, pieces, tables)
    answers = jnp.stack(
        [answers[0]] + [swap(answers[shift], shift, n) for shift in range(1, n)]
    )
    by_group = jnp.stack(
        [lax.dynamic_index_in_dim(answers, me ^ at, 0, keepdims=False) for at in range(used)]
    )
    by_kind = (
        by_group.reshape(seq_count, per, 4, block_len, width)
        .transpose(2, 0, 3, 1, 4)
        .reshape(4, rows, model)
    )
    mixed_heads = by_kind[0]

    mlp_out, grad_two, grad_up, grad_down, grad_up_b = mlp(
        normed_two, cot, w_up, b_up.reshape(1, -1), w_down
    )
    attn_branch = jnp.dot(mixed_heads, w_out, preferred_element_type=F32) + b_out
    layer_out = (
        (inputs + attn_branch + mlp_out + b_down)
        .astype(BF)
        .reshape(seq_count, block_len, model)
        .transpose(1, 0, 2)
    )
    column_sums = jnp.sum(cot_f, axis=0)
    grad_out = outer_sum(mixed_heads, cot)
    grad_kinds = [outer_sum(normed_one, by_kind[t]) for t in (1, 2, 3)]
    grad_qkv_b = jnp.concatenate([jnp.sum(by_kind[t].astype(F32), axis=0) for t in (1, 2, 3)])
    grad_one = sum(
        back_dot(by_kind[t], w_qkv[:, (t - 1) * model : t * model]) for t in (1, 2, 3)
    )
    _, norm_back_one = jax.vjp(layer_norm, inputs, gain_one, bias_one)
    grad_in_one, grad_gain_one, grad_bias_one = norm_back_one(grad_one)
    _, norm_back_two = jax.vjp(layer_norm, inputs, gain_two, bias_two)
    grad_in_two, grad_gain_two, grad_bias_two = norm_back_two(grad_two)
    tokens_grad = (
        (cot_f + grad_in_one + grad_in_two)
        .astype(BF)
        .reshape(seq_count, block_len, model)
        .transpose(1, 0, 2)
    )

    grad_vectors = (
        grad_gain_one, grad_bias_one, grad_gain_two, grad_bias_two, grad_qkv_b, column_sums,
        grad_up_b.reshape(-1),
    )
    grad_sizes = [v.shape[0] // shards for v in grad_vectors]
    grad_lines = 32
    packed_grads = jnp.concatenate([v.reshape(shards, -1) for v in grad_vectors], axis=1)
    packed_grads = jnp.pad(
        packed_grads, ((0, 0), (0, grad_lines * model - packed_grads.shape[1]))
    ).reshape(shards, grad_lines, model)
    last = jnp.concatenate(
        [g.astype(BF).reshape(shards, own_rows, model) for g in grad_kinds + [grad_out]]
        + [packed_grads.astype(BF)],
        axis=1,
    ).reshape(-1, model)

    def shard_sum(value):
        return lax.psum_scatter(value, "fsdp", scatter_dimension=0, tiled=True)

    part_down = sum_over_ctx(shard_sum(grad_down), n).astype(F32)
    part_up = sum_over_ctx(shard_sum(grad_up), n).astype(F32)
    part_last = sum_over_ctx(shard_sum(last), n).astype(F32)
    part_qkv = jnp.concatenate(
        [part_last[t * own_rows : (t + 1) * own_rows] for t in range(3)], axis=1
    )
    part_out = part_last[3 * own_rows : 4 * own_rows]
    line_sums = part_last[4 * own_rows :].reshape(-1)
    found, start = [], 0
    for size in grad_sizes:
        found.append(line_sums[start : start + size])
        start += size
    gain1, bias1, gain2, bias2, qkv_b, columns, up_b = found
    return (
        layer_out, tokens_grad, gain1, bias1, gain2, bias2, part_qkv, qkv_b, part_out, columns,
        part_up, up_b, part_down, columns,
    )


def solution(mesh):
    blocks = P("ctx", "fsdp", None)
    line, matrix = P("fsdp"), P("fsdp", None)
    return jax.shard_map(
        body,
        mesh=mesh,
        in_specs=(
            blocks, line, line, line, line, matrix, line, matrix, line, matrix, line, matrix, line,
            blocks,
        ),
        out_specs=(
            blocks, blocks, line, line, line, line, matrix, line, matrix, line, matrix, line,
            matrix, line,
        ),
        check_vma=False,
    )
```

```python
import functools

import jax
import jax.numpy as jnp
import numpy as np
from jax import lax
from jax.experimental import pallas as pl
from jax.experimental.pallas import tpu as pltpu
from jax.sharding import PartitionSpec as P

H = 12
HD = 64
ROT = 16
LANES = 128
EPS = 1e-05
MASKED = -1e30
VMEM = 56 * 1024 * 1024
BF = jnp.bfloat16
F32 = jnp.float32


def dot(left, right, dims=((1,), (0,))):
    return lax.dot_general(left, right, (dims, ((), ())), preferred_element_type=F32)


def back_dot(left, right):
    return dot(left, right, ((1,), (1,)))


def outer_sum(left, right):
    return dot(left, right, ((0,), (0,)))


def normalized(values):
    center = values - jnp.mean(values, axis=-1, keepdims=True)
    spread = jnp.mean(center * center, axis=-1, keepdims=True)
    inverse = lax.rsqrt(spread + EPS)
    return center * inverse, inverse


def norm_back(hat, inverse, gain, grad):
    scaled = grad * gain
    first = jnp.mean(scaled, axis=-1, keepdims=True)
    second = jnp.mean(scaled * hat, axis=-1, keepdims=True)
    return (
        inverse * (scaled - first - hat * second),
        jnp.sum(grad * hat, axis=0, keepdims=True),
        jnp.sum(grad, axis=0, keepdims=True),
    )


def rotary_tables(length):
    half = ROT // 2
    inverse = np.float32(10000.0) ** (-np.arange(0, ROT, 2, dtype=np.float32) / np.float32(ROT))
    phase = np.arange(length, dtype=np.float32)[:, None] * inverse[None, :].astype(np.float32)
    cosine, sine = np.cos(phase), np.sin(phase)
    c = np.ones((length, HD), np.float32)
    s1 = np.zeros((length, HD), np.float32)
    s2 = np.zeros((length, HD), np.float32)
    c[:, :half] = cosine
    c[:, half:ROT] = cosine
    s1[:, :half] = -sine
    s2[:, half:ROT] = sine
    return tuple(np.concatenate([t, t], axis=1) for t in (c, s1, s2))


def turn(values, c, s1, s2):
    half = ROT // 2
    return (
        values * c
        + pltpu.roll(values, LANES - half, 1) * s1
        + pltpu.roll(values, half, 1) * s2
    )


def project_kernel(
    n, block_len, used, me, tokens, cot, gain, bias, w, b, c_ref, s1_ref, s2_ref, *rest
):
    outs, normed = rest[:n], rest[n]
    kind = pl.program_id(0)

    @pl.when(kind == 0)
    def _():
        hat, _inverse = normalized(tokens[...].astype(F32))
        normed[...] = (hat * gain[...] + bias[...]).astype(BF)

    width = outs[0].shape[-1]
    per = w.shape[-1] // width

    def operands(shift, left):
        group = jnp.minimum(me[0] ^ shift, used - 1)
        rows = pl.multiple_of((group // per) * block_len, block_len)
        cols = pl.multiple_of((group % per) * width, LANES)
        return left[pl.ds(rows, block_len)], pl.ds(cols, width)

    @pl.when(kind < 2)
    def _():
        c, s1, s2 = c_ref[...], s1_ref[...], s2_ref[...]
        for shift in range(n):
            left, cols = operands(shift, normed)
            full = dot(left, w[0, :, cols]) + b[0, :, cols]
            for j in range(width // LANES):
                at = slice(j * LANES, (j + 1) * LANES)
                outs[shift][0, :, at] = turn(full[:, at], c, s1, s2).astype(BF)

    @pl.when(kind == 2)
    def _():
        for shift in range(n):
            left, cols = operands(shift, normed)
            outs[shift][0] = (dot(left, w[0, :, cols]) + b[0, :, cols]).astype(BF)

    @pl.when(kind == 3)
    def _():
        for shift in range(n):
            left, cols = operands(shift, cot)
            outs[shift][0] = back_dot(left, w[0, cols]).astype(BF)


def project(n, me, tokens, cot, gain, bias, w, b, tables, block_len, width, used):
    rows, model = tokens.shape
    whole = pl.BlockSpec((rows, model), lambda kind, me_ref: (0, 0))
    line = pl.BlockSpec((1, model), lambda kind, me_ref: (0, 0))
    own = pl.BlockSpec((block_len, LANES), lambda kind, me_ref: (0, 0))
    return pl.pallas_call(
        functools.partial(project_kernel, n, block_len, used),
        grid_spec=pltpu.PrefetchScalarGridSpec(
            num_scalar_prefetch=1,
            grid=(4,),
            in_specs=[
                whole,
                whole,
                line,
                line,
                pl.BlockSpec((1, model, model), lambda kind, me_ref: (kind, 0, 0)),
                pl.BlockSpec((1, 1, model), lambda kind, me_ref: (jnp.minimum(kind, 2), 0, 0)),
                own,
                own,
                own,
            ],
            out_specs=[pl.BlockSpec((1, block_len, width), lambda kind, me_ref: (kind, 0, 0))] * n,
            scratch_shapes=[pltpu.VMEM((rows, model), BF)],
        ),
        out_shape=[jax.ShapeDtypeStruct((4, block_len, width), BF)] * n,
        compiler_params=pltpu.CompilerParams(vmem_limit_bytes=VMEM),
        cost_estimate=pl.CostEstimate(
            flops=8 * rows * model * model,
            bytes_accessed=2 * (4 * model * model + 6 * rows * model),
            transcendentals=0,
        ),
        name="project",
    )(me, tokens, cot, gain, bias, w, b.reshape(3, 1, model), *tables)


def attend_kernel(n, block, me, *refs):
    ins = refs[:n]
    c_ref, s1_ref, s2_ref = refs[n : n + 3]
    outs = refs[n + 3 : 2 * n + 3]
    (q_s, k_s, v_s, g_s, qt_s, kt_s, vt_s, gt_s, sc, pb, dk, dv, o_s, dq_s) = refs[2 * n + 3 :]
    two = 2 * block
    scale = HD**-0.5

    for shift in range(n):
        at = ins[shift]
        place = me[0] ^ shift
        for kind, plain, flipped in ((0, q_s, qt_s), (1, k_s, kt_s), (2, v_s, vt_s), (3, g_s, gt_s)):
            piece = at[kind].astype(F32)
            if kind == 0:
                piece = piece * scale
            plain[place] = piece.astype(BF)
            flipped[place] = piece.T.astype(BF)

    lane = lax.broadcasted_iota(jnp.int32, (block, LANES), 1) < HD
    row = lax.broadcasted_iota(jnp.int32, (LANES, block), 0) < HD
    key_at = lax.broadcasted_iota(jnp.int32, (block, two), 0)
    query_at = lax.broadcasted_iota(jnp.int32, (block, two), 1)
    query_at = jnp.where(query_at >= block, query_at - block, query_at)
    allowed = key_at <= query_at

    def beside(flipped):
        zero = jnp.zeros_like(flipped)
        return jnp.concatenate([jnp.where(row, flipped, zero), jnp.where(row, zero, flipped)], axis=1)

    def below(plain):
        zero = jnp.zeros_like(plain)
        return jnp.concatenate([jnp.where(lane, plain, zero), jnp.where(lane, zero, plain)], axis=0)

    def loop(upto, body, init):
        if isinstance(upto, int):
            for j in range(upto):
                init = body(j, init)
            return init
        return lax.fori_loop(0, upto, body, init)

    def query_block(i, _):
        queries_t = beside(qt_s[i].astype(F32)).astype(BF)
        grads_t = beside(gt_s[i].astype(F32)).astype(BF)
        queries = below(q_s[i].astype(F32)).astype(BF)
        grads = below(g_s[i].astype(F32)).astype(BF)

        def score(j, top):
            found = dot(k_s[j], queries_t)
            sc[j] = found
            return jnp.maximum(top, jnp.max(found, axis=0, keepdims=True))

        diagonal = jnp.where(allowed, dot(k_s[i], queries_t), MASKED)
        sc[i] = diagonal
        top = loop(i, score, jnp.max(diagonal, axis=0, keepdims=True))

        def weigh(j, total):
            exps = jnp.exp(sc[j] - top)
            sc[j] = exps
            return total + jnp.sum(exps, axis=0, keepdims=True)

        total = loop(i + 1, weigh, jnp.zeros((1, two), F32))
        inverse = 1.0 / total

        def mix(j, heads):
            probs = sc[j] * inverse
            sc[j] = probs
            low = probs.astype(BF)
            pb[j] = low
            return tuple(
                heads[h] + dot(vt_s[j, h * HD : (h + 1) * HD], low[:, h * block : (h + 1) * block])
                for h in range(2)
            )

        none = jnp.zeros((HD, block), F32)
        heads = loop(i + 1, mix, (none, none))
        delta = jnp.concatenate(
            [
                jnp.sum(heads[h] * gt_s[i, h * HD : (h + 1) * HD].astype(F32), axis=0, keepdims=True)
                for h in range(2)
            ],
            axis=1,
        )
        o_s[i] = jnp.concatenate(heads, axis=0).T.astype(BF)

        def back(j, found, first):
            grad_scores = (sc[j] * (dot(v_s[j], grads_t) - delta)).astype(BF)
            key_part = dot(grad_scores, queries)
            value_part = dot(pb[j], grads)
            if first:
                dk[j] = key_part
                dv[j] = value_part
            else:
                dk[j] = dk[j] + key_part
                dv[j] = dv[j] + value_part
            return tuple(
                found[h]
                + dot(kt_s[j, h * HD : (h + 1) * HD], grad_scores[:, h * block : (h + 1) * block])
                for h in range(2)
            )

        found = back(i, (none, none), True)
        found = loop(i, lambda j, kept: back(j, kept, False), found)
        grad_query = jnp.concatenate(found, axis=0).T * scale
        dq_s[i] = turn(grad_query, c_ref[i], -s1_ref[i], -s2_ref[i]).astype(BF)
        return 0

    if n <= 4:
        for i in range(n):
            query_block(i, 0)
    else:
        lax.fori_loop(0, n, query_block, 0)

    for shift in range(n):
        place = me[0] ^ shift
        c, s1, s2 = c_ref[place], -s1_ref[place], -s2_ref[place]
        outs[shift][0] = o_s[place]
        outs[shift][1] = dq_s[place]
        outs[shift][2] = turn(dk[place], c, s1, s2).astype(BF)
        outs[shift][3] = dv[place].astype(BF)


def attend(n, me, pieces, tables):
    _, block, width = pieces[0].shape
    length = n * block
    spec = pl.BlockSpec((4, block, LANES), lambda j, me_ref: (0, 0, j))
    table_spec = pl.BlockSpec((n, block, LANES), lambda j, me_ref: (0, 0, 0))
    plain = pltpu.VMEM((n, block, LANES), BF)
    flipped = pltpu.VMEM((n, LANES, block), BF)
    total = pltpu.VMEM((n, block, LANES), F32)
    work = width // HD * length * (length + block) // 2
    return pl.pallas_call(
        functools.partial(attend_kernel, n, block),
        grid_spec=pltpu.PrefetchScalarGridSpec(
            num_scalar_prefetch=1,
            grid=(width // LANES,),
            in_specs=[spec] * n + [table_spec] * 3,
            out_specs=[spec] * n,
            scratch_shapes=[
                plain, plain, plain, plain,
                flipped, flipped, flipped, flipped,
                pltpu.VMEM((n, block, 2 * block), F32),
                pltpu.VMEM((n, block, 2 * block), BF),
                total, total, plain, plain,
            ],
        ),
        out_shape=[jax.ShapeDtypeStruct((4, block, width), BF)] * n,
        compiler_params=pltpu.CompilerParams(vmem_limit_bytes=VMEM),
        cost_estimate=pl.CostEstimate(
            flops=12 * work * 4 * HD, bytes_accessed=2 * 8 * length * width, transcendentals=work
        ),
        name="attend",
    )(me, *pieces, *(jnp.asarray(t).reshape(n, block, LANES) for t in tables))


def mlp_kernel(
    tokens, cot, gain, bias, b_sum, w_up, b_up, w_down,
    out, grad_in, grad_up, grad_down, grad_b, sums,
    normed,
):
    step = pl.program_id(0)

    @pl.when(step == 0)
    def _():
        values = tokens[...].astype(F32)
        hat, _inverse = normalized(values)
        normed[...] = (hat * gain[...] + bias[...]).astype(BF)
        out[...] = values + b_sum[...]
        grad_in[...] = jnp.zeros_like(grad_in)

    hidden = dot(normed[...], w_up[...]) + b_up[...]
    share = 0.5 + 0.5 * lax.erf(hidden * (0.5**0.5))
    slope = share + hidden * (jnp.exp(-0.5 * hidden * hidden) * ((2.0 * np.pi) ** -0.5))
    active = (hidden * share).astype(BF)
    grad_hidden = (back_dot(cot[...], w_down[...]) * slope).astype(BF)
    grad_b[...] = jnp.sum(grad_hidden.astype(F32), axis=0, keepdims=True)
    out[...] = out[...] + dot(active, w_down[...])
    grad_in[...] = grad_in[...] + back_dot(grad_hidden, w_up[...])
    grad_down[...] = outer_sum(active, cot[...]).astype(BF)
    grad_up[...] = outer_sum(normed[...], grad_hidden).astype(BF)

    @pl.when(step == pl.num_programs(0) - 1)
    def _():
        hat, inverse = normalized(tokens[...].astype(F32))
        upstream = cot[...].astype(F32)
        back, grad_gain, grad_bias = norm_back(hat, inverse, gain[...], grad_in[...])
        grad_in[...] = upstream + back
        sums[0:1] = grad_gain
        sums[1:2] = grad_bias
        sums[2:3] = jnp.sum(upstream, axis=0, keepdims=True)
        sums[3:8] = jnp.zeros((5, sums.shape[1]), F32)


def mlp(tokens, cot, gain, bias, b_sum, w_up, b_up, w_down):
    rows, model = tokens.shape
    hidden = w_up.shape[1]
    chunk = 384
    whole = pl.BlockSpec((rows, model), lambda j: (0, 0))
    flat_line = pl.BlockSpec((1, model), lambda j: (0, 0))
    tall = pl.BlockSpec((model, chunk), lambda j: (0, j))
    flat = pl.BlockSpec((chunk, model), lambda j: (j, 0))
    line = pl.BlockSpec((1, chunk), lambda j: (0, j))
    return pl.pallas_call(
        mlp_kernel,
        grid=(hidden // chunk,),
        in_specs=[whole, whole, flat_line, flat_line, flat_line, tall, line, flat],
        out_specs=[whole, whole, tall, flat, line, pl.BlockSpec((8, model), lambda j: (0, 0))],
        out_shape=[
            jax.ShapeDtypeStruct((rows, model), F32),
            jax.ShapeDtypeStruct((rows, model), F32),
            jax.ShapeDtypeStruct((model, hidden), BF),
            jax.ShapeDtypeStruct((hidden, model), BF),
            jax.ShapeDtypeStruct((1, hidden), F32),
            jax.ShapeDtypeStruct((8, model), F32),
        ],
        scratch_shapes=[pltpu.VMEM((rows, model), BF)],
        compiler_params=pltpu.CompilerParams(vmem_limit_bytes=VMEM),
        cost_estimate=pl.CostEstimate(
            flops=12 * rows * model * hidden,
            bytes_accessed=8 * model * hidden + 12 * rows * model,
            transcendentals=2 * rows * hidden,
        ),
        name="mlp",
    )(tokens, cot, gain, bias, b_sum, w_up, b_up, w_down)


def finish_kernel(n, block_len, used, shards, at, *refs):
    answers = refs[:n]
    (tokens, cot, gain, bias, base, grad_base, w, out, grad_out, own, other, sums, normed, grad_in, held, grads) = refs[n:]
    kind = pl.program_id(0)
    width = answers[0].shape[-1]
    per = w.shape[-1] // width
    own_rows = own.shape[-2]

    for shift in range(n):
        group = jnp.minimum(at[0] ^ shift, used - 1)
        rows = pl.multiple_of((group // per) * block_len, block_len)
        cols = pl.multiple_of((group % per) * width, LANES)
        if used == n:
            held[pl.ds(rows, block_len), pl.ds(cols, width)] = answers[shift][0]
        else:
            @pl.when((at[0] ^ shift) < used)
            def _(rows=rows, cols=cols, shift=shift):
                held[pl.ds(rows, block_len), pl.ds(cols, width)] = answers[shift][0]

    @pl.when(kind == 0)
    def _():
        hat, _inverse = normalized(tokens[...].astype(F32))
        normed[...] = (hat * gain[...] + bias[...]).astype(BF)
        out[...] = (base[...] + dot(held[...], w[0])).astype(BF)
        grad_in[...] = jnp.zeros_like(grad_in)
        sums[...] = jnp.zeros_like(sums)
        grads[...] = outer_sum(held[...], cot[...]).astype(BF).reshape(grads.shape)

    @pl.when(kind > 0)
    def _():
        grads[...] = outer_sum(normed[...], held[...]).astype(BF).reshape(grads.shape)
        grad_in[...] = grad_in[...] + back_dot(held[...], w[0])
        sums[pl.ds(kind, 1)] = jnp.sum(held[...].astype(F32), axis=0, keepdims=True)

    for z in range(shards // 2):
        own[0, z] = grads[z, at[1]]
        other[0, z] = grads[z, at[1] ^ 1]

    @pl.when(kind == 3)
    def _():
        hat, inverse = normalized(tokens[...].astype(F32))
        back, grad_gain, grad_bias = norm_back(hat, inverse, gain[...], grad_in[...])
        grad_out[...] = (grad_base[...] + back).astype(BF)
        sums[4:5] = grad_gain
        sums[5:6] = grad_bias


def finish(n, me, core, answers, tokens, cot, gain, bias, base, grad_base, w, shards, used):
    rows, model = tokens.shape
    block_len, width = answers[0].shape[1:]
    whole = pl.BlockSpec((rows, model), lambda kind, at: (0, 0))
    line = pl.BlockSpec((1, model), lambda kind, at: (0, 0))
    own_rows = model // shards

    def unit(kind, at):
        return (lax.rem(kind + 3, 4), 0, 0)

    half = pl.BlockSpec(
        (1, shards // 2, own_rows, model), lambda kind, at: (lax.rem(kind + 3, 4), 0, 0, 0)
    )
    return pl.pallas_call(
        functools.partial(finish_kernel, n, block_len, used, shards),
        grid_spec=pltpu.PrefetchScalarGridSpec(
            num_scalar_prefetch=1,
            grid=(4,),
            in_specs=[pl.BlockSpec((1, block_len, width), lambda kind, at: (kind, 0, 0))] * n
            + [whole, whole, line, line, whole, whole, pl.BlockSpec((1, model, model), unit)],
            out_specs=[
                whole, whole, half, half, pl.BlockSpec((8, model), lambda kind, at: (0, 0)),
            ],
            scratch_shapes=[
                pltpu.VMEM((rows, model), BF),
                pltpu.VMEM((rows, model), F32),
                pltpu.VMEM((rows, model), BF),
                pltpu.VMEM((shards // 2, 2, own_rows, model), BF),
            ],
        ),
        out_shape=[
            jax.ShapeDtypeStruct((rows, model), BF),
            jax.ShapeDtypeStruct((rows, model), BF),
            jax.ShapeDtypeStruct((4, shards // 2, own_rows, model), BF),
            jax.ShapeDtypeStruct((4, shards // 2, own_rows, model), BF),
            jax.ShapeDtypeStruct((8, model), F32),
        ],
        compiler_params=pltpu.CompilerParams(vmem_limit_bytes=VMEM),
        cost_estimate=pl.CostEstimate(
            flops=16 * rows * model * model, bytes_accessed=40 * rows * model, transcendentals=0
        ),
        name="finish",
    )(jnp.stack([me, core]).astype(jnp.int32), *answers, tokens, cot, gain, bias, base, grad_base, w)


def swap(value, shift, n):
    return lax.ppermute(value, "ctx", [(i, i ^ shift) for i in range(n)])


def swap_shard(value, shift, m):
    return lax.ppermute(value, "fsdp", [(i, i ^ shift) for i in range(m)])


def assemble_kernel(where, counted, shard_first, at, *refs):
    ins, out = refs[:counted], refs[counted]
    for piece, index, place in where:
        unit, shard = place(at)
        if shard_first:
            out[shard, unit] = ins[piece][index]
        else:
            out[unit, shard] = ins[piece][index]


def gather_units(units, n, m, shard_first=False):
    q, f = lax.axis_index("ctx"), lax.axis_index("fsdp")
    steps = list(range(2, m, 2))
    mine = lax.dynamic_index_in_dim(units, q, 0, keepdims=False)
    other = swap_shard(units, 1, m)
    along = jnp.stack([swap_shard(mine, step, m) for step in steps])
    columns = [along] + [swap(along, shift, n) for shift in range(1, n)]
    crossed = [swap_shard(held, 1, m) for held in columns]
    pieces = [units, other] + columns + crossed
    where = []
    for unit in range(n):
        where.append((0, unit, lambda at, unit=unit: (unit, at[1])))
        where.append((1, unit, lambda at, unit=unit: (unit, at[1] ^ 1)))
    for core in range(2):
        for shift in range(n):
            for index, step in enumerate(steps):
                where.append(
                    (
                        2 + core * n + shift,
                        index,
                        lambda at, shift=shift, step=step, core=core: (at[0] ^ shift, at[1] ^ step ^ core),
                    )
                )
    full = ((m, n) if shard_first else (n, m)) + units.shape[1:]
    return pl.pallas_call(
        functools.partial(assemble_kernel, where, len(pieces), shard_first),
        grid_spec=pltpu.PrefetchScalarGridSpec(
            num_scalar_prefetch=1,
            grid=(1,),
            in_specs=[pl.BlockSpec(p.shape, lambda i, at, r=p.ndim: (0,) * r) for p in pieces],
            out_specs=pl.BlockSpec(full, lambda i, at: (0, 0, 0, 0)),
        ),
        out_shape=jax.ShapeDtypeStruct(full, units.dtype),
        compiler_params=pltpu.CompilerParams(vmem_limit_bytes=VMEM),
        cost_estimate=pl.CostEstimate(
            flops=0, bytes_accessed=4 * n * m * mine.size, transcendentals=0
        ),
        name="assemble",
    )(jnp.stack([q, f]).astype(jnp.int32), *pieces)


def add_up(*pieces):
    return sum(p.astype(F32) for p in pieces).astype(BF)


def sum_units(own, other, n, m):
    q, z = lax.axis_index("ctx"), lax.axis_index("fsdp") // 2

    def pick(value, at, axis):
        return lax.dynamic_index_in_dim(value, at, axis, keepdims=False)

    chip = add_up(own, swap_shard(other, 1, m))
    unit = add_up(pick(chip, q, 0), *[swap(pick(chip, q ^ s, 0), s, n) for s in range(1, n)])
    own = add_up(
        pick(unit, z, 0), *[swap_shard(pick(unit, z ^ s, 0), 2 * s, m) for s in range(1, m // 2)]
    )
    gathered = jnp.stack([own] + [swap(own, s, n) for s in range(1, n)])
    return jnp.stack([pick(gathered, q ^ at, 0) for at in range(n)])


def sum_lines(lines, n, m):
    step = 1
    while step < m:
        lines = lines + swap_shard(lines, step, m)
        step *= 2
    step = 1
    while step < n:
        lines = lines + swap(lines, step, n)
        step *= 2
    return lines


def gather_lines(line, m):
    f = lax.axis_index("fsdp")
    step = 1
    while step < m:
        line = jnp.concatenate([line, swap_shard(line, step, m)], axis=0)
        step *= 2
    return jnp.take(line, f ^ jnp.arange(m), axis=0)


def sum_over_ctx(shard, n):
    me = lax.axis_index("ctx")
    rows = shard.shape[0] // n
    parts = shard.reshape((n, rows) + shard.shape[1:])

    def part(at):
        return lax.dynamic_index_in_dim(parts, at, 0, keepdims=False)

    total = part(me).astype(F32)
    for shift in range(1, n):
        total = total + swap(part(me ^ shift), shift, n).astype(F32)
    own = total.astype(BF)
    gathered = jnp.stack([own] + [swap(own, shift, n) for shift in range(1, n)])
    return jnp.stack(
        [lax.dynamic_index_in_dim(gathered, me ^ at, 0, keepdims=False) for at in range(n)]
    ).reshape(shard.shape)


def body(
    tokens,
    norm1_gain,
    norm1_bias,
    norm2_gain,
    norm2_bias,
    qkv_weight,
    qkv_bias,
    out_weight,
    out_bias,
    up_weight,
    up_bias,
    down_weight,
    down_bias,
    cotangent,
):
    block_len, seq_count, model = tokens.shape
    n = lax.axis_size("ctx")
    shards = lax.axis_size("fsdp")
    rows = block_len * seq_count
    hidden = up_weight.shape[1]
    me = lax.axis_index("ctx")
    me_arr = me.astype(jnp.int32).reshape(1)
    width = -(-seq_count * model // (n * LANES)) * LANES
    used = seq_count * model // width
    per = model // width

    parts = n // 4
    own_rows = out_weight.shape[0]

    vectors = (
        norm1_gain, norm1_bias, norm2_gain, norm2_bias, qkv_bias, out_bias, up_bias, down_bias,
    )
    sizes = [v.shape[0] for v in vectors]
    packed = jnp.concatenate(vectors)
    lines = -(-packed.shape[0] // LANES)
    packed = jnp.pad(packed, (0, lines * LANES - packed.shape[0])).reshape(lines, LANES)
    flat = gather_lines(packed.reshape(1, lines * LANES), shards)
    whole, start = [], 0
    for size in sizes:
        whole.append(flat[:, start : start + size].astype(F32).reshape(1, shards * size))
        start += size
    gain_one, bias_one, gain_two, bias_two, b_qkv, b_out, b_up, b_down = whole

    w_up = lax.all_gather(up_weight, "fsdp", axis=0, tiled=True)
    units = jnp.concatenate(
        [qkv_weight[None, :, t * model : (t + 1) * model] for t in range(3)] + [out_weight[None]]
    )
    w_units = gather_units(units.reshape(n, own_rows // parts, model), n, shards)
    w_units = (
        w_units.reshape(4, parts, shards, own_rows // parts, model)
        .transpose(0, 2, 1, 3, 4)
        .reshape(4, model, model)
    )
    w_out = w_units[3]
    down_units, _ = lax.optimization_barrier(
        (down_weight.reshape(n, down_weight.shape[0] // n, model), w_units)
    )
    w_down = gather_units(down_units, n, shards, True).reshape(hidden, model)

    inputs = tokens.transpose(1, 0, 2).reshape(rows, model)
    cot = cotangent.transpose(1, 0, 2).reshape(rows, model)

    tables = rotary_tables(n * block_len)
    own_tables = tuple(
        lax.dynamic_slice_in_dim(jnp.asarray(t), me * block_len, block_len, 0) for t in tables
    )

    sent = project(
        n, me_arr, inputs, cot, gain_one, bias_one, w_units, b_qkv, own_tables, block_len, width, used
    )
    pieces = [sent[0]] + [swap(sent[shift], shift, n) for shift in range(1, n)]
    answers = attend(n, me_arr, pieces, tables)
    mlp_inputs, *answers = lax.optimization_barrier((inputs, *answers))
    answers = [answers[0]] + [swap(answers[shift], shift, n) for shift in range(1, n)]

    base, grad_base, grad_up, grad_down, grad_up_b, sums_two = mlp(
        mlp_inputs, cot, gain_two, bias_two, b_out + b_down, w_up, b_up, w_down
    )
    core = lax.axis_index("fsdp") % 2
    layer_out, tokens_grad, own, other, sums_one = finish(
        n, me, core, answers, inputs, cot, gain_one, bias_one, base, grad_base, w_units, shards, used
    )

    def placed(value):
        return value.reshape(seq_count, block_len, model).transpose(1, 0, 2)

    def cut(value):
        return (
            value.reshape(4, shards // 2, parts, own_rows // parts, model)
            .transpose(0, 2, 1, 3, 4)
            .reshape(n, shards // 2, own_rows // parts, model)
        )

    def shard_sum(value):
        return lax.psum_scatter(value, "fsdp", scatter_dimension=0, tiled=True)

    part_units = sum_units(cut(own), cut(other), n, shards).reshape(4, own_rows, model).astype(F32)
    part_qkv = jnp.concatenate([part_units[t] for t in range(3)], axis=1)
    part_down = sum_over_ctx(shard_sum(grad_down), n).astype(F32)
    part_up = sum_over_ctx(shard_sum(grad_up), n).astype(F32)

    line_sums = sum_lines(
        jnp.concatenate([sums_one, sums_two, grad_up_b.reshape(-1, model)], axis=0), n, shards
    )
    f = lax.axis_index("fsdp")

    def shard_of(first, count):
        size = count * model // shards
        return lax.dynamic_slice_in_dim(line_sums[first : first + count].reshape(-1), f * size, size, 0)

    columns = shard_of(10, 1)
    return (
        placed(layer_out), placed(tokens_grad), shard_of(4, 1), shard_of(5, 1), shard_of(8, 1),
        shard_of(9, 1), part_qkv, shard_of(1, 3), part_units[3], columns, part_up,
        shard_of(16, hidden // model), part_down, columns,
    )


def solution(mesh):
    blocks = P("ctx", "fsdp", None)
    line, matrix = P("fsdp"), P("fsdp", None)
    return jax.shard_map(
        body,
        mesh=mesh,
        in_specs=(
            blocks, line, line, line, line, matrix, line, matrix, line, matrix, line, matrix, line,
            blocks,
        ),
        out_specs=(
            blocks, blocks, line, line, line, line, matrix, line, matrix, line, matrix, line,
            matrix, line,
        ),
        check_vma=False,
    )
```

```python
import functools

import jax
import jax.numpy as jnp
import numpy as np
from jax import lax
from jax.experimental import pallas as pl
from jax.experimental.pallas import tpu as pltpu
from jax.sharding import PartitionSpec as P

H = 12
HD = 64
ROT = 16
LANES = 128
EPS = 1e-05
MASKED = -1e30
VMEM = 56 * 1024 * 1024
BF = jnp.bfloat16
F32 = jnp.float32


def dot(left, right, dims=((1,), (0,))):
    return lax.dot_general(left, right, (dims, ((), ())), preferred_element_type=F32)


def back_dot(left, right):
    return dot(left, right, ((1,), (1,)))


def outer_sum(left, right):
    return dot(left, right, ((0,), (0,)))


def normalized(values):
    center = values - jnp.mean(values, axis=-1, keepdims=True)
    spread = jnp.mean(center * center, axis=-1, keepdims=True)
    inverse = lax.rsqrt(spread + EPS)
    return center * inverse, inverse


def norm_back(hat, inverse, gain, grad):
    scaled = grad * gain
    first = jnp.mean(scaled, axis=-1, keepdims=True)
    second = jnp.mean(scaled * hat, axis=-1, keepdims=True)
    return (
        inverse * (scaled - first - hat * second),
        jnp.sum(grad * hat, axis=0, keepdims=True),
        jnp.sum(grad, axis=0, keepdims=True),
    )


def rotary_tables(length):
    half = ROT // 2
    inverse = np.float32(10000.0) ** (-np.arange(0, ROT, 2, dtype=np.float32) / np.float32(ROT))
    phase = np.arange(length, dtype=np.float32)[:, None] * inverse[None, :].astype(np.float32)
    cosine, sine = np.cos(phase), np.sin(phase)
    c = np.ones((length, HD), np.float32)
    s1 = np.zeros((length, HD), np.float32)
    s2 = np.zeros((length, HD), np.float32)
    c[:, :half] = cosine
    c[:, half:ROT] = cosine
    s1[:, :half] = -sine
    s2[:, half:ROT] = sine
    return tuple(np.concatenate([t, t], axis=1) for t in (c, s1, s2))


def turn(values, c, s1, s2):
    half = ROT // 2
    return (
        values * c
        + pltpu.roll(values, LANES - half, 1) * s1
        + pltpu.roll(values, half, 1) * s2
    )


def project_kernel(
    n, block_len, used, me, tokens, cot, gain, bias, w, b, c_ref, s1_ref, s2_ref, *rest
):
    outs, normed = rest[:n], rest[n]
    kind = pl.program_id(0)

    @pl.when(kind == 0)
    def _():
        hat, _inverse = normalized(tokens[...].astype(F32))
        normed[...] = (hat * gain[...] + bias[...]).astype(BF)

    width = outs[0].shape[-1]
    per = w.shape[-1] // width

    def operands(shift, left):
        group = jnp.minimum(me[0] ^ shift, used - 1)
        rows = pl.multiple_of((group // per) * block_len, block_len)
        cols = pl.multiple_of((group % per) * width, LANES)
        return left[pl.ds(rows, block_len)], pl.ds(cols, width)

    @pl.when(kind < 2)
    def _():
        c, s1, s2 = c_ref[...], s1_ref[...], s2_ref[...]
        for shift in range(n):
            left, cols = operands(shift, normed)
            full = dot(left, w[0, :, cols]) + b[0, :, cols]
            for j in range(width // LANES):
                at = slice(j * LANES, (j + 1) * LANES)
                outs[shift][0, :, at] = turn(full[:, at], c, s1, s2).astype(BF)

    @pl.when(kind == 2)
    def _():
        for shift in range(n):
            left, cols = operands(shift, normed)
            outs[shift][0] = (dot(left, w[0, :, cols]) + b[0, :, cols]).astype(BF)

    @pl.when(kind == 3)
    def _():
        for shift in range(n):
            left, cols = operands(shift, cot)
            outs[shift][0] = back_dot(left, w[0, cols]).astype(BF)


def project(n, me, tokens, cot, gain, bias, w, b, tables, block_len, width, used):
    rows, model = tokens.shape
    whole = pl.BlockSpec((rows, model), lambda kind, me_ref: (0, 0))
    line = pl.BlockSpec((1, model), lambda kind, me_ref: (0, 0))
    own = pl.BlockSpec((block_len, LANES), lambda kind, me_ref: (me_ref[0], 0))
    return pl.pallas_call(
        functools.partial(project_kernel, n, block_len, used),
        grid_spec=pltpu.PrefetchScalarGridSpec(
            num_scalar_prefetch=1,
            grid=(4,),
            in_specs=[
                whole,
                whole,
                line,
                line,
                pl.BlockSpec((1, model, model), lambda kind, me_ref: (kind, 0, 0)),
                pl.BlockSpec((1, 1, model), lambda kind, me_ref: (jnp.minimum(kind, 2), 0, 0)),
                own,
                own,
                own,
            ],
            out_specs=[pl.BlockSpec((1, block_len, width), lambda kind, me_ref: (kind, 0, 0))] * n,
            scratch_shapes=[pltpu.VMEM((rows, model), BF)],
        ),
        out_shape=[jax.ShapeDtypeStruct((4, block_len, width), BF)] * n,
        compiler_params=pltpu.CompilerParams(vmem_limit_bytes=VMEM),
        cost_estimate=pl.CostEstimate(
            flops=8 * rows * model * model,
            bytes_accessed=2 * (4 * model * model + 6 * rows * model),
            transcendentals=0,
        ),
        name="project",
    )(me, tokens, cot, gain, bias, w, b.reshape(3, 1, model), *(jnp.asarray(t) for t in tables))


def attend_kernel(n, block, me, *refs):
    ins = refs[:n]
    c_ref, s1_ref, s2_ref = refs[n : n + 3]
    outs = refs[n + 3 : 2 * n + 3]
    (q_s, k_s, v_s, g_s, qt_s, kt_s, vt_s, gt_s, sc, pb, dk, dv, o_s, dq_s) = refs[2 * n + 3 :]
    two = 2 * block
    scale = HD**-0.5

    for shift in range(n):
        at = ins[shift]
        place = me[0] ^ shift
        for kind, plain, flipped in ((0, q_s, qt_s), (1, k_s, kt_s), (2, v_s, vt_s), (3, g_s, gt_s)):
            piece = at[kind].astype(F32)
            if kind == 0:
                piece = piece * scale
            plain[place] = piece.astype(BF)
            flipped[place] = piece.T.astype(BF)

    lane = lax.broadcasted_iota(jnp.int32, (block, LANES), 1) < HD
    row = lax.broadcasted_iota(jnp.int32, (LANES, block), 0) < HD
    key_at = lax.broadcasted_iota(jnp.int32, (block, two), 0)
    query_at = lax.broadcasted_iota(jnp.int32, (block, two), 1)
    query_at = jnp.where(query_at >= block, query_at - block, query_at)
    allowed = key_at <= query_at

    def beside(flipped):
        zero = jnp.zeros_like(flipped)
        return jnp.concatenate([jnp.where(row, flipped, zero), jnp.where(row, zero, flipped)], axis=1)

    def below(plain):
        zero = jnp.zeros_like(plain)
        return jnp.concatenate([jnp.where(lane, plain, zero), jnp.where(lane, zero, plain)], axis=0)

    def loop(upto, body, init):
        if isinstance(upto, int):
            for j in range(upto):
                init = body(j, init)
            return init
        return lax.fori_loop(0, upto, body, init)

    def query_block(i, _):
        queries_t = beside(qt_s[i].astype(F32)).astype(BF)
        grads_t = beside(gt_s[i].astype(F32)).astype(BF)
        queries = below(q_s[i].astype(F32)).astype(BF)
        grads = below(g_s[i].astype(F32)).astype(BF)

        def score(j, top):
            found = dot(k_s[j], queries_t)
            sc[j] = found
            return jnp.maximum(top, jnp.max(found, axis=0, keepdims=True))

        diagonal = jnp.where(allowed, dot(k_s[i], queries_t), MASKED)
        sc[i] = diagonal
        top = loop(i, score, jnp.max(diagonal, axis=0, keepdims=True))

        def weigh(j, total):
            exps = jnp.exp(sc[j] - top)
            sc[j] = exps
            return total + jnp.sum(exps, axis=0, keepdims=True)

        total = loop(i + 1, weigh, jnp.zeros((1, two), F32))
        inverse = 1.0 / total

        def mix(j, heads):
            probs = sc[j] * inverse
            sc[j] = probs
            low = probs.astype(BF)
            pb[j] = low
            return tuple(
                heads[h] + dot(vt_s[j, h * HD : (h + 1) * HD], low[:, h * block : (h + 1) * block])
                for h in range(2)
            )

        none = jnp.zeros((HD, block), F32)
        heads = loop(i + 1, mix, (none, none))
        delta = jnp.concatenate(
            [
                jnp.sum(heads[h] * gt_s[i, h * HD : (h + 1) * HD].astype(F32), axis=0, keepdims=True)
                for h in range(2)
            ],
            axis=1,
        )
        o_s[i] = jnp.concatenate(heads, axis=0).T.astype(BF)

        def back(j, found, first):
            grad_scores = (sc[j] * (dot(v_s[j], grads_t) - delta)).astype(BF)
            key_part = dot(grad_scores, queries)
            value_part = dot(pb[j], grads)
            if first:
                dk[j] = key_part
                dv[j] = value_part
            else:
                dk[j] = dk[j] + key_part
                dv[j] = dv[j] + value_part
            return tuple(
                found[h]
                + dot(kt_s[j, h * HD : (h + 1) * HD], grad_scores[:, h * block : (h + 1) * block])
                for h in range(2)
            )

        found = back(i, (none, none), True)
        found = loop(i, lambda j, kept: back(j, kept, False), found)
        grad_query = jnp.concatenate(found, axis=0).T * scale
        dq_s[i] = turn(grad_query, c_ref[i], -s1_ref[i], -s2_ref[i]).astype(BF)
        return 0

    if n <= 4:
        for i in range(n):
            query_block(i, 0)
    else:
        lax.fori_loop(0, n, query_block, 0)

    for shift in range(n):
        place = me[0] ^ shift
        c, s1, s2 = c_ref[place], -s1_ref[place], -s2_ref[place]
        outs[shift][0] = o_s[place]
        outs[shift][1] = dq_s[place]
        outs[shift][2] = turn(dk[place], c, s1, s2).astype(BF)
        outs[shift][3] = dv[place].astype(BF)


def attend(n, me, pieces, tables):
    _, block, width = pieces[0].shape
    length = n * block
    spec = pl.BlockSpec((4, block, LANES), lambda j, me_ref: (0, 0, j))
    table_spec = pl.BlockSpec((n, block, LANES), lambda j, me_ref: (0, 0, 0))
    plain = pltpu.VMEM((n, block, LANES), BF)
    flipped = pltpu.VMEM((n, LANES, block), BF)
    total = pltpu.VMEM((n, block, LANES), F32)
    work = width // HD * length * (length + block) // 2
    return pl.pallas_call(
        functools.partial(attend_kernel, n, block),
        grid_spec=pltpu.PrefetchScalarGridSpec(
            num_scalar_prefetch=1,
            grid=(width // LANES,),
            in_specs=[spec] * n + [table_spec] * 3,
            out_specs=[spec] * n,
            scratch_shapes=[
                plain, plain, plain, plain,
                flipped, flipped, flipped, flipped,
                pltpu.VMEM((n, block, 2 * block), F32),
                pltpu.VMEM((n, block, 2 * block), BF),
                total, total, plain, plain,
            ],
        ),
        out_shape=[jax.ShapeDtypeStruct((4, block, width), BF)] * n,
        compiler_params=pltpu.CompilerParams(vmem_limit_bytes=VMEM),
        cost_estimate=pl.CostEstimate(
            flops=12 * work * 4 * HD * 10, bytes_accessed=2 * 8 * length * width, transcendentals=work
        ),
        name="attend",
    )(me, *pieces, *(jnp.asarray(t).reshape(n, block, LANES) for t in tables))


def mlp_kernel(
    tokens, cot, gain, bias, b_sum, w_up, b_up, w_down,
    out, grad_in, grad_up, grad_down, grad_b, sums,
    normed,
):
    step = pl.program_id(0)

    @pl.when(step == 0)
    def _():
        values = tokens[...].astype(F32)
        hat, _inverse = normalized(values)
        normed[...] = (hat * gain[...] + bias[...]).astype(BF)
        out[...] = values + b_sum[...]
        grad_in[...] = jnp.zeros_like(grad_in)

    hidden = dot(normed[...], w_up[...]) + b_up[...]
    share = 0.5 + 0.5 * lax.erf(hidden * (0.5**0.5))
    slope = share + hidden * (jnp.exp(-0.5 * hidden * hidden) * ((2.0 * np.pi) ** -0.5))
    active = (hidden * share).astype(BF)
    grad_hidden = (back_dot(cot[...], w_down[...]) * slope).astype(BF)
    grad_b[...] = jnp.sum(grad_hidden.astype(F32), axis=0, keepdims=True)
    out[...] = out[...] + dot(active, w_down[...])
    grad_in[...] = grad_in[...] + back_dot(grad_hidden, w_up[...])
    grad_down[...] = outer_sum(active, cot[...]).astype(BF)
    grad_up[...] = outer_sum(normed[...], grad_hidden).astype(BF)

    @pl.when(step == pl.num_programs(0) - 1)
    def _():
        hat, inverse = normalized(tokens[...].astype(F32))
        upstream = cot[...].astype(F32)
        back, grad_gain, grad_bias = norm_back(hat, inverse, gain[...], grad_in[...])
        grad_in[...] = upstream + back
        sums[0:1] = grad_gain
        sums[1:2] = grad_bias
        sums[2:3] = jnp.sum(upstream, axis=0, keepdims=True)
        sums[3:8] = jnp.zeros((5, sums.shape[1]), F32)


def mlp(tokens, cot, gain, bias, b_sum, w_up, b_up, w_down):
    rows, model = tokens.shape
    hidden = w_up.shape[1]
    chunk = 384
    whole = pl.BlockSpec((rows, model), lambda j: (0, 0))
    flat_line = pl.BlockSpec((1, model), lambda j: (0, 0))
    tall = pl.BlockSpec((model, chunk), lambda j: (0, j))
    flat = pl.BlockSpec((chunk, model), lambda j: (j, 0))
    line = pl.BlockSpec((1, chunk), lambda j: (0, j))
    return pl.pallas_call(
        mlp_kernel,
        grid=(hidden // chunk,),
        in_specs=[whole, whole, flat_line, flat_line, flat_line, tall, line, flat],
        out_specs=[whole, whole, tall, flat, line, pl.BlockSpec((8, model), lambda j: (0, 0))],
        out_shape=[
            jax.ShapeDtypeStruct((rows, model), F32),
            jax.ShapeDtypeStruct((rows, model), F32),
            jax.ShapeDtypeStruct((model, hidden), BF),
            jax.ShapeDtypeStruct((hidden, model), BF),
            jax.ShapeDtypeStruct((1, hidden), F32),
            jax.ShapeDtypeStruct((8, model), F32),
        ],
        scratch_shapes=[pltpu.VMEM((rows, model), BF)],
        compiler_params=pltpu.CompilerParams(vmem_limit_bytes=VMEM),
        cost_estimate=pl.CostEstimate(
            flops=12 * rows * model * hidden,
            bytes_accessed=8 * model * hidden + 12 * rows * model,
            transcendentals=2 * rows * hidden,
        ),
        name="mlp",
    )(tokens, cot, gain, bias, b_sum, w_up, b_up, w_down)


def finish_kernel(n, block_len, used, shards, at, *refs):
    answers = refs[:n]
    (tokens, cot, gain, bias, base, grad_base, w, out, grad_out, own, other, sums, normed, grad_in, held, grads) = refs[n:]
    kind = pl.program_id(0)
    width = answers[0].shape[-1]
    per = w.shape[-1] // width
    own_rows = own.shape[-2]

    for shift in range(n):
        group = jnp.minimum(at[0] ^ shift, used - 1)
        rows = pl.multiple_of((group // per) * block_len, block_len)
        cols = pl.multiple_of((group % per) * width, LANES)
        if used == n:
            held[pl.ds(rows, block_len), pl.ds(cols, width)] = answers[shift][0]
        else:
            @pl.when((at[0] ^ shift) < used)
            def _(rows=rows, cols=cols, shift=shift):
                held[pl.ds(rows, block_len), pl.ds(cols, width)] = answers[shift][0]

    @pl.when(kind == 0)
    def _():
        hat, _inverse = normalized(tokens[...].astype(F32))
        normed[...] = (hat * gain[...] + bias[...]).astype(BF)
        out[...] = (base[...] + dot(held[...], w[0])).astype(BF)
        grad_in[...] = jnp.zeros_like(grad_in)
        sums[...] = jnp.zeros_like(sums)
        grads[...] = outer_sum(held[...], cot[...]).astype(BF).reshape(grads.shape)

    @pl.when(kind > 0)
    def _():
        grads[...] = outer_sum(normed[...], held[...]).astype(BF).reshape(grads.shape)
        grad_in[...] = grad_in[...] + back_dot(held[...], w[0])
        sums[pl.ds(kind, 1)] = jnp.sum(held[...].astype(F32), axis=0, keepdims=True)

    for z in range(shards // 2):
        own[0, z] = grads[z, at[1]]
        other[0, z] = grads[z, at[1] ^ 1]

    @pl.when(kind == 3)
    def _():
        hat, inverse = normalized(tokens[...].astype(F32))
        back, grad_gain, grad_bias = norm_back(hat, inverse, gain[...], grad_in[...])
        grad_out[...] = (grad_base[...] + back).astype(BF)
        sums[4:5] = grad_gain
        sums[5:6] = grad_bias


def finish(n, me, core, answers, tokens, cot, gain, bias, base, grad_base, w, shards, used):
    rows, model = tokens.shape
    block_len, width = answers[0].shape[1:]
    whole = pl.BlockSpec((rows, model), lambda kind, at: (0, 0))
    line = pl.BlockSpec((1, model), lambda kind, at: (0, 0))
    own_rows = model // shards

    def unit(kind, at):
        return (lax.rem(kind + 3, 4), 0, 0)

    half = pl.BlockSpec(
        (1, shards // 2, own_rows, model), lambda kind, at: (lax.rem(kind + 3, 4), 0, 0, 0)
    )
    return pl.pallas_call(
        functools.partial(finish_kernel, n, block_len, used, shards),
        grid_spec=pltpu.PrefetchScalarGridSpec(
            num_scalar_prefetch=1,
            grid=(4,),
            in_specs=[pl.BlockSpec((1, block_len, width), lambda kind, at: (kind, 0, 0))] * n
            + [whole, whole, line, line, whole, whole, pl.BlockSpec((1, model, model), unit)],
            out_specs=[
                whole, whole, half, half, pl.BlockSpec((8, model), lambda kind, at: (0, 0)),
            ],
            scratch_shapes=[
                pltpu.VMEM((rows, model), BF),
                pltpu.VMEM((rows, model), F32),
                pltpu.VMEM((rows, model), BF),
                pltpu.VMEM((shards // 2, 2, own_rows, model), BF),
            ],
        ),
        out_shape=[
            jax.ShapeDtypeStruct((rows, model), BF),
            jax.ShapeDtypeStruct((rows, model), BF),
            jax.ShapeDtypeStruct((4, shards // 2, own_rows, model), BF),
            jax.ShapeDtypeStruct((4, shards // 2, own_rows, model), BF),
            jax.ShapeDtypeStruct((8, model), F32),
        ],
        compiler_params=pltpu.CompilerParams(vmem_limit_bytes=VMEM),
        cost_estimate=pl.CostEstimate(
            flops=16 * rows * model * model, bytes_accessed=40 * rows * model, transcendentals=0
        ),
        name="finish",
    )(jnp.stack([me, core]).astype(jnp.int32), *answers, tokens, cot, gain, bias, base, grad_base, w)


def swap(value, shift, n):
    return lax.ppermute(value, "ctx", [(i, i ^ shift) for i in range(n)])


def swap_shard(value, shift, m):
    return lax.ppermute(value, "fsdp", [(i, i ^ shift) for i in range(m)])


def assemble_kernel(where, counted, shard_first, at, *refs):
    ins, out = refs[:counted], refs[counted]
    for piece, index, place in where:
        unit, shard = place(at)
        if shard_first:
            out[shard, unit] = ins[piece][index]
        else:
            out[unit, shard] = ins[piece][index]


def along_z(units, m):
    mine = pick(units, lax.axis_index("ctx"))
    return jnp.stack([swap_shard(mine, step, m) for step in range(2, m, 2)])


def gather_lines(lines, m):
    chips = jnp.stack([lines] + [swap_shard(lines, step, m) for step in range(2, m, 2)])
    both = jnp.stack([chips, swap_shard(chips, 1, m)], axis=1).reshape((m,) + lines.shape)
    return in_order(both, lax.axis_index("fsdp"))


def between_columns(along, n):
    return [along] + [swap(along, shift, n) for shift in range(1, n)]


def between_cores(units, columns, n, m, shard_first=False):
    other = swap_shard(units, 1, m)
    crossed = [swap_shard(held, 1, m) for held in columns]
    steps = list(range(2, m, 2))
    pieces = [units, other] + columns + crossed
    where = []
    for unit in range(n):
        where.append((0, unit, lambda at, unit=unit: (unit, at[1])))
        where.append((1, unit, lambda at, unit=unit: (unit, at[1] ^ 1)))
    for core in range(2):
        for shift in range(n):
            for index, step in enumerate(steps):
                where.append(
                    (
                        2 + core * n + shift,
                        index,
                        lambda at, shift=shift, step=step, core=core: (at[0] ^ shift, at[1] ^ step ^ core),
                    )
                )
    full = ((m, n) if shard_first else (n, m)) + units.shape[1:]
    at = jnp.stack([lax.axis_index("ctx"), lax.axis_index("fsdp")]).astype(jnp.int32)
    return pl.pallas_call(
        functools.partial(assemble_kernel, where, len(pieces), shard_first),
        grid_spec=pltpu.PrefetchScalarGridSpec(
            num_scalar_prefetch=1,
            grid=(1,),
            in_specs=[pl.BlockSpec(p.shape, lambda i, at, r=p.ndim: (0,) * r) for p in pieces],
            out_specs=pl.BlockSpec(full, lambda i, at: (0, 0, 0, 0)),
        ),
        out_shape=jax.ShapeDtypeStruct(full, units.dtype),
        compiler_params=pltpu.CompilerParams(vmem_limit_bytes=VMEM),
        cost_estimate=pl.CostEstimate(flops=0, bytes_accessed=4 * m * units.size, transcendentals=0),
        name="assemble",
    )(at, *pieces)


def add_up(*pieces):
    return sum(p.astype(F32) for p in pieces).astype(BF)


def pick(value, at, axis=0):
    return lax.dynamic_index_in_dim(value, at, axis, keepdims=False)


def sum_units(own, other, lines, shard, n, m):
    q, z = lax.axis_index("ctx"), lax.axis_index("fsdp") // 2
    steps = range(1, n)
    shard_parts = shard.reshape((n, shard.shape[0] // n) + shard.shape[1:])

    own, other, shard_parts = lax.optimization_barrier((own, other, shard_parts))
    chip = add_up(own, swap_shard(other, 1, m))
    lines = lines + swap_shard(lines, 1, m)
    shard_sum = add_up(pick(shard_parts, q), *[swap(pick(shard_parts, q ^ s), s, n) for s in steps])
    unit = add_up(pick(chip, q), *[swap(pick(chip, q ^ s), s, n) for s in steps])
    lines = sum_in_order([lines] + [swap(lines, s, n) for s in steps], q)
    unit, shard_sum = lax.optimization_barrier((unit, shard_sum))
    shard_all = [shard_sum] + [swap(shard_sum, s, n) for s in steps]
    z_steps = range(1, m // 2)
    own = add_up(pick(unit, z), *[swap_shard(pick(unit, z ^ s), 2 * s, m) for s in z_steps])
    lines = sum_in_order([lines] + [swap_shard(lines, 2 * s, m) for s in z_steps], z)
    own, shard_all = lax.optimization_barrier((own, shard_all))
    every = in_order([own] + [swap(own, s, n) for s in steps], q)
    return every, in_order(shard_all, q).reshape(shard.shape), lines


def in_order(pieces, at):
    stacked = jnp.stack(pieces)
    return jnp.stack([pick(stacked, at ^ place) for place in range(len(pieces))])


def sum_in_order(pieces, at):
    return jnp.sum(in_order(pieces, at), axis=0)


def sum_over_ctx(shard, n):
    me = lax.axis_index("ctx")
    rows = shard.shape[0] // n
    parts = shard.reshape((n, rows) + shard.shape[1:])

    def part(at):
        return lax.dynamic_index_in_dim(parts, at, 0, keepdims=False)

    total = part(me).astype(F32)
    for shift in range(1, n):
        total = total + swap(part(me ^ shift), shift, n).astype(F32)
    own = total.astype(BF)
    gathered = jnp.stack([own] + [swap(own, shift, n) for shift in range(1, n)])
    return jnp.stack(
        [lax.dynamic_index_in_dim(gathered, me ^ at, 0, keepdims=False) for at in range(n)]
    ).reshape(shard.shape)


def body(
    tokens,
    norm1_gain,
    norm1_bias,
    norm2_gain,
    norm2_bias,
    qkv_weight,
    qkv_bias,
    out_weight,
    out_bias,
    up_weight,
    up_bias,
    down_weight,
    down_bias,
    cotangent,
):
    block_len, seq_count, model = tokens.shape
    n = lax.axis_size("ctx")
    shards = lax.axis_size("fsdp")
    rows = block_len * seq_count
    hidden = up_weight.shape[1]
    me = lax.axis_index("ctx")
    me_arr = me.astype(jnp.int32).reshape(1)
    width = -(-seq_count * model // (n * LANES)) * LANES
    used = seq_count * model // width
    per = model // width

    parts = n // 4
    own_rows = out_weight.shape[0]

    vectors = (
        norm1_gain, norm1_bias, norm2_gain, norm2_bias, qkv_bias, out_bias, up_bias, down_bias,
    )
    sizes = [v.shape[0] for v in vectors]
    packed = jnp.concatenate(vectors)
    lines = -(-packed.shape[0] // (8 * LANES)) * 8
    packed = jnp.pad(packed, (0, lines * LANES - packed.shape[0])).reshape(lines, LANES)

    units = jnp.concatenate(
        [qkv_weight[None, :, t * model : (t + 1) * model] for t in range(3)] + [out_weight[None]]
    ).reshape(n, own_rows // parts, model)
    along_units = along_z(units, shards)
    flat = gather_lines(packed, shards).reshape(shards, lines * LANES)
    down_units = down_weight.reshape(n, down_weight.shape[0] // n, model)
    down_units, up_weight, along_units = lax.optimization_barrier(
        (down_units, up_weight, along_units)
    )
    w_up = lax.all_gather(up_weight, "fsdp", axis=0, tiled=True)
    unit_columns = between_columns(along_units, n)
    along_down = along_z(down_units, shards)
    w_units = (
        between_cores(units, unit_columns, n, shards)
        .reshape(4, parts, shards, own_rows // parts, model)
        .transpose(0, 2, 1, 3, 4)
        .reshape(4, model, model)
    )
    along_down, _ = lax.optimization_barrier((along_down, w_units))
    down_columns = between_columns(along_down, n)
    whole, start = [], 0
    for size in sizes:
        whole.append(flat[:, start : start + size].astype(F32).reshape(1, shards * size))
        start += size
    gain_one, bias_one, gain_two, bias_two, b_qkv, b_out, b_up, b_down = whole

    inputs = tokens.transpose(1, 0, 2).reshape(rows, model)
    cot = cotangent.transpose(1, 0, 2).reshape(rows, model)

    tables = rotary_tables(n * block_len)
    def shard_sum(value):
        return lax.psum_scatter(value, "fsdp", scatter_dimension=0, tiled=True)

    sent = project(
        n, me_arr, inputs, cot, gain_one, bias_one, w_units, b_qkv, tables, block_len, width, used
    )
    pieces = [sent[0]] + [swap(sent[shift], shift, n) for shift in range(1, n)]
    mlp_inputs, down_columns, _ = lax.optimization_barrier((inputs, down_columns, sent))
    w_down = between_cores(down_units, down_columns, n, shards, True).reshape(hidden, model)
    base, grad_base, grad_up, grad_down, grad_up_b, sums_two = mlp(
        mlp_inputs, cot, gain_two, bias_two, b_out + b_down, w_up, b_up, w_down
    )
    grad_down, pieces = lax.optimization_barrier((grad_down, pieces))
    answers = attend(n, me_arr, pieces, tables)
    answers = [answers[0]] + [swap(answers[shift], shift, n) for shift in range(1, n)]
    shard_down, grad_up, answers = lax.optimization_barrier((shard_sum(grad_down), grad_up, answers))
    core = lax.axis_index("fsdp") % 2
    layer_out, tokens_grad, own, other, sums_one = finish(
        n, me, core, answers, inputs, cot, gain_one, bias_one, base, grad_base, w_units, shards, used
    )

    def placed(value):
        return value.reshape(seq_count, block_len, model).transpose(1, 0, 2)

    def cut(value):
        return (
            value.reshape(4, shards // 2, parts, own_rows // parts, model)
            .transpose(0, 2, 1, 3, 4)
            .reshape(n, shards // 2, own_rows // parts, model)
        )

    lines = jnp.concatenate([sums_one, sums_two, grad_up_b.reshape(-1, model)], axis=0)
    part_units, part_down, line_sums = sum_units(
        cut(own), cut(other), lines, shard_down, n, shards
    )
    part_units = part_units.reshape(4, own_rows, model).astype(F32)
    part_down = part_down.astype(F32)
    part_qkv = jnp.concatenate([part_units[t] for t in range(3)], axis=1)
    part_up = sum_over_ctx(shard_sum(grad_up), n).astype(F32)
    f = lax.axis_index("fsdp")

    def shard_of(first, count):
        size = count * model // shards
        return lax.dynamic_slice_in_dim(line_sums[first : first + count].reshape(-1), f * size, size, 0)

    columns = shard_of(10, 1)
    return (
        placed(layer_out), placed(tokens_grad), shard_of(4, 1), shard_of(5, 1), shard_of(8, 1),
        shard_of(9, 1), part_qkv, shard_of(1, 3), part_units[3], columns, part_up,
        shard_of(16, hidden // model), part_down, columns,
    )


def solution(mesh):
    blocks = P("ctx", "fsdp", None)
    line, matrix = P("fsdp"), P("fsdp", None)
    return jax.shard_map(
        body,
        mesh=mesh,
        in_specs=(
            blocks, line, line, line, line, matrix, line, matrix, line, matrix, line, matrix, line,
            blocks,
        ),
        out_specs=(
            blocks, blocks, line, line, line, line, matrix, line, matrix, line, matrix, line,
            matrix, line,
        ),
        check_vma=False,
    )
```

```python
import functools

import jax
import jax.numpy as jnp
import numpy as np
from jax import lax
from jax.experimental import pallas as pl
from jax.experimental.pallas import tpu as pltpu
from jax.sharding import PartitionSpec as P

H = 12
HD = 64
ROT = 16
LANES = 128
EPS = 1e-05
MASKED = -1e30
VMEM = 56 * 1024 * 1024
BF = jnp.bfloat16
F32 = jnp.float32


def dot(left, right, dims=((1,), (0,))):
    return lax.dot_general(left, right, (dims, ((), ())), preferred_element_type=F32)


def back_dot(left, right):
    return dot(left, right, ((1,), (1,)))


def outer_sum(left, right):
    return dot(left, right, ((0,), (0,)))


def normalized(values):
    center = values - jnp.mean(values, axis=-1, keepdims=True)
    spread = jnp.mean(center * center, axis=-1, keepdims=True)
    inverse = lax.rsqrt(spread + EPS)
    return center * inverse, inverse


def norm_back(hat, inverse, gain, grad):
    scaled = grad * gain
    first = jnp.mean(scaled, axis=-1, keepdims=True)
    second = jnp.mean(scaled * hat, axis=-1, keepdims=True)
    return (
        inverse * (scaled - first - hat * second),
        jnp.sum(grad * hat, axis=0, keepdims=True),
        jnp.sum(grad, axis=0, keepdims=True),
    )


def rotary_tables(length):
    half = ROT // 2
    inverse = np.float32(10000.0) ** (-np.arange(0, ROT, 2, dtype=np.float32) / np.float32(ROT))
    phase = np.arange(length, dtype=np.float32)[:, None] * inverse[None, :].astype(np.float32)
    cosine, sine = np.cos(phase), np.sin(phase)
    c = np.ones((length, HD), np.float32)
    s1 = np.zeros((length, HD), np.float32)
    s2 = np.zeros((length, HD), np.float32)
    c[:, :half] = cosine
    c[:, half:ROT] = cosine
    s1[:, :half] = -sine
    s2[:, half:ROT] = sine
    return tuple(np.concatenate([t, t], axis=1) for t in (c, s1, s2))


def turn(values, c, s1, s2):
    half = ROT // 2
    return (
        values * c
        + pltpu.roll(values, LANES - half, 1) * s1
        + pltpu.roll(values, half, 1) * s2
    )


def project_kernel(
    n, block_len, used, me, tokens, cot, vectors, c_ref, s1_ref, s2_ref, *rest
):
    own, other = rest[:2]
    columns, crossed = rest[2 : 2 + n], rest[2 + n : 2 + 2 * n]
    outs = rest[2 + 2 * n : 2 + 3 * n]
    w, normed, b, laid = rest[2 + 3 * n :]
    kind = pl.program_id(0)
    model = tokens.shape[1]
    parts = n // 4
    f = me[1]

    for part in range(parts):
        unit = kind * parts + part
        laid[f, part] = own[unit]
        laid[f ^ 1, part] = other[unit]
        for shift in range(n):

            @pl.when((unit ^ me[0]) == shift)
            def _(shift=shift, part=part):
                for index in range(columns[shift].shape[0]):
                    step = 2 * (index + 1)
                    laid[f ^ step, part] = columns[shift][index]
                    laid[f ^ step ^ 1, part] = crossed[shift][index]

    w[0] = laid[...].reshape(model, model)

    @pl.when(kind == 0)
    def _():
        hat, _inverse = normalized(tokens[...].astype(F32))
        normed[...] = (hat * vectors[0:1, :model] + vectors[1:2, :model]).astype(BF)

    for t in range(3):

        @pl.when(kind == t)
        def _(t=t):
            b[...] = vectors[4:5, t * model : (t + 1) * model]

    width = outs[0].shape[-1]
    per = w.shape[-1] // width

    def operands(shift, left):
        group = jnp.minimum(me[0] ^ shift, used - 1)
        rows = pl.multiple_of((group // per) * block_len, block_len)
        cols = pl.multiple_of((group % per) * width, LANES)
        return left[pl.ds(rows, block_len)], pl.ds(cols, width)

    @pl.when(kind < 2)
    def _():
        c, s1, s2 = c_ref[...], s1_ref[...], s2_ref[...]
        for shift in range(n):
            left, cols = operands(shift, normed)
            full = dot(left, w[0, :, cols]) + b[:, cols]
            for j in range(width // LANES):
                at = slice(j * LANES, (j + 1) * LANES)
                outs[shift][0, :, at] = turn(full[:, at], c, s1, s2).astype(BF)

    @pl.when(kind == 2)
    def _():
        for shift in range(n):
            left, cols = operands(shift, normed)
            outs[shift][0] = (dot(left, w[0, :, cols]) + b[:, cols]).astype(BF)

    @pl.when(kind == 3)
    def _():
        for shift in range(n):
            left, cols = operands(shift, cot)
            outs[shift][0] = back_dot(left, w[0, cols]).astype(BF)


def project(n, m, at, tokens, cot, vectors, pieces, tables, block_len, width, used):
    rows, model = tokens.shape
    parts = n // 4
    whole = pl.BlockSpec((rows, model), lambda kind, me_ref: (0, 0))
    own = pl.BlockSpec((block_len, LANES), lambda kind, me_ref: (me_ref[0], 0))
    return pl.pallas_call(
        functools.partial(project_kernel, n, block_len, used),
        grid_spec=pltpu.PrefetchScalarGridSpec(
            num_scalar_prefetch=1,
            grid=(4,),
            in_specs=[
                whole,
                whole,
                pl.BlockSpec(vectors.shape, lambda kind, me_ref: (0, 0)),
                own,
                own,
                own,
            ]
            + [pl.BlockSpec(p.shape, lambda kind, me_ref: (0, 0, 0)) for p in pieces],
            out_specs=[pl.BlockSpec((1, block_len, width), lambda kind, me_ref: (kind, 0, 0))] * n
            + [pl.BlockSpec((1, model, model), lambda kind, me_ref: (kind, 0, 0))],
            scratch_shapes=[
                pltpu.VMEM((rows, model), BF),
                pltpu.VMEM((1, model), F32),
                pltpu.VMEM((m, parts, model // m // parts, model), BF),
            ],
        ),
        out_shape=[jax.ShapeDtypeStruct((4, block_len, width), BF)] * n
        + [jax.ShapeDtypeStruct((4, model, model), BF)],
        compiler_params=pltpu.CompilerParams(vmem_limit_bytes=VMEM),
        cost_estimate=pl.CostEstimate(
            flops=8 * rows * model * model,
            bytes_accessed=2 * (4 * model * model + 6 * rows * model),
            transcendentals=0,
        ),
        name="project",
    )(at, tokens, cot, vectors, *(jnp.asarray(t) for t in tables), *pieces)


def attend_kernel(n, block, me, *refs):
    ins = refs[:n]
    c_ref, s1_ref, s2_ref = refs[n : n + 3]
    outs = refs[n + 3 : 2 * n + 3]
    (q_s, k_s, v_s, g_s, qt_s, kt_s, vt_s, gt_s, sc, pb, dk, dv, o_s, dq_s) = refs[2 * n + 3 :]
    two = 2 * block
    scale = HD**-0.5

    for shift in range(n):
        at = ins[shift]
        place = me[0] ^ shift
        for kind, plain, flipped in ((0, q_s, qt_s), (1, k_s, kt_s), (2, v_s, vt_s), (3, g_s, gt_s)):
            piece = at[kind].astype(F32)
            if kind == 0:
                piece = piece * scale
            plain[place] = piece.astype(BF)
            flipped[place] = piece.T.astype(BF)

    lane = lax.broadcasted_iota(jnp.int32, (block, LANES), 1) < HD
    row = lax.broadcasted_iota(jnp.int32, (LANES, block), 0) < HD
    key_at = lax.broadcasted_iota(jnp.int32, (block, two), 0)
    query_at = lax.broadcasted_iota(jnp.int32, (block, two), 1)
    query_at = jnp.where(query_at >= block, query_at - block, query_at)
    allowed = key_at <= query_at

    def beside(flipped):
        zero = jnp.zeros_like(flipped)
        return jnp.concatenate([jnp.where(row, flipped, zero), jnp.where(row, zero, flipped)], axis=1)

    def below(plain):
        zero = jnp.zeros_like(plain)
        return jnp.concatenate([jnp.where(lane, plain, zero), jnp.where(lane, zero, plain)], axis=0)

    def loop(upto, body, init):
        if isinstance(upto, int):
            for j in range(upto):
                init = body(j, init)
            return init
        return lax.fori_loop(0, upto, body, init)

    def query_block(i, _):
        queries_t = beside(qt_s[i].astype(F32)).astype(BF)
        grads_t = beside(gt_s[i].astype(F32)).astype(BF)
        queries = below(q_s[i].astype(F32)).astype(BF)
        grads = below(g_s[i].astype(F32)).astype(BF)

        def score(j, top):
            found = dot(k_s[j], queries_t)
            sc[j] = found
            return jnp.maximum(top, jnp.max(found, axis=0, keepdims=True))

        diagonal = jnp.where(allowed, dot(k_s[i], queries_t), MASKED)
        sc[i] = diagonal
        top = loop(i, score, jnp.max(diagonal, axis=0, keepdims=True))

        def weigh(j, total):
            exps = jnp.exp(sc[j] - top)
            sc[j] = exps
            return total + jnp.sum(exps, axis=0, keepdims=True)

        total = loop(i + 1, weigh, jnp.zeros((1, two), F32))
        inverse = 1.0 / total

        def mix(j, heads):
            probs = sc[j] * inverse
            sc[j] = probs
            low = probs.astype(BF)
            pb[j] = low
            return tuple(
                heads[h] + dot(vt_s[j, h * HD : (h + 1) * HD], low[:, h * block : (h + 1) * block])
                for h in range(2)
            )

        none = jnp.zeros((HD, block), F32)
        heads = loop(i + 1, mix, (none, none))
        delta = jnp.concatenate(
            [
                jnp.sum(heads[h] * gt_s[i, h * HD : (h + 1) * HD].astype(F32), axis=0, keepdims=True)
                for h in range(2)
            ],
            axis=1,
        )
        o_s[i] = jnp.concatenate(heads, axis=0).T.astype(BF)

        def back(j, found, first):
            grad_scores = (sc[j] * (dot(v_s[j], grads_t) - delta)).astype(BF)
            key_part = dot(grad_scores, queries)
            value_part = dot(pb[j], grads)
            if first:
                dk[j] = key_part
                dv[j] = value_part
            else:
                dk[j] = dk[j] + key_part
                dv[j] = dv[j] + value_part
            return tuple(
                found[h]
                + dot(kt_s[j, h * HD : (h + 1) * HD], grad_scores[:, h * block : (h + 1) * block])
                for h in range(2)
            )

        found = back(i, (none, none), True)
        found = loop(i, lambda j, kept: back(j, kept, False), found)
        grad_query = jnp.concatenate(found, axis=0).T * scale
        dq_s[i] = turn(grad_query, c_ref[i], -s1_ref[i], -s2_ref[i]).astype(BF)
        return 0

    if n <= 4:
        for i in range(n):
            query_block(i, 0)
    else:
        lax.fori_loop(0, n, query_block, 0)

    for shift in range(n):
        place = me[0] ^ shift
        c, s1, s2 = c_ref[place], -s1_ref[place], -s2_ref[place]
        outs[shift][0] = o_s[place]
        outs[shift][1] = dq_s[place]
        outs[shift][2] = turn(dk[place], c, s1, s2).astype(BF)
        outs[shift][3] = dv[place].astype(BF)


def attend(n, me, pieces, tables):
    _, block, width = pieces[0].shape
    length = n * block
    spec = pl.BlockSpec((4, block, LANES), lambda j, me_ref: (0, 0, j))
    table_spec = pl.BlockSpec((n, block, LANES), lambda j, me_ref: (0, 0, 0))
    plain = pltpu.VMEM((n, block, LANES), BF)
    flipped = pltpu.VMEM((n, LANES, block), BF)
    total = pltpu.VMEM((n, block, LANES), F32)
    work = width // HD * length * (length + block) // 2
    return pl.pallas_call(
        functools.partial(attend_kernel, n, block),
        grid_spec=pltpu.PrefetchScalarGridSpec(
            num_scalar_prefetch=1,
            grid=(width // LANES,),
            in_specs=[spec] * n + [table_spec] * 3,
            out_specs=[spec] * n,
            scratch_shapes=[
                plain, plain, plain, plain,
                flipped, flipped, flipped, flipped,
                pltpu.VMEM((n, block, 2 * block), F32),
                pltpu.VMEM((n, block, 2 * block), BF),
                total, total, plain, plain,
            ],
        ),
        out_shape=[jax.ShapeDtypeStruct((4, block, width), BF)] * n,
        compiler_params=pltpu.CompilerParams(vmem_limit_bytes=VMEM),
        cost_estimate=pl.CostEstimate(
            flops=12 * work * 4 * HD * 10, bytes_accessed=2 * 8 * length * width, transcendentals=work
        ),
        name="attend",
    )(me, *pieces, *(jnp.asarray(t).reshape(n, block, LANES) for t in tables))


def mlp_kernel(last, *refs):
    tokens, cot, vectors, w_up, b_up, w_down = refs[:6]
    model = tokens.shape[1]
    if last:
        start_out, start_grad, out, grad_in, grad_up, grad_down, grad_b, sums, normed = refs[6:]
    else:
        out, grad_in, grad_up, grad_down, grad_b, normed = refs[6:]
    step = pl.program_id(0)
    row = 7 if last else 6
    gain, bias = vectors[2:3, :model], vectors[3:4, :model]

    @pl.when(step == 0)
    def _():
        values = tokens[...].astype(F32)
        hat, _inverse = normalized(values)
        normed[...] = (hat * gain + bias).astype(BF)
        if last:
            out[...] = start_out[...]
            grad_in[...] = start_grad[...]
        else:
            out[...] = values + (vectors[5:6, :model] + vectors[8:9, :model])
            grad_in[...] = jnp.zeros_like(grad_in)

    up = w_up[...].reshape(model, -1)
    down = w_down[...].reshape(-1, model)
    hidden = dot(normed[...], up) + b_up[row : row + 1]
    share = 0.5 + 0.5 * lax.erf(hidden * (0.5**0.5))
    slope = share + hidden * (jnp.exp(-0.5 * hidden * hidden) * ((2.0 * np.pi) ** -0.5))
    active = (hidden * share).astype(BF)
    grad_hidden = (back_dot(cot[...], down) * slope).astype(BF)
    grad_b[...] = jnp.sum(grad_hidden.astype(F32), axis=0, keepdims=True)
    out[...] = out[...] + dot(active, down)
    grad_in[...] = grad_in[...] + back_dot(grad_hidden, up)
    grad_down[...] = outer_sum(active, cot[...]).astype(BF).reshape(grad_down.shape)
    grad_up[...] = outer_sum(normed[...], grad_hidden).astype(BF).reshape(grad_up.shape)

    if last:

        @pl.when(step == pl.num_programs(0) - 1)
        def _():
            hat, inverse = normalized(tokens[...].astype(F32))
            upstream = cot[...].astype(F32)
            back, grad_gain, grad_bias = norm_back(hat, inverse, gain, grad_in[...])
            grad_in[...] = upstream + back
            sums[0:1] = grad_gain
            sums[1:2] = grad_bias
            sums[2:3] = jnp.sum(upstream, axis=0, keepdims=True)
            sums[3:8] = jnp.zeros((5, sums.shape[1]), F32)


def mlp(tokens, cot, vectors, weights, start=None):
    rows, model = tokens.shape
    shards, units, shard_rows, _ = weights.shape
    half = units // 2 * model
    chunk = model // 2
    group = chunk * shards // half
    last = start is not None
    whole = pl.BlockSpec((rows, model), lambda j: (0, 0))
    line = pl.BlockSpec((1, chunk), lambda j: (0, j))
    tall = (shards, 1, shard_rows, chunk)
    flat = (group, units // 2, shard_rows, model)
    total = jax.ShapeDtypeStruct((rows, model), F32)
    grads = jax.ShapeDtypeStruct((shards, units // 2, shard_rows, model), BF)
    return pl.pallas_call(
        functools.partial(mlp_kernel, last),
        grid=(half // chunk,),
        in_specs=[
            whole,
            whole,
            pl.BlockSpec(vectors.shape, lambda j: (0, 0)),
            pl.BlockSpec(tall, lambda j: (0, j // 2, 0, j % 2)),
            pl.BlockSpec((16, chunk), lambda j: (0, j)),
            pl.BlockSpec(flat, lambda j: (j, 1, 0, 0)),
        ]
        + [whole] * (2 * last),
        out_specs=[
            whole,
            whole,
            pl.BlockSpec(tall, lambda j: (0, j // 2, 0, j % 2)),
            pl.BlockSpec(flat, lambda j: (j, 0, 0, 0)),
            line,
        ]
        + ([pl.BlockSpec((8, model), lambda j: (0, 0))] if last else []),
        out_shape=[total, total, grads, grads, jax.ShapeDtypeStruct((1, half), F32)]
        + ([jax.ShapeDtypeStruct((8, model), F32)] if last else []),
        scratch_shapes=[pltpu.VMEM((rows, model), BF)],
        compiler_params=pltpu.CompilerParams(vmem_limit_bytes=VMEM),
        cost_estimate=pl.CostEstimate(
            flops=12 * rows * model * half,
            bytes_accessed=8 * model * half + 12 * rows * model,
            transcendentals=2 * rows * half,
        ),
        name="mlp",
    )(tokens, cot, vectors, weights, vectors, weights, *(start or ()))


def finish_kernel(n, block_len, used, shards, at, *refs):
    answers = refs[:n]
    tokens, cot, vectors, base, grad_base, w, sums_two, grad_b = refs[n : n + 8]
    out, grad_out, own, other, line_own, line_other = refs[n + 8 : n + 14]
    held, normed, grads, grad_in, sums, lines = refs[n + 14 :]
    kind = pl.program_id(0)
    model = tokens.shape[1]
    width = answers[0].shape[-1]
    per = model // width

    for shift in range(n):
        group = jnp.minimum(at[0] ^ shift, used - 1)
        rows = pl.multiple_of((group // per) * block_len, block_len)
        cols = pl.multiple_of((group % per) * width, LANES)
        if used == n:
            held[pl.ds(rows, block_len), pl.ds(cols, width)] = answers[shift][0]
        else:

            @pl.when((at[0] ^ shift) < used)
            def _(rows=rows, cols=cols, shift=shift):
                held[pl.ds(rows, block_len), pl.ds(cols, width)] = answers[shift][0]

    @pl.when(kind == 0)
    def _():
        hat, _inverse = normalized(tokens[...].astype(F32))
        normed[...] = (hat * vectors[0:1, :model] + vectors[1:2, :model]).T.astype(BF)
        grad_in[...] = jnp.zeros_like(grad_in)
        out[...] = (base[...] + dot(held[...], w[0])).astype(BF)
        grads[...] = outer_sum(held[...], cot[...]).astype(BF).reshape(grads.shape)

    @pl.when(kind > 0)
    def _():
        grads[...] = dot(normed[...], held[...]).astype(BF).reshape(grads.shape)
        grad_in[...] = grad_in[...] + back_dot(held[...], w[0])
        sums[pl.ds(kind, 1)] = jnp.sum(held[...].astype(F32), axis=0, keepdims=True)

    for z in range(shards // 2):
        own[0, z] = grads[z, at[1]]
        other[0, z] = grads[z, at[1] ^ 1]

    @pl.when(kind == 3)
    def _():
        hat, inverse = normalized(tokens[...].astype(F32))
        back, grad_gain, grad_bias = norm_back(hat, inverse, vectors[0:1, :model], grad_in[...])
        grad_out[...] = (grad_base[...] + back).astype(BF)
        qkv = jnp.concatenate([sums[t : t + 1] for t in (1, 2, 3)], axis=1)
        whole = [
            grad_gain, grad_bias, sums_two[0:1], sums_two[1:2], sums_two[2:3], qkv, grad_b[0:1],
            grad_b[1:2],
        ]
        lines[...] = jnp.zeros_like(lines)
        for index, line in enumerate(whole):
            size = line.shape[1] // shards
            for f in range(shards):
                lines[f // 2, f % 2, index : index + 1, :size] = line[:, f * size : (f + 1) * size]
        for z in range(shards // 2):
            line_own[z] = lines[z, at[1]]
            line_other[z] = lines[z, at[1] ^ 1]


def finish(n, me, core, answers, tokens, cot, vectors, base, grad_base, w, sums_two, grad_b, shards, used):
    rows, model = tokens.shape
    block_len, width = answers[0].shape[1:]
    whole = pl.BlockSpec((rows, model), lambda kind, at: (0, 0))
    own_rows = model // shards

    def unit(kind, at):
        return lax.rem(kind + 3, 4)

    half = pl.BlockSpec(
        (1, shards // 2, own_rows, model), lambda kind, at: (unit(kind, at), 0, 0, 0)
    )
    half_shape = jax.ShapeDtypeStruct((4, shards // 2, own_rows, model), BF)
    half_lines = pl.BlockSpec((shards // 2, 8, model), lambda kind, at: (0, 0, 0))
    half_lines_shape = jax.ShapeDtypeStruct((shards // 2, 8, model), F32)
    return pl.pallas_call(
        functools.partial(finish_kernel, n, block_len, used, shards),
        grid_spec=pltpu.PrefetchScalarGridSpec(
            num_scalar_prefetch=1,
            grid=(4,),
            in_specs=[pl.BlockSpec((1, block_len, width), lambda kind, at: (kind, 0, 0))] * n
            + [
                whole,
                whole,
                pl.BlockSpec(vectors.shape, lambda kind, at: (0, 0)),
                whole,
                whole,
                pl.BlockSpec((1, model, model), lambda kind, at: (unit(kind, at), 0, 0)),
                pl.BlockSpec((8, model), lambda kind, at: (0, 0)),
                pl.BlockSpec(grad_b.shape, lambda kind, at: (0, 0)),
            ],
            out_specs=[whole, whole, half, half, half_lines, half_lines],
            scratch_shapes=[
                pltpu.VMEM((rows, model), BF),
                pltpu.VMEM((model, rows), BF),
                pltpu.VMEM((shards // 2, 2, own_rows, model), BF),
                pltpu.VMEM((rows, model), F32),
                pltpu.VMEM((8, model), F32),
                pltpu.VMEM((shards // 2, 2, 8, model), F32),
            ],
        ),
        out_shape=[
            jax.ShapeDtypeStruct((rows, model), BF),
            jax.ShapeDtypeStruct((rows, model), BF),
            half_shape,
            half_shape,
            half_lines_shape,
            half_lines_shape,
        ],
        compiler_params=pltpu.CompilerParams(vmem_limit_bytes=VMEM),
        cost_estimate=pl.CostEstimate(
            flops=16 * rows * model * model, bytes_accessed=40 * rows * model, transcendentals=0
        ),
        name="finish",
    )(
        jnp.stack([me, core]).astype(jnp.int32),
        *answers, tokens, cot, vectors, base, grad_base, w, sums_two, grad_b,
    )


def swap(value, shift, n):
    return lax.ppermute(value, "ctx", [(i, i ^ shift) for i in range(n)])


def swap_shard(value, shift, m):
    return lax.ppermute(value, "fsdp", [(i, i ^ shift) for i in range(m)])


def pack_kernel(*refs):
    out = refs[-1]
    rows = []
    for ref in refs[:-1]:
        line = ref[...].astype(F32)
        rows.append(jnp.concatenate([line, jnp.zeros((1, out.shape[1] - line.shape[1]), F32)], axis=1))
    rows.append(jnp.zeros((out.shape[0] - len(rows), out.shape[1]), F32))
    out[...] = jnp.concatenate(rows, axis=0).astype(BF)


def pack(vectors, width):
    return pl.pallas_call(
        pack_kernel,
        out_shape=jax.ShapeDtypeStruct((16, width), BF),
        name="pack",
    )(*[v.reshape(1, -1) for v in vectors])


def unpack_kernel(sizes, half, at, own, other, out):
    chips = own.shape[0]
    out[...] = jnp.zeros_like(out)
    rows = []
    for f in range(2 * chips):
        rel = f ^ at[0]
        both = jnp.where(rel % 2 == 0, own[rel // 2].astype(F32), other[rel // 2].astype(F32))
        rows.append(both)
    for index, size in enumerate(sizes):
        if index == half + 1:
            continue
        if index == half:
            cut = size // 2
            for h in range(2):
                line = [r[index : index + 1, h * cut : (h + 1) * cut] for r in rows]
                out[index + h : index + h + 1, : len(rows) * cut] = jnp.concatenate(line, axis=1)
        else:
            line = [r[index : index + 1, :size] for r in rows]
            out[index : index + 1, : len(rows) * size] = jnp.concatenate(line, axis=1)


def unpack(f, own, other, sizes, half):
    width = 2 * own.shape[0] * max(sizes[:half] + [sizes[half] // 2])
    full = pl.BlockSpec(own.shape, lambda i, at: (0, 0, 0))
    return pl.pallas_call(
        functools.partial(unpack_kernel, sizes, half),
        grid_spec=pltpu.PrefetchScalarGridSpec(
            num_scalar_prefetch=1,
            grid=(1,),
            in_specs=[full, full],
            out_specs=pl.BlockSpec((16, width), lambda i, at: (0, 0)),
        ),
        out_shape=jax.ShapeDtypeStruct((16, width), F32),
        name="unpack",
    )(f.astype(jnp.int32).reshape(1), own, other)


def along_z(units, m, extra=None):
    mine = pick(units, lax.axis_index("ctx"))
    rows = mine.shape[0]
    if extra is None:
        return [swap_shard(mine, step, m) for step in range(2, m, 2)]
    mine = jnp.concatenate([mine, extra], axis=0)
    came = [swap_shard(mine, step, m) for step in range(2, m, 2)]
    return jnp.stack([c[:rows] for c in came]), jnp.stack([extra] + [c[rows:] for c in came])


def between_columns(along, n):
    return [along] + [swap(along, shift, n) for shift in range(1, n)]


def assemble_kernel(where, at, *refs):
    out = refs[-1]
    for piece, index, place in where:
        unit, shard = place(at)
        out[shard, unit] = refs[piece][index]


def assemble(at, pieces, n, m):
    where = []
    for unit in range(n):
        where.append((0, unit, lambda at, unit=unit: (unit, at[1])))
        where.append((1, unit, lambda at, unit=unit: (unit, at[1] ^ 1)))
    for core in range(2):
        for shift in range(n):
            for index in range(m // 2 - 1):
                where.append(
                    (
                        2 + core * n + shift,
                        index,
                        lambda at, shift=shift, flip=2 * (index + 1) ^ core: (at[0] ^ shift, at[1] ^ flip),
                    )
                )
    full = (m, n) + pieces[0].shape[1:]
    return pl.pallas_call(
        functools.partial(assemble_kernel, where),
        grid_spec=pltpu.PrefetchScalarGridSpec(
            num_scalar_prefetch=1,
            grid=(1,),
            in_specs=[pl.BlockSpec(p.shape, lambda i, at: (0, 0, 0)) for p in pieces],
            out_specs=pl.BlockSpec(full, lambda i, at: (0, 0, 0, 0)),
        ),
        out_shape=jax.ShapeDtypeStruct(full, pieces[0].dtype),
        compiler_params=pltpu.CompilerParams(vmem_limit_bytes=VMEM),
        name="assemble",
    )(at, *pieces)


def add_up(*pieces):
    return sum(p.astype(F32) for p in pieces).astype(BF)


def pick(value, at, axis=0):
    return lax.dynamic_index_in_dim(value, at, axis, keepdims=False)


def swapped(value, n):
    return [value] + [swap(value, s, n) for s in range(1, n)]


def sum_over_ctx(shard, n):
    steps = [2**i for i in range(n.bit_length() - 1)]
    half = shard.shape[0] // 2
    halves = [shard[:half], shard[half:]]
    for i in range(len(steps)):
        for j in range(2):
            value = halves[j] if i == 0 else add_up(*halves[j])
            halves[j] = (value, swap(value, steps[(i + j) % len(steps)], n))
    return [term for half in halves for term in half]


def lay_kernel(shards, *refs):
    up, down = refs[8:]
    model = up.shape[1] // 4
    size = up.shape[1] // shards // 2
    ups = []
    for h in range(2):
        terms = refs[4 * h : 4 * h + 4]
        total = terms[0][...].astype(F32) + terms[1][...].astype(F32)
        ups.append(jnp.concatenate([total[0], total[1]], axis=1))
        rows = down.shape[0] // 4
        for unit in range(2):
            at = (2 * h + unit) * rows
            down[at : at + rows] = terms[2][unit].astype(F32) + terms[3][unit].astype(F32)
    for f in range(shards):
        line = [ups[h][:, f * size : (f + 1) * size] for h in range(2)]
        up[:, 2 * f * size : 2 * (f + 1) * size] = jnp.concatenate(line, axis=1)


def lay(first, second, shards, up_shape, down_shape):
    return pl.pallas_call(
        functools.partial(lay_kernel, shards),
        out_shape=[jax.ShapeDtypeStruct(up_shape, F32), jax.ShapeDtypeStruct(down_shape, F32)],
        compiler_params=pltpu.CompilerParams(vmem_limit_bytes=VMEM),
        name="lay",
    )(*first, *second)


def in_order(pieces, at):
    stacked = jnp.stack(pieces)
    return jnp.stack([pick(stacked, at ^ place) for place in range(len(pieces))])


def body(
    tokens,
    norm1_gain,
    norm1_bias,
    norm2_gain,
    norm2_bias,
    qkv_weight,
    qkv_bias,
    out_weight,
    out_bias,
    up_weight,
    up_bias,
    down_weight,
    down_bias,
    cotangent,
):
    block_len, seq_count, model = tokens.shape
    n = lax.axis_size("ctx")
    shards = lax.axis_size("fsdp")
    rows = block_len * seq_count
    hidden = up_weight.shape[1]
    me = lax.axis_index("ctx")
    me_arr = me.astype(jnp.int32).reshape(1)
    width = -(-seq_count * model // (n * LANES)) * LANES
    used = seq_count * model // width
    per = model // width

    parts = n // 4
    own_rows = out_weight.shape[0]

    vectors = (
        norm1_gain, norm1_bias, norm2_gain, norm2_bias, qkv_bias, out_bias, up_bias, out_bias,
        down_bias,
    )
    sizes = [v.shape[0] for v in vectors]
    packed = pack(vectors, model)

    per_shard = hidden // shards // 2

    def half_weights(h):
        up = up_weight.reshape(own_rows, shards, 2, per_shard)[:, :, h].reshape(own_rows, -1, model)
        down = down_weight[h * per_shard : (h + 1) * per_shard].reshape(-1, own_rows, model)
        return jnp.concatenate([up.transpose(1, 0, 2), down], axis=0)

    units = jnp.concatenate(
        [qkv_weight[None, :, t * model : (t + 1) * model] for t in range(3)] + [out_weight[None]]
    ).reshape(n, own_rows // parts, model)
    along_units, chips = along_z(units, shards, packed)
    first_half, second_half, _ = lax.optimization_barrier(
        (half_weights(0), half_weights(1), along_units)
    )
    w_first = lax.all_gather(first_half, "fsdp", axis=0, tiled=False)
    unit_columns = between_columns(along_units, n)
    vectors = unpack(
        lax.axis_index("fsdp"), chips, swap_shard(chips, 1, shards), sizes, 6
    )
    vectors, unit_columns = lax.optimization_barrier((vectors, unit_columns))
    crossed = [swap_shard(held, 1, shards) for held in unit_columns]
    unit_pieces = [units, swap_shard(units, 1, shards)] + unit_columns + crossed

    inputs = tokens.transpose(1, 0, 2).reshape(rows, model)
    cot = cotangent.transpose(1, 0, 2).reshape(rows, model)

    tables = rotary_tables(n * block_len)
    def shard_sum(value):
        return lax.psum_scatter(value, "fsdp", scatter_dimension=0, tiled=False)

    at = jnp.stack([me, lax.axis_index("fsdp")]).astype(jnp.int32)
    *sent, w_units = project(
        n, shards, at, inputs, cot, vectors, unit_pieces, tables, block_len, width, used
    )
    pieces = [sent[0]] + [swap(sent[shift], shift, n) for shift in range(1, n)]
    mlp_inputs, second_half, _ = lax.optimization_barrier((inputs, second_half, (sent, w_first)))
    second_units = second_half.reshape(n, -1, model)
    along_second = along_z(second_units, shards)
    base, grad_base, grad_up, grad_down, grad_b_first = mlp(
        mlp_inputs, cot, vectors, w_first
    )
    first_grads, pieces = lax.optimization_barrier(
        (jnp.concatenate([grad_up, grad_down], axis=1), pieces)
    )
    first_shard = shard_sum(first_grads)
    along_second, _ = lax.optimization_barrier((along_second, pieces))
    second_columns = between_columns(jnp.stack(along_second), n)
    made = attend(n, me_arr, pieces, tables)
    mlp_inputs, second_columns, second_units, _ = lax.optimization_barrier(
        (inputs, second_columns, second_units, made)
    )
    second_pieces = [second_units, swap_shard(second_units, 1, shards)] + second_columns
    second_pieces += [swap_shard(held, 1, shards) for held in second_columns]
    w_second = assemble(at, second_pieces, n, shards).reshape(shards, 4, own_rows, model)
    answers = [made[0]] + [swap(made[shift], shift, n) for shift in range(1, n)]
    base, grad_base, grad_up, grad_down, grad_b_second, sums_two = mlp(
        mlp_inputs, cot, vectors, w_second, start=(base, grad_base)
    )
    second_grads, answers = lax.optimization_barrier(
        (jnp.concatenate([grad_up, grad_down], axis=1), answers)
    )
    second_shard = shard_sum(second_grads)
    core = lax.axis_index("fsdp") % 2
    layer_out, tokens_grad, own, other, line_own, line_other = finish(
        n, me, core, answers, inputs, cot, vectors, base, grad_base, w_units, sums_two,
        jnp.concatenate([grad_b_first, grad_b_second]), shards, used,
    )

    def placed(value):
        return value.reshape(seq_count, block_len, model).transpose(1, 0, 2)

    z = lax.axis_index("fsdp") // 2
    chip = add_up(own, swap_shard(other, 1, shards))
    line_chip = add_up(line_own, swap_shard(line_other, 1, shards))
    chip = jnp.concatenate([chip, jnp.pad(line_chip[None], ((0, 3), (0, 0), (0, 0), (0, 0)))], axis=2)
    chip = (
        chip.reshape(4, shards // 2, parts, -1, model)
        .transpose(0, 2, 1, 3, 4)
        .reshape(n, shards // 2, -1, model)
    )
    unit = add_up(pick(chip, me), *[swap(pick(chip, me ^ s), s, n) for s in range(1, n)])
    unit, first_shard, second_shard = lax.optimization_barrier((unit, first_shard, second_shard))
    first_sum, second_sum = sum_over_ctx(first_shard, n), sum_over_ctx(second_shard, n)
    mine = add_up(
        pick(unit, z),
        *[swap_shard(pick(unit, z ^ s), 2 * s, shards) for s in range(1, shards // 2)],
    )
    unit_all = swapped(mine, n)
    part_units = in_order(unit_all, me).reshape(4, -1, model).astype(F32)
    line_sums = part_units[0, own_rows:]
    part_units = part_units[:, :own_rows]
    part_qkv = jnp.concatenate([part_units[t] for t in range(3)], axis=1)
    part_up, part_down = lay(first_sum, second_sum, shards, up_weight.shape, down_weight.shape)
    sizes = [own_rows] * 5 + [3 * own_rows, per_shard, per_shard]
    gain1, bias1, gain2, bias2, columns, qkv_b, *up_b = [
        line_sums[index, :size] for index, size in enumerate(sizes)
    ]
    return (
        placed(layer_out), placed(tokens_grad), gain1, bias1, gain2, bias2, part_qkv, qkv_b,
        part_units[3], columns, part_up, jnp.concatenate(up_b), part_down, columns,
    )


def solution(mesh):
    blocks = P("ctx", "fsdp", None)
    line, matrix = P("fsdp"), P("fsdp", None)
    return jax.shard_map(
        body,
        mesh=mesh,
        in_specs=(
            blocks, line, line, line, line, matrix, line, matrix, line, matrix, line, matrix, line,
            blocks,
        ),
        out_specs=(
            blocks, blocks, line, line, line, line, matrix, line, matrix, line, matrix, line,
            matrix, line,
        ),
        check_vma=False,
    )
```

```python
import functools

import jax
import jax.numpy as jnp
import numpy as np
from jax import lax
from jax.experimental import pallas as pl
from jax.experimental.pallas import tpu as pltpu
from jax.sharding import PartitionSpec as P

H = 12
HD = 64
ROT = 16
LANES = 128
EPS = 1e-05
MASKED = -1e30
VMEM = 56 * 1024 * 1024
BF = jnp.bfloat16
F32 = jnp.float32


def dot(left, right, dims=((1,), (0,))):
    return lax.dot_general(left, right, (dims, ((), ())), preferred_element_type=F32)


def back_dot(left, right):
    return dot(left, right, ((1,), (1,)))


def outer_sum(left, right):
    return dot(left, right, ((0,), (0,)))


def normalized(values):
    center = values - jnp.mean(values, axis=-1, keepdims=True)
    spread = jnp.mean(center * center, axis=-1, keepdims=True)
    inverse = lax.rsqrt(spread + EPS)
    return center * inverse, inverse


def norm_back(hat, inverse, gain, grad):
    scaled = grad * gain
    first = jnp.mean(scaled, axis=-1, keepdims=True)
    second = jnp.mean(scaled * hat, axis=-1, keepdims=True)
    return (
        inverse * (scaled - first - hat * second),
        jnp.sum(grad * hat, axis=0, keepdims=True),
        jnp.sum(grad, axis=0, keepdims=True),
    )


def rotary_tables(length):
    half = ROT // 2
    inverse = np.float32(10000.0) ** (-np.arange(0, ROT, 2, dtype=np.float32) / np.float32(ROT))
    phase = np.arange(length, dtype=np.float32)[:, None] * inverse[None, :].astype(np.float32)
    cosine, sine = np.cos(phase), np.sin(phase)
    c = np.ones((length, HD), np.float32)
    s1 = np.zeros((length, HD), np.float32)
    s2 = np.zeros((length, HD), np.float32)
    c[:, :half] = cosine
    c[:, half:ROT] = cosine
    s1[:, :half] = -sine
    s2[:, half:ROT] = sine
    return tuple(np.concatenate([t, t], axis=1) for t in (c, s1, s2))


def turn(values, c, s1, s2):
    half = ROT // 2
    return (
        values * c
        + pltpu.roll(values, LANES - half, 1) * s1
        + pltpu.roll(values, half, 1) * s2
    )


def project_kernel(
    n, block_len, used, me, tokens, cot, vectors, c_ref, s1_ref, s2_ref, *rest
):
    own, other = rest[:2]
    columns, crossed = rest[2 : 2 + n], rest[2 + n : 2 + 2 * n]
    outs = rest[2 + 2 * n : 2 + 3 * n]
    w, normed, b, laid = rest[2 + 3 * n :]
    kind = pl.program_id(0)
    model = tokens.shape[1]
    parts = n // 4
    f = me[1]

    for part in range(parts):
        unit = kind * parts + part
        laid[f, part] = own[unit]
        laid[f ^ 1, part] = other[unit]
        for shift in range(n):

            @pl.when((unit ^ me[0]) == shift)
            def _(shift=shift, part=part):
                for index in range(columns[shift].shape[0]):
                    step = 2 * (index + 1)
                    laid[f ^ step, part] = columns[shift][index]
                    laid[f ^ step ^ 1, part] = crossed[shift][index]

    w[0] = laid[...].reshape(model, model)

    @pl.when(kind == 0)
    def _():
        hat, _inverse = normalized(tokens[...].astype(F32))
        normed[...] = (hat * vectors[0:1, :model] + vectors[1:2, :model]).astype(BF)

    for t in range(3):

        @pl.when(kind == t)
        def _(t=t):
            b[...] = vectors[4:5, t * model : (t + 1) * model]

    width = outs[0].shape[-1]
    per = w.shape[-1] // width

    def operands(shift, left):
        group = jnp.minimum(me[0] ^ shift, used - 1)
        rows = pl.multiple_of((group // per) * block_len, block_len)
        cols = pl.multiple_of((group % per) * width, LANES)
        return left[pl.ds(rows, block_len)], pl.ds(cols, width)

    @pl.when(kind < 2)
    def _():
        c, s1, s2 = c_ref[...], s1_ref[...], s2_ref[...]
        for shift in range(n):
            left, cols = operands(shift, normed)
            full = dot(left, w[0, :, cols]) + b[:, cols]
            for j in range(width // LANES):
                at = slice(j * LANES, (j + 1) * LANES)
                outs[shift][0, :, at] = turn(full[:, at], c, s1, s2).astype(BF)

    @pl.when(kind == 2)
    def _():
        for shift in range(n):
            left, cols = operands(shift, normed)
            outs[shift][0] = (dot(left, w[0, :, cols]) + b[:, cols]).astype(BF)

    @pl.when(kind == 3)
    def _():
        for shift in range(n):
            left, cols = operands(shift, cot)
            outs[shift][0] = back_dot(left, w[0, cols]).astype(BF)


def project(n, m, at, tokens, cot, vectors, pieces, tables, block_len, width, used):
    rows, model = tokens.shape
    parts = n // 4
    whole = pl.BlockSpec((rows, model), lambda kind, me_ref: (0, 0))
    own = pl.BlockSpec((block_len, LANES), lambda kind, me_ref: (me_ref[0], 0))
    return pl.pallas_call(
        functools.partial(project_kernel, n, block_len, used),
        grid_spec=pltpu.PrefetchScalarGridSpec(
            num_scalar_prefetch=1,
            grid=(4,),
            in_specs=[
                whole,
                whole,
                pl.BlockSpec(vectors.shape, lambda kind, me_ref: (0, 0)),
                own,
                own,
                own,
            ]
            + [pl.BlockSpec(p.shape, lambda kind, me_ref: (0, 0, 0)) for p in pieces],
            out_specs=[pl.BlockSpec((1, block_len, width), lambda kind, me_ref: (kind, 0, 0))] * n
            + [pl.BlockSpec((1, model, model), lambda kind, me_ref: (kind, 0, 0))],
            scratch_shapes=[
                pltpu.VMEM((rows, model), BF),
                pltpu.VMEM((1, model), F32),
                pltpu.VMEM((m, parts, model // m // parts, model), BF),
            ],
        ),
        out_shape=[jax.ShapeDtypeStruct((4, block_len, width), BF)] * n
        + [jax.ShapeDtypeStruct((4, model, model), BF)],
        compiler_params=pltpu.CompilerParams(vmem_limit_bytes=VMEM),
        cost_estimate=pl.CostEstimate(
            flops=8 * rows * model * model,
            bytes_accessed=2 * (4 * model * model + 6 * rows * model),
            transcendentals=0,
        ),
        name="project",
    )(at, tokens, cot, vectors, *(jnp.asarray(t) for t in tables), *pieces)


def attend_kernel(n, block, me, *refs):
    ins = refs[:n]
    c_ref, s1_ref, s2_ref = refs[n : n + 3]
    outs = refs[n + 3 : 2 * n + 3]
    (q_s, k_s, v_s, g_s, qt_s, kt_s, vt_s, gt_s, sc, pb, dk, dv, o_s, dq_s) = refs[2 * n + 3 :]
    two = 2 * block
    scale = HD**-0.5

    for shift in range(n):
        at = ins[shift]
        place = me[0] ^ shift
        for kind, plain, flipped in ((0, q_s, qt_s), (1, k_s, kt_s), (2, v_s, vt_s), (3, g_s, gt_s)):
            piece = at[kind].astype(F32)
            if kind == 0:
                piece = piece * scale
            plain[place] = piece.astype(BF)
            flipped[place] = piece.T.astype(BF)

    lane = lax.broadcasted_iota(jnp.int32, (block, LANES), 1) < HD
    row = lax.broadcasted_iota(jnp.int32, (LANES, block), 0) < HD
    key_at = lax.broadcasted_iota(jnp.int32, (block, two), 0)
    query_at = lax.broadcasted_iota(jnp.int32, (block, two), 1)
    query_at = jnp.where(query_at >= block, query_at - block, query_at)
    allowed = key_at <= query_at

    def beside(flipped):
        zero = jnp.zeros_like(flipped)
        return jnp.concatenate([jnp.where(row, flipped, zero), jnp.where(row, zero, flipped)], axis=1)

    def below(plain):
        zero = jnp.zeros_like(plain)
        return jnp.concatenate([jnp.where(lane, plain, zero), jnp.where(lane, zero, plain)], axis=0)

    def loop(upto, body, init):
        if isinstance(upto, int):
            for j in range(upto):
                init = body(j, init)
            return init
        return lax.fori_loop(0, upto, body, init)

    def query_block(i, _):
        queries_t = beside(qt_s[i].astype(F32)).astype(BF)
        grads_t = beside(gt_s[i].astype(F32)).astype(BF)
        queries = below(q_s[i].astype(F32)).astype(BF)
        grads = below(g_s[i].astype(F32)).astype(BF)

        def score(j, top):
            found = dot(k_s[j], queries_t)
            sc[j] = found
            return jnp.maximum(top, jnp.max(found, axis=0, keepdims=True))

        diagonal = jnp.where(allowed, dot(k_s[i], queries_t), MASKED)
        sc[i] = diagonal
        top = loop(i, score, jnp.max(diagonal, axis=0, keepdims=True))

        def weigh(j, total):
            exps = jnp.exp(sc[j] - top)
            sc[j] = exps
            return total + jnp.sum(exps, axis=0, keepdims=True)

        total = loop(i + 1, weigh, jnp.zeros((1, two), F32))
        inverse = 1.0 / total

        def mix(j, heads):
            probs = sc[j] * inverse
            sc[j] = probs
            low = probs.astype(BF)
            pb[j] = low
            return tuple(
                heads[h] + dot(vt_s[j, h * HD : (h + 1) * HD], low[:, h * block : (h + 1) * block])
                for h in range(2)
            )

        none = jnp.zeros((HD, block), F32)
        heads = loop(i + 1, mix, (none, none))
        delta = jnp.concatenate(
            [
                jnp.sum(heads[h] * gt_s[i, h * HD : (h + 1) * HD].astype(F32), axis=0, keepdims=True)
                for h in range(2)
            ],
            axis=1,
        )
        o_s[i] = jnp.concatenate(heads, axis=0).T.astype(BF)

        def back(j, found, first):
            grad_scores = (sc[j] * (dot(v_s[j], grads_t) - delta)).astype(BF)
            key_part = dot(grad_scores, queries)
            value_part = dot(pb[j], grads)
            if first:
                dk[j] = key_part
                dv[j] = value_part
            else:
                dk[j] = dk[j] + key_part
                dv[j] = dv[j] + value_part
            return tuple(
                found[h]
                + dot(kt_s[j, h * HD : (h + 1) * HD], grad_scores[:, h * block : (h + 1) * block])
                for h in range(2)
            )

        found = back(i, (none, none), True)
        found = loop(i, lambda j, kept: back(j, kept, False), found)
        grad_query = jnp.concatenate(found, axis=0).T * scale
        dq_s[i] = turn(grad_query, c_ref[i], -s1_ref[i], -s2_ref[i]).astype(BF)
        return 0

    if n <= 4:
        for i in range(n):
            query_block(i, 0)
    else:
        lax.fori_loop(0, n, query_block, 0)

    for shift in range(n):
        place = me[0] ^ shift
        c, s1, s2 = c_ref[place], -s1_ref[place], -s2_ref[place]
        outs[shift][0] = o_s[place]
        outs[shift][1] = dq_s[place]
        outs[shift][2] = turn(dk[place], c, s1, s2).astype(BF)
        outs[shift][3] = dv[place].astype(BF)


def attend(n, me, pieces, tables):
    _, block, width = pieces[0].shape
    length = n * block
    spec = pl.BlockSpec((4, block, LANES), lambda j, me_ref: (0, 0, j))
    table_spec = pl.BlockSpec((n, block, LANES), lambda j, me_ref: (0, 0, 0))
    plain = pltpu.VMEM((n, block, LANES), BF)
    flipped = pltpu.VMEM((n, LANES, block), BF)
    total = pltpu.VMEM((n, block, LANES), F32)
    work = width // HD * length * (length + block) // 2
    return pl.pallas_call(
        functools.partial(attend_kernel, n, block),
        grid_spec=pltpu.PrefetchScalarGridSpec(
            num_scalar_prefetch=1,
            grid=(width // LANES,),
            in_specs=[spec] * n + [table_spec] * 3,
            out_specs=[spec] * n,
            scratch_shapes=[
                plain, plain, plain, plain,
                flipped, flipped, flipped, flipped,
                pltpu.VMEM((n, block, 2 * block), F32),
                pltpu.VMEM((n, block, 2 * block), BF),
                total, total, plain, plain,
            ],
        ),
        out_shape=[jax.ShapeDtypeStruct((4, block, width), BF)] * n,
        compiler_params=pltpu.CompilerParams(vmem_limit_bytes=VMEM),
        cost_estimate=pl.CostEstimate(
            flops=12 * work * 4 * HD * 10, bytes_accessed=2 * 8 * length * width, transcendentals=work
        ),
        name="attend",
    )(me, *pieces, *(jnp.asarray(t).reshape(n, block, LANES) for t in tables))


def mlp_kernel(last, *refs):
    tokens, cot, vectors, w_up, b_up, w_down = refs[:6]
    model = tokens.shape[1]
    if last:
        start_out, start_grad, out, grad_in, grad_up, grad_down, grad_b, sums, normed = refs[6:]
    else:
        out, grad_in, grad_up, grad_down, grad_b, normed = refs[6:]
    step = pl.program_id(0)
    row = 7 if last else 6
    gain, bias = vectors[2:3, :model], vectors[3:4, :model]

    @pl.when(step == 0)
    def _():
        values = tokens[...].astype(F32)
        hat, _inverse = normalized(values)
        normed[...] = (hat * gain + bias).astype(BF)
        if last:
            out[...] = start_out[...]
            grad_in[...] = start_grad[...]
        else:
            out[...] = values + (vectors[5:6, :model] + vectors[8:9, :model])
            grad_in[...] = jnp.zeros_like(grad_in)

    up = w_up[...].reshape(model, -1)
    down = w_down[...].reshape(-1, model)
    hidden = dot(normed[...], up) + b_up[row : row + 1]
    share = 0.5 + 0.5 * lax.erf(hidden * (0.5**0.5))
    slope = share + hidden * (jnp.exp(-0.5 * hidden * hidden) * ((2.0 * np.pi) ** -0.5))
    active = (hidden * share).astype(BF)
    grad_hidden = (back_dot(cot[...], down) * slope).astype(BF)
    grad_b[...] = jnp.sum(grad_hidden.astype(F32), axis=0, keepdims=True)
    out[...] = out[...] + dot(active, down)
    grad_in[...] = grad_in[...] + back_dot(grad_hidden, up)
    grad_down[...] = outer_sum(active, cot[...]).astype(BF).reshape(grad_down.shape)
    grad_up[...] = outer_sum(normed[...], grad_hidden).astype(BF).reshape(grad_up.shape)

    if last:

        @pl.when(step == pl.num_programs(0) - 1)
        def _():
            hat, inverse = normalized(tokens[...].astype(F32))
            upstream = cot[...].astype(F32)
            back, grad_gain, grad_bias = norm_back(hat, inverse, gain, grad_in[...])
            grad_in[...] = upstream + back
            sums[0:1] = grad_gain
            sums[1:2] = grad_bias
            sums[2:3] = jnp.sum(upstream, axis=0, keepdims=True)
            sums[3:8] = jnp.zeros((5, sums.shape[1]), F32)


def mlp(tokens, cot, vectors, weights, start=None):
    rows, model = tokens.shape
    shards, units, shard_rows, _ = weights.shape
    half = units // 2 * model
    chunk = model // 2
    group = chunk * shards // half
    last = start is not None
    whole = pl.BlockSpec((rows, model), lambda j: (0, 0))
    line = pl.BlockSpec((1, chunk), lambda j: (0, j))
    tall = (shards, 1, shard_rows, chunk)
    flat = (group, units // 2, shard_rows, model)
    total = jax.ShapeDtypeStruct((rows, model), F32)
    grads = jax.ShapeDtypeStruct((shards, units // 2, shard_rows, model), BF)
    return pl.pallas_call(
        functools.partial(mlp_kernel, last),
        grid=(half // chunk,),
        in_specs=[
            whole,
            whole,
            pl.BlockSpec(vectors.shape, lambda j: (0, 0)),
            pl.BlockSpec(tall, lambda j: (0, j // 2, 0, j % 2)),
            pl.BlockSpec((16, chunk), lambda j: (0, j)),
            pl.BlockSpec(flat, lambda j: (j, 1, 0, 0)),
        ]
        + [whole] * (2 * last),
        out_specs=[
            whole,
            whole,
            pl.BlockSpec(tall, lambda j: (0, j // 2, 0, j % 2)),
            pl.BlockSpec(flat, lambda j: (j, 0, 0, 0)),
            line,
        ]
        + ([pl.BlockSpec((8, model), lambda j: (0, 0))] if last else []),
        out_shape=[total, total, grads, grads, jax.ShapeDtypeStruct((1, half), F32)]
        + ([jax.ShapeDtypeStruct((8, model), F32)] if last else []),
        scratch_shapes=[pltpu.VMEM((rows, model), BF)],
        compiler_params=pltpu.CompilerParams(vmem_limit_bytes=VMEM),
        cost_estimate=pl.CostEstimate(
            flops=12 * rows * model * half,
            bytes_accessed=8 * model * half + 12 * rows * model,
            transcendentals=2 * rows * half,
        ),
        name="mlp",
    )(tokens, cot, vectors, weights, vectors, weights, *(start or ()))


def finish_kernel(n, block_len, used, shards, at, *refs):
    answers = refs[:n]
    tokens, cot, vectors, base, grad_base, w, sums_two, grad_b = refs[n : n + 8]
    out, grad_out, own, other, line_own, line_other = refs[n + 8 : n + 14]
    held, normed, grads, grad_in, sums, lines = refs[n + 14 :]
    kind = pl.program_id(0)
    model = tokens.shape[1]
    width = answers[0].shape[-1]
    per = model // width

    for shift in range(n):
        group = jnp.minimum(at[0] ^ shift, used - 1)
        rows = pl.multiple_of((group // per) * block_len, block_len)
        cols = pl.multiple_of((group % per) * width, LANES)
        if used == n:
            held[pl.ds(rows, block_len), pl.ds(cols, width)] = answers[shift][0]
        else:

            @pl.when((at[0] ^ shift) < used)
            def _(rows=rows, cols=cols, shift=shift):
                held[pl.ds(rows, block_len), pl.ds(cols, width)] = answers[shift][0]

    @pl.when(kind == 0)
    def _():
        hat, _inverse = normalized(tokens[...].astype(F32))
        normed[...] = (hat * vectors[0:1, :model] + vectors[1:2, :model]).T.astype(BF)
        grad_in[...] = jnp.zeros_like(grad_in)
        out[...] = (base[...] + dot(held[...], w[0])).astype(BF)
        grads[...] = outer_sum(held[...], cot[...]).astype(BF).reshape(grads.shape)

    @pl.when(kind > 0)
    def _():
        grads[...] = dot(normed[...], held[...]).astype(BF).reshape(grads.shape)
        grad_in[...] = grad_in[...] + back_dot(held[...], w[0])
        sums[pl.ds(kind, 1)] = jnp.sum(held[...].astype(F32), axis=0, keepdims=True)

    for z in range(shards // 2):
        own[0, z] = grads[z, at[1]]
        other[0, z] = grads[z, at[1] ^ 1]

    @pl.when(kind == 3)
    def _():
        hat, inverse = normalized(tokens[...].astype(F32))
        back, grad_gain, grad_bias = norm_back(hat, inverse, vectors[0:1, :model], grad_in[...])
        grad_out[...] = (grad_base[...] + back).astype(BF)
        qkv = jnp.concatenate([sums[t : t + 1] for t in (1, 2, 3)], axis=1)
        whole = [
            grad_gain, grad_bias, sums_two[0:1], sums_two[1:2], sums_two[2:3], qkv, grad_b[0:1],
            grad_b[1:2],
        ]
        lines[...] = jnp.zeros_like(lines)
        for index, line in enumerate(whole):
            size = line.shape[1] // shards
            for f in range(shards):
                lines[f // 2, f % 2, index : index + 1, :size] = line[:, f * size : (f + 1) * size]
        for z in range(shards // 2):
            line_own[z] = lines[z, at[1]]
            line_other[z] = lines[z, at[1] ^ 1]


def finish(n, me, core, answers, tokens, cot, vectors, base, grad_base, w, sums_two, grad_b, shards, used):
    rows, model = tokens.shape
    block_len, width = answers[0].shape[1:]
    whole = pl.BlockSpec((rows, model), lambda kind, at: (0, 0))
    own_rows = model // shards

    def unit(kind, at):
        return lax.rem(kind + 3, 4)

    half = pl.BlockSpec(
        (1, shards // 2, own_rows, model), lambda kind, at: (unit(kind, at), 0, 0, 0)
    )
    half_shape = jax.ShapeDtypeStruct((4, shards // 2, own_rows, model), BF)
    half_lines = pl.BlockSpec((shards // 2, 8, model), lambda kind, at: (0, 0, 0))
    half_lines_shape = jax.ShapeDtypeStruct((shards // 2, 8, model), F32)
    return pl.pallas_call(
        functools.partial(finish_kernel, n, block_len, used, shards),
        grid_spec=pltpu.PrefetchScalarGridSpec(
            num_scalar_prefetch=1,
            grid=(4,),
            in_specs=[pl.BlockSpec((1, block_len, width), lambda kind, at: (kind, 0, 0))] * n
            + [
                whole,
                whole,
                pl.BlockSpec(vectors.shape, lambda kind, at: (0, 0)),
                whole,
                whole,
                pl.BlockSpec((1, model, model), lambda kind, at: (unit(kind, at), 0, 0)),
                pl.BlockSpec((8, model), lambda kind, at: (0, 0)),
                pl.BlockSpec(grad_b.shape, lambda kind, at: (0, 0)),
            ],
            out_specs=[whole, whole, half, half, half_lines, half_lines],
            scratch_shapes=[
                pltpu.VMEM((rows, model), BF),
                pltpu.VMEM((model, rows), BF),
                pltpu.VMEM((shards // 2, 2, own_rows, model), BF),
                pltpu.VMEM((rows, model), F32),
                pltpu.VMEM((8, model), F32),
                pltpu.VMEM((shards // 2, 2, 8, model), F32),
            ],
        ),
        out_shape=[
            jax.ShapeDtypeStruct((rows, model), BF),
            jax.ShapeDtypeStruct((rows, model), BF),
            half_shape,
            half_shape,
            half_lines_shape,
            half_lines_shape,
        ],
        compiler_params=pltpu.CompilerParams(vmem_limit_bytes=VMEM),
        cost_estimate=pl.CostEstimate(
            flops=16 * rows * model * model, bytes_accessed=40 * rows * model, transcendentals=0
        ),
        name="finish",
    )(
        jnp.stack([me, core]).astype(jnp.int32),
        *answers, tokens, cot, vectors, base, grad_base, w, sums_two, grad_b,
    )


def swap(value, shift, n):
    return lax.ppermute(value, "ctx", [(i, i ^ shift) for i in range(n)])


def swap_shard(value, shift, m):
    return lax.ppermute(value, "fsdp", [(i, i ^ shift) for i in range(m)])


def pack_kernel(q, qkv, out_w, *refs):
    out = refs[-1]
    rows = out_w.shape[0]
    out[:rows] = jnp.where(q[0] < 3, qkv[...].astype(F32), out_w[...].astype(F32)).astype(BF)
    lines = []
    for ref in refs[:-1]:
        line = ref[...].astype(F32)
        lines.append(jnp.concatenate([line, jnp.zeros((1, out.shape[1] - line.shape[1]), F32)], axis=1))
    lines.append(jnp.zeros((out.shape[0] - rows - len(lines), out.shape[1]), F32))
    out[rows:] = jnp.concatenate(lines, axis=0).astype(BF)


def pack(q, qkv, out_w, vectors):
    rows, model = out_w.shape
    lines = [v.reshape(1, -1) for v in vectors]
    return pl.pallas_call(
        pack_kernel,
        grid_spec=pltpu.PrefetchScalarGridSpec(
            num_scalar_prefetch=1,
            grid=(1,),
            in_specs=[
                pl.BlockSpec((rows, model), lambda i, at: (0, jnp.minimum(at[0], 2))),
                pl.BlockSpec((rows, model), lambda i, at: (0, 0)),
            ]
            + [pl.BlockSpec(v.shape, lambda i, at: (0, 0)) for v in lines],
            out_specs=pl.BlockSpec((rows + 16, model), lambda i, at: (0, 0)),
        ),
        out_shape=jax.ShapeDtypeStruct((rows + 16, model), BF),
        name="pack",
    )(q.astype(jnp.int32).reshape(1), qkv, out_w, *lines)


def unpack_kernel(sizes, half, at, own, other, out):
    chips = own.shape[0]
    out[...] = jnp.zeros_like(out)
    rows = []
    for f in range(2 * chips):
        rel = f ^ at[0]
        both = jnp.where(rel % 2 == 0, own[rel // 2].astype(F32), other[rel // 2].astype(F32))
        rows.append(both)
    for index, size in enumerate(sizes):
        if index == half + 1:
            continue
        if index == half:
            cut = size // 2
            for h in range(2):
                line = [r[index : index + 1, h * cut : (h + 1) * cut] for r in rows]
                out[index + h : index + h + 1, : len(rows) * cut] = jnp.concatenate(line, axis=1)
        else:
            line = [r[index : index + 1, :size] for r in rows]
            out[index : index + 1, : len(rows) * size] = jnp.concatenate(line, axis=1)


def unpack(f, own, other, sizes, half):
    width = 2 * own.shape[0] * max(sizes[:half] + [sizes[half] // 2])
    full = pl.BlockSpec(own.shape, lambda i, at: (0, 0, 0))
    return pl.pallas_call(
        functools.partial(unpack_kernel, sizes, half),
        grid_spec=pltpu.PrefetchScalarGridSpec(
            num_scalar_prefetch=1,
            grid=(1,),
            in_specs=[full, full],
            out_specs=pl.BlockSpec((16, width), lambda i, at: (0, 0)),
        ),
        out_shape=jax.ShapeDtypeStruct((16, width), F32),
        name="unpack",
    )(f.astype(jnp.int32).reshape(1), own, other)


def along_z(mine, m):
    return [swap_shard(mine, step, m) for step in range(2, m, 2)]


def between_columns(along, n):
    return [along] + [swap(along, shift, n) for shift in range(1, n)]


def assemble_kernel(where, at, *refs):
    out = refs[-1]
    for piece, index, place in where:
        unit, shard = place(at)
        out[shard, unit] = refs[piece][index]


def assemble(at, pieces, n, m):
    where = []
    for unit in range(n):
        where.append((0, unit, lambda at, unit=unit: (unit, at[1])))
        where.append((1, unit, lambda at, unit=unit: (unit, at[1] ^ 1)))
    for core in range(2):
        for shift in range(n):
            for index in range(m // 2 - 1):
                where.append(
                    (
                        2 + core * n + shift,
                        index,
                        lambda at, shift=shift, flip=2 * (index + 1) ^ core: (at[0] ^ shift, at[1] ^ flip),
                    )
                )
    full = (m, n) + pieces[0].shape[1:]
    return pl.pallas_call(
        functools.partial(assemble_kernel, where),
        grid_spec=pltpu.PrefetchScalarGridSpec(
            num_scalar_prefetch=1,
            grid=(1,),
            in_specs=[pl.BlockSpec(p.shape, lambda i, at: (0, 0, 0)) for p in pieces],
            out_specs=pl.BlockSpec(full, lambda i, at: (0, 0, 0, 0)),
        ),
        out_shape=jax.ShapeDtypeStruct(full, pieces[0].dtype),
        compiler_params=pltpu.CompilerParams(vmem_limit_bytes=VMEM),
        name="assemble",
    )(at, *pieces)


def add_up(*pieces):
    return sum(p.astype(F32) for p in pieces).astype(BF)


def pick(value, at, axis=0):
    return lax.dynamic_index_in_dim(value, at, axis, keepdims=False)


def swapped(value, n):
    return [value] + [swap(value, s, n) for s in range(1, n)]


def ctx_step(halves, i, n):
    steps = [2**i for i in range(n.bit_length() - 1)]
    return [(value, swap(value, steps[(i + j) % len(steps)], n)) for j, value in enumerate(halves)]


def ctx_sum(halves, begin, n):
    terms = halves
    for i in range(begin, n.bit_length() - 1):
        terms = ctx_step([add_up(*t) for t in terms] if i else terms, i, n)
    return [term for half in terms for term in half]


def lay_kernel(shards, *refs):
    up, down = refs[8:]
    model = up.shape[1] // 4
    size = up.shape[1] // shards // 2
    ups = []
    for h in range(2):
        terms = refs[4 * h : 4 * h + 4]
        total = terms[0][...].astype(F32) + terms[1][...].astype(F32)
        ups.append(jnp.concatenate([total[0], total[1]], axis=1))
        rows = down.shape[0] // 4
        for unit in range(2):
            at = (2 * h + unit) * rows
            down[at : at + rows] = terms[2][unit].astype(F32) + terms[3][unit].astype(F32)
    for f in range(shards):
        line = [ups[h][:, f * size : (f + 1) * size] for h in range(2)]
        up[:, 2 * f * size : 2 * (f + 1) * size] = jnp.concatenate(line, axis=1)


def lay(first, second, shards, up_shape, down_shape):
    return pl.pallas_call(
        functools.partial(lay_kernel, shards),
        out_shape=[jax.ShapeDtypeStruct(up_shape, F32), jax.ShapeDtypeStruct(down_shape, F32)],
        compiler_params=pltpu.CompilerParams(vmem_limit_bytes=VMEM),
        name="lay",
    )(*first, *second)


def in_order(pieces, at):
    stacked = jnp.stack(pieces)
    return jnp.stack([pick(stacked, at ^ place) for place in range(len(pieces))])


def body(
    tokens,
    norm1_gain,
    norm1_bias,
    norm2_gain,
    norm2_bias,
    qkv_weight,
    qkv_bias,
    out_weight,
    out_bias,
    up_weight,
    up_bias,
    down_weight,
    down_bias,
    cotangent,
):
    block_len, seq_count, model = tokens.shape
    n = lax.axis_size("ctx")
    shards = lax.axis_size("fsdp")
    rows = block_len * seq_count
    hidden = up_weight.shape[1]
    me = lax.axis_index("ctx")
    me_arr = me.astype(jnp.int32).reshape(1)
    width = -(-seq_count * model // (n * LANES)) * LANES
    used = seq_count * model // width
    per = model // width

    parts = n // 4
    own_rows = out_weight.shape[0]

    vectors = (
        norm1_gain, norm1_bias, norm2_gain, norm2_bias, qkv_bias, out_bias, up_bias, out_bias,
        down_bias,
    )
    sizes = [v.shape[0] for v in vectors]
    per_shard = hidden // shards // 2

    def half_weights(h):
        up = up_weight.reshape(own_rows, shards, 2, per_shard)[:, :, h].reshape(own_rows, -1, model)
        down = down_weight[h * per_shard : (h + 1) * per_shard].reshape(-1, own_rows, model)
        return jnp.concatenate([up.transpose(1, 0, 2), down], axis=0)

    units = jnp.concatenate(
        [qkv_weight[None, :, t * model : (t + 1) * model] for t in range(3)] + [out_weight[None]]
    ).reshape(n, own_rows // parts, model)
    if n == 4:
        mine = pack(me, qkv_weight, out_weight, vectors)
    else:
        lines = [jnp.pad(v, (0, model - v.shape[0])) for v in vectors]
        lines = jnp.pad(jnp.stack(lines), ((0, 16 - len(vectors)), (0, 0)))
        mine = jnp.concatenate([pick(units, me), lines], axis=0)
    mine_rows = units.shape[1]
    came = along_z(mine, shards)
    along_units = jnp.stack([c[:mine_rows] for c in came])
    chips = jnp.stack([c[mine_rows:] for c in [mine] + came])
    first_half, _ = lax.optimization_barrier((half_weights(0), along_units))
    w_first = lax.all_gather(first_half, "fsdp", axis=0, tiled=False)
    unit_columns = between_columns(along_units, n)
    vectors = unpack(
        lax.axis_index("fsdp"), chips, swap_shard(chips, 1, shards), sizes, 6
    )
    inputs = tokens.transpose(1, 0, 2).reshape(rows, model)
    cot = cotangent.transpose(1, 0, 2).reshape(rows, model)
    vectors, inputs, cot, unit_columns = lax.optimization_barrier((vectors, inputs, cot, unit_columns))
    crossed = [swap_shard(held, 1, shards) for held in unit_columns]
    unit_pieces = [units, swap_shard(units, 1, shards)] + unit_columns + crossed

    tables = rotary_tables(n * block_len)
    def shard_sum(value):
        return lax.psum_scatter(value, "fsdp", scatter_dimension=0, tiled=False)

    at = jnp.stack([me, lax.axis_index("fsdp")]).astype(jnp.int32)
    *sent, w_units = project(
        n, shards, at, inputs, cot, vectors, unit_pieces, tables, block_len, width, used
    )
    pieces = [sent[0]] + [swap(sent[shift], shift, n) for shift in range(1, n)]
    mlp_inputs, second_half, _ = lax.optimization_barrier(
        (inputs, half_weights(1), (sent, w_first))
    )
    second_units = second_half.reshape(n, -1, model)
    along_second = along_z(pick(second_units, me), shards)
    base, grad_base, grad_up, grad_down, grad_b_first = mlp(
        mlp_inputs, cot, vectors, w_first
    )
    first_grads, pieces = lax.optimization_barrier(
        (jnp.concatenate([grad_up, grad_down], axis=1), pieces)
    )
    first_shard = shard_sum(first_grads)
    along_second, _ = lax.optimization_barrier((along_second, pieces))
    second_columns = between_columns(jnp.stack(along_second), n)
    made = attend(n, me_arr, pieces, tables)
    mlp_inputs, second_columns, second_units, _ = lax.optimization_barrier(
        (inputs, second_columns, second_units, made)
    )
    second_pieces = [second_units, swap_shard(second_units, 1, shards)] + second_columns
    second_pieces += [swap_shard(held, 1, shards) for held in second_columns]
    w_second = assemble(at, second_pieces, n, shards).reshape(shards, 4, own_rows, model)
    answers = [made[0]] + [swap(made[shift], shift, n) for shift in range(1, n)]
    base, grad_base, grad_up, grad_down, grad_b_second, sums_two = mlp(
        mlp_inputs, cot, vectors, w_second, start=(base, grad_base)
    )
    second_grads, answers = lax.optimization_barrier(
        (jnp.concatenate([grad_up, grad_down], axis=1), answers)
    )
    second_shard = shard_sum(second_grads)
    core = lax.axis_index("fsdp") % 2
    layer_out, tokens_grad, own, other, line_own, line_other = finish(
        n, me, core, answers, inputs, cot, vectors, base, grad_base, w_units, sums_two,
        jnp.concatenate([grad_b_first, grad_b_second]), shards, used,
    )

    def placed(value):
        return value.reshape(seq_count, block_len, model).transpose(1, 0, 2)

    z = lax.axis_index("fsdp") // 2
    chip = add_up(own, swap_shard(other, 1, shards))
    line_chip = add_up(line_own, swap_shard(line_other, 1, shards))
    chip = jnp.concatenate([chip, jnp.pad(line_chip[None], ((0, 3), (0, 0), (0, 0), (0, 0)))], axis=2)
    chip = (
        chip.reshape(4, shards // 2, parts, -1, model)
        .transpose(0, 2, 1, 3, 4)
        .reshape(n, shards // 2, -1, model)
    )
    unit = add_up(pick(chip, me), *[swap(pick(chip, me ^ s), s, n) for s in range(1, n)])
    unit, first_shard, second_shard = lax.optimization_barrier((unit, first_shard, second_shard))
    first_sum = ctx_sum([first_shard[:2], first_shard[2:]], 0, n)
    second_sum = ctx_sum([second_shard[:2], second_shard[2:]], 0, n)
    mine = add_up(
        pick(unit, z),
        *[swap_shard(pick(unit, z ^ s), 2 * s, shards) for s in range(1, shards // 2)],
    )
    unit_all = swapped(mine, n)
    part_units = in_order(unit_all, me).reshape(4, -1, model).astype(F32)
    line_sums = part_units[0, own_rows:]
    part_units = part_units[:, :own_rows]
    part_qkv = jnp.concatenate([part_units[t] for t in range(3)], axis=1)
    part_up, part_down = lay(first_sum, second_sum, shards, up_weight.shape, down_weight.shape)
    sizes = [own_rows] * 5 + [3 * own_rows, per_shard, per_shard]
    gain1, bias1, gain2, bias2, columns, qkv_b, *up_b = [
        line_sums[index, :size] for index, size in enumerate(sizes)
    ]
    return (
        placed(layer_out), placed(tokens_grad), gain1, bias1, gain2, bias2, part_qkv, qkv_b,
        part_units[3], columns, part_up, jnp.concatenate(up_b), part_down, columns,
    )


def solution(mesh):
    blocks = P("ctx", "fsdp", None)
    line, matrix = P("fsdp"), P("fsdp", None)
    return jax.shard_map(
        body,
        mesh=mesh,
        in_specs=(
            blocks, line, line, line, line, matrix, line, matrix, line, matrix, line, matrix, line,
            blocks,
        ),
        out_specs=(
            blocks, blocks, line, line, line, line, matrix, line, matrix, line, matrix, line,
            matrix, line,
        ),
        check_vma=False,
    )
```

```python
import functools

import jax
import jax.numpy as jnp
import numpy as np
from jax import lax
from jax.experimental import pallas as pl
from jax.experimental.pallas import tpu as pltpu
from jax.sharding import PartitionSpec as P

H = 12
HD = 64
ROT = 16
LANES = 128
EPS = 1e-05
MASKED = -1e30
VMEM = 56 * 1024 * 1024
BF = jnp.bfloat16
F32 = jnp.float32


def dot(left, right, dims=((1,), (0,))):
    return lax.dot_general(left, right, (dims, ((), ())), preferred_element_type=F32)


def back_dot(left, right):
    return dot(left, right, ((1,), (1,)))


def outer_sum(left, right):
    return dot(left, right, ((0,), (0,)))


def normalized(values):
    center = values - jnp.mean(values, axis=-1, keepdims=True)
    spread = jnp.mean(center * center, axis=-1, keepdims=True)
    inverse = lax.rsqrt(spread + EPS)
    return center * inverse, inverse


def norm_back(hat, inverse, gain, grad):
    scaled = grad * gain
    first = jnp.mean(scaled, axis=-1, keepdims=True)
    second = jnp.mean(scaled * hat, axis=-1, keepdims=True)
    return (
        inverse * (scaled - first - hat * second),
        jnp.sum(grad * hat, axis=0, keepdims=True),
        jnp.sum(grad, axis=0, keepdims=True),
    )


def rotary_tables(length):
    half = ROT // 2
    inverse = np.float32(10000.0) ** (-np.arange(0, ROT, 2, dtype=np.float32) / np.float32(ROT))
    phase = np.arange(length, dtype=np.float32)[:, None] * inverse[None, :].astype(np.float32)
    cosine, sine = np.cos(phase), np.sin(phase)
    c = np.ones((length, HD), np.float32)
    s1 = np.zeros((length, HD), np.float32)
    s2 = np.zeros((length, HD), np.float32)
    c[:, :half] = cosine
    c[:, half:ROT] = cosine
    s1[:, :half] = -sine
    s2[:, half:ROT] = sine
    return tuple(np.concatenate([t, t], axis=1) for t in (c, s1, s2))


def turn(values, c, s1, s2):
    half = ROT // 2
    return (
        values * c
        + pltpu.roll(values, LANES - half, 1) * s1
        + pltpu.roll(values, half, 1) * s2
    )


def project_kernel(
    n, block_len, used, me, tokens, cot, vectors, c_ref, s1_ref, s2_ref, *rest
):
    own, other = rest[:2]
    columns, crossed = rest[2 : 2 + n], rest[2 + n : 2 + 2 * n]
    outs = rest[2 + 2 * n : 2 + 3 * n]
    w, normed, b, laid = rest[2 + 3 * n :]
    kind = pl.program_id(0)
    model = tokens.shape[1]
    parts = n // 4
    f = me[1]

    for part in range(parts):
        unit = kind * parts + part
        laid[f, part] = own[unit]
        laid[f ^ 1, part] = other[unit]
        for shift in range(n):

            @pl.when((unit ^ me[0]) == shift)
            def _(shift=shift, part=part):
                for index in range(columns[shift].shape[0]):
                    step = 2 * (index + 1)
                    laid[f ^ step, part] = columns[shift][index]
                    laid[f ^ step ^ 1, part] = crossed[shift][index]

    w[0] = laid[...].reshape(model, model)

    @pl.when(kind == 0)
    def _():
        hat, _inverse = normalized(tokens[...].astype(F32))
        normed[...] = (hat * vectors[0:1, :model] + vectors[1:2, :model]).astype(BF)

    for t in range(3):

        @pl.when(kind == t)
        def _(t=t):
            b[...] = vectors[4:5, t * model : (t + 1) * model]

    width = outs[0].shape[-1]
    per = w.shape[-1] // width

    def operands(shift, left):
        group = jnp.minimum(me[0] ^ shift, used - 1)
        rows = pl.multiple_of((group // per) * block_len, block_len)
        cols = pl.multiple_of((group % per) * width, LANES)
        return left[pl.ds(rows, block_len)], pl.ds(cols, width)

    @pl.when(kind < 2)
    def _():
        c, s1, s2 = c_ref[...], s1_ref[...], s2_ref[...]
        for shift in range(n):
            left, cols = operands(shift, normed)
            full = dot(left, w[0, :, cols]) + b[:, cols]
            for j in range(width // LANES):
                at = slice(j * LANES, (j + 1) * LANES)
                outs[shift][0, :, at] = turn(full[:, at], c, s1, s2).astype(BF)

    @pl.when(kind == 2)
    def _():
        for shift in range(n):
            left, cols = operands(shift, normed)
            outs[shift][0] = (dot(left, w[0, :, cols]) + b[:, cols]).astype(BF)

    @pl.when(kind == 3)
    def _():
        for shift in range(n):
            left, cols = operands(shift, cot)
            outs[shift][0] = back_dot(left, w[0, cols]).astype(BF)


def project(n, m, at, tokens, cot, vectors, pieces, tables, block_len, width, used):
    rows, model = tokens.shape
    parts = n // 4
    whole = pl.BlockSpec((rows, model), lambda kind, me_ref: (0, 0))
    own = pl.BlockSpec((block_len, LANES), lambda kind, me_ref: (me_ref[0], 0))
    return pl.pallas_call(
        functools.partial(project_kernel, n, block_len, used),
        grid_spec=pltpu.PrefetchScalarGridSpec(
            num_scalar_prefetch=1,
            grid=(4,),
            in_specs=[
                whole,
                whole,
                pl.BlockSpec(vectors.shape, lambda kind, me_ref: (0, 0)),
                own,
                own,
                own,
            ]
            + [pl.BlockSpec(p.shape, lambda kind, me_ref: (0, 0, 0)) for p in pieces],
            out_specs=[pl.BlockSpec((1, block_len, width), lambda kind, me_ref: (kind, 0, 0))] * n
            + [pl.BlockSpec((1, model, model), lambda kind, me_ref: (kind, 0, 0))],
            scratch_shapes=[
                pltpu.VMEM((rows, model), BF),
                pltpu.VMEM((1, model), F32),
                pltpu.VMEM((m, parts, model // m // parts, model), BF),
            ],
        ),
        out_shape=[jax.ShapeDtypeStruct((4, block_len, width), BF)] * n
        + [jax.ShapeDtypeStruct((4, model, model), BF)],
        compiler_params=pltpu.CompilerParams(vmem_limit_bytes=VMEM),
        cost_estimate=pl.CostEstimate(
            flops=8 * rows * model * model,
            bytes_accessed=2 * (4 * model * model + 6 * rows * model),
            transcendentals=0,
        ),
        name="project",
    )(at, tokens, cot, vectors, *(jnp.asarray(t) for t in tables), *pieces)


def attend_kernel(n, block, me, *refs):
    ins = refs[:n]
    c_ref, s1_ref, s2_ref = refs[n : n + 3]
    outs = refs[n + 3 : 2 * n + 3]
    (q_s, k_s, v_s, g_s, qt_s, kt_s, vt_s, gt_s, sc, pb, dk, dv, o_s, dq_s) = refs[2 * n + 3 :]
    two = 2 * block
    scale = HD**-0.5

    for shift in range(n):
        at = ins[shift]
        place = me[0] ^ shift
        for kind, plain, flipped in ((0, q_s, qt_s), (1, k_s, kt_s), (2, v_s, vt_s), (3, g_s, gt_s)):
            piece = at[kind].astype(F32)
            if kind == 0:
                piece = piece * scale
            plain[place] = piece.astype(BF)
            flipped[place] = piece.T.astype(BF)

    lane = lax.broadcasted_iota(jnp.int32, (block, LANES), 1) < HD
    row = lax.broadcasted_iota(jnp.int32, (LANES, block), 0) < HD
    key_at = lax.broadcasted_iota(jnp.int32, (block, two), 0)
    query_at = lax.broadcasted_iota(jnp.int32, (block, two), 1)
    query_at = jnp.where(query_at >= block, query_at - block, query_at)
    allowed = key_at <= query_at

    def beside(flipped):
        zero = jnp.zeros_like(flipped)
        return jnp.concatenate([jnp.where(row, flipped, zero), jnp.where(row, zero, flipped)], axis=1)

    def below(plain):
        zero = jnp.zeros_like(plain)
        return jnp.concatenate([jnp.where(lane, plain, zero), jnp.where(lane, zero, plain)], axis=0)

    def loop(upto, body, init):
        if isinstance(upto, int):
            for j in range(upto):
                init = body(j, init)
            return init
        return lax.fori_loop(0, upto, body, init)

    def query_block(i, _):
        queries_t = beside(qt_s[i].astype(F32)).astype(BF)
        grads_t = beside(gt_s[i].astype(F32)).astype(BF)
        queries = below(q_s[i].astype(F32)).astype(BF)
        grads = below(g_s[i].astype(F32)).astype(BF)

        def score(j, top):
            found = dot(k_s[j], queries_t)
            sc[j] = found
            return jnp.maximum(top, jnp.max(found, axis=0, keepdims=True))

        diagonal = jnp.where(allowed, dot(k_s[i], queries_t), MASKED)
        sc[i] = diagonal
        top = loop(i, score, jnp.max(diagonal, axis=0, keepdims=True))

        def weigh(j, total):
            exps = jnp.exp(sc[j] - top)
            sc[j] = exps
            return total + jnp.sum(exps, axis=0, keepdims=True)

        total = loop(i + 1, weigh, jnp.zeros((1, two), F32))
        inverse = 1.0 / total

        def mix(j, heads):
            probs = sc[j] * inverse
            sc[j] = probs
            low = probs.astype(BF)
            pb[j] = low
            return tuple(
                heads[h] + dot(vt_s[j, h * HD : (h + 1) * HD], low[:, h * block : (h + 1) * block])
                for h in range(2)
            )

        none = jnp.zeros((HD, block), F32)
        heads = loop(i + 1, mix, (none, none))
        delta = jnp.concatenate(
            [
                jnp.sum(heads[h] * gt_s[i, h * HD : (h + 1) * HD].astype(F32), axis=0, keepdims=True)
                for h in range(2)
            ],
            axis=1,
        )
        o_s[i] = jnp.concatenate(heads, axis=0).T.astype(BF)

        def back(j, found, first):
            grad_scores = (sc[j] * (dot(v_s[j], grads_t) - delta)).astype(BF)
            key_part = dot(grad_scores, queries)
            value_part = dot(pb[j], grads)
            if first:
                dk[j] = key_part
                dv[j] = value_part
            else:
                dk[j] = dk[j] + key_part
                dv[j] = dv[j] + value_part
            return tuple(
                found[h]
                + dot(kt_s[j, h * HD : (h + 1) * HD], grad_scores[:, h * block : (h + 1) * block])
                for h in range(2)
            )

        found = back(i, (none, none), True)
        found = loop(i, lambda j, kept: back(j, kept, False), found)
        grad_query = jnp.concatenate(found, axis=0).T * scale
        dq_s[i] = turn(grad_query, c_ref[i], -s1_ref[i], -s2_ref[i]).astype(BF)
        return 0

    if n <= 4:
        for i in range(n):
            query_block(i, 0)
    else:
        lax.fori_loop(0, n, query_block, 0)

    for shift in range(n):
        place = me[0] ^ shift
        c, s1, s2 = c_ref[place], -s1_ref[place], -s2_ref[place]
        outs[shift][0] = o_s[place]
        outs[shift][1] = dq_s[place]
        outs[shift][2] = turn(dk[place], c, s1, s2).astype(BF)
        outs[shift][3] = dv[place].astype(BF)


def attend(n, me, pieces, tables):
    _, block, width = pieces[0].shape
    length = n * block
    spec = pl.BlockSpec((4, block, LANES), lambda j, me_ref: (0, 0, j))
    table_spec = pl.BlockSpec((n, block, LANES), lambda j, me_ref: (0, 0, 0))
    plain = pltpu.VMEM((n, block, LANES), BF)
    flipped = pltpu.VMEM((n, LANES, block), BF)
    total = pltpu.VMEM((n, block, LANES), F32)
    work = width // HD * length * (length + block) // 2
    return pl.pallas_call(
        functools.partial(attend_kernel, n, block),
        grid_spec=pltpu.PrefetchScalarGridSpec(
            num_scalar_prefetch=1,
            grid=(width // LANES,),
            in_specs=[spec] * n + [table_spec] * 3,
            out_specs=[spec] * n,
            scratch_shapes=[
                plain, plain, plain, plain,
                flipped, flipped, flipped, flipped,
                pltpu.VMEM((n, block, 2 * block), F32),
                pltpu.VMEM((n, block, 2 * block), BF),
                total, total, plain, plain,
            ],
        ),
        out_shape=[jax.ShapeDtypeStruct((4, block, width), BF)] * n,
        compiler_params=pltpu.CompilerParams(vmem_limit_bytes=VMEM),
        cost_estimate=pl.CostEstimate(
            flops=12 * work * 4 * HD * 10, bytes_accessed=2 * 8 * length * width, transcendentals=work
        ),
        name="attend",
    )(me, *pieces, *(jnp.asarray(t).reshape(n, block, LANES) for t in tables))


def mlp_kernel(last, *refs):
    tokens, cot, vectors, w_up, b_up, w_down = refs[:6]
    model = tokens.shape[1]
    if last:
        start_out, start_grad, out, grad_in, grad_up, grad_down, grad_b, sums, normed = refs[6:]
    else:
        out, grad_in, grad_up, grad_down, grad_b, normed = refs[6:]
    step = pl.program_id(0)
    row = 7 if last else 6
    gain, bias = vectors[2:3, :model], vectors[3:4, :model]

    @pl.when(step == 0)
    def _():
        values = tokens[...].astype(F32)
        hat, _inverse = normalized(values)
        normed[...] = (hat * gain + bias).astype(BF)
        if last:
            out[...] = start_out[...]
            grad_in[...] = start_grad[...]
        else:
            out[...] = values + (vectors[5:6, :model] + vectors[8:9, :model])
            grad_in[...] = jnp.zeros_like(grad_in)

    up = w_up[...].reshape(model, -1)
    down = w_down[...].reshape(-1, model)
    hidden = dot(normed[...], up) + b_up[row : row + 1]
    share = 0.5 + 0.5 * lax.erf(hidden * (0.5**0.5))
    slope = share + hidden * (jnp.exp(-0.5 * hidden * hidden) * ((2.0 * np.pi) ** -0.5))
    active = (hidden * share).astype(BF)
    grad_hidden = (back_dot(cot[...], down) * slope).astype(BF)
    grad_b[...] = jnp.sum(grad_hidden.astype(F32), axis=0, keepdims=True)
    out[...] = out[...] + dot(active, down)
    grad_in[...] = grad_in[...] + back_dot(grad_hidden, up)
    grad_down[...] = outer_sum(active, cot[...]).astype(BF).reshape(grad_down.shape)
    grad_up[...] = outer_sum(normed[...], grad_hidden).astype(BF).reshape(grad_up.shape)

    if last:

        @pl.when(step == pl.num_programs(0) - 1)
        def _():
            hat, inverse = normalized(tokens[...].astype(F32))
            upstream = cot[...].astype(F32)
            back, grad_gain, grad_bias = norm_back(hat, inverse, gain, grad_in[...])
            grad_in[...] = upstream + back
            sums[0:1] = grad_gain
            sums[1:2] = grad_bias
            sums[2:3] = jnp.sum(upstream, axis=0, keepdims=True)
            sums[3:8] = jnp.zeros((5, sums.shape[1]), F32)


def mlp(tokens, cot, vectors, weights, start=None):
    rows, model = tokens.shape
    shards, units, shard_rows, _ = weights.shape
    half = units // 2 * model
    chunk = model // 2
    group = chunk * shards // half
    last = start is not None
    whole = pl.BlockSpec((rows, model), lambda j: (0, 0))
    line = pl.BlockSpec((1, chunk), lambda j: (0, j))
    tall = (shards, 1, shard_rows, chunk)
    flat = (group, units // 2, shard_rows, model)
    total = jax.ShapeDtypeStruct((rows, model), F32)
    grads = jax.ShapeDtypeStruct((shards, units // 2, shard_rows, model), BF)
    return pl.pallas_call(
        functools.partial(mlp_kernel, last),
        grid=(half // chunk,),
        in_specs=[
            whole,
            whole,
            pl.BlockSpec(vectors.shape, lambda j: (0, 0)),
            pl.BlockSpec(tall, lambda j: (0, j // 2, 0, j % 2)),
            pl.BlockSpec((16, chunk), lambda j: (0, j)),
            pl.BlockSpec(flat, lambda j: (j, 1, 0, 0)),
        ]
        + [whole] * (2 * last),
        out_specs=[
            whole,
            whole,
            pl.BlockSpec(tall, lambda j: (0, j // 2, 0, j % 2)),
            pl.BlockSpec(flat, lambda j: (j, 0, 0, 0)),
            line,
        ]
        + ([pl.BlockSpec((8, model), lambda j: (0, 0))] if last else []),
        out_shape=[total, total, grads, grads, jax.ShapeDtypeStruct((1, half), F32)]
        + ([jax.ShapeDtypeStruct((8, model), F32)] if last else []),
        scratch_shapes=[pltpu.VMEM((rows, model), BF)],
        compiler_params=pltpu.CompilerParams(vmem_limit_bytes=VMEM),
        cost_estimate=pl.CostEstimate(
            flops=12 * rows * model * half,
            bytes_accessed=8 * model * half + 12 * rows * model,
            transcendentals=2 * rows * half,
        ),
        name="mlp",
    )(tokens, cot, vectors, weights, vectors, weights, *(start or ()))


def finish_kernel(n, block_len, used, shards, at, *refs):
    answers = refs[:n]
    tokens, cot, vectors, base, grad_base, w, sums_two, grad_b = refs[n : n + 8]
    out, grad_out, own, other, line_own, line_other = refs[n + 8 : n + 14]
    held, normed, grads, grad_in, sums, lines = refs[n + 14 :]
    kind = pl.program_id(0)
    model = tokens.shape[1]
    width = answers[0].shape[-1]
    per = model // width

    for shift in range(n):
        group = jnp.minimum(at[0] ^ shift, used - 1)
        rows = pl.multiple_of((group // per) * block_len, block_len)
        cols = pl.multiple_of((group % per) * width, LANES)
        if used == n:
            held[pl.ds(rows, block_len), pl.ds(cols, width)] = answers[shift][0]
        else:

            @pl.when((at[0] ^ shift) < used)
            def _(rows=rows, cols=cols, shift=shift):
                held[pl.ds(rows, block_len), pl.ds(cols, width)] = answers[shift][0]

    @pl.when(kind == 0)
    def _():
        hat, _inverse = normalized(tokens[...].astype(F32))
        normed[...] = (hat * vectors[0:1, :model] + vectors[1:2, :model]).T.astype(BF)
        grad_in[...] = jnp.zeros_like(grad_in)
        out[...] = (base[...] + dot(held[...], w[0])).astype(BF)
        grads[...] = outer_sum(held[...], cot[...]).astype(BF).reshape(grads.shape)

    @pl.when(kind > 0)
    def _():
        grads[...] = dot(normed[...], held[...]).astype(BF).reshape(grads.shape)
        grad_in[...] = grad_in[...] + back_dot(held[...], w[0])
        sums[pl.ds(kind, 1)] = jnp.sum(held[...].astype(F32), axis=0, keepdims=True)

    for z in range(shards // 2):
        own[0, z] = grads[z, at[1]]
        other[0, z] = grads[z, at[1] ^ 1]

    @pl.when(kind == 3)
    def _():
        hat, inverse = normalized(tokens[...].astype(F32))
        back, grad_gain, grad_bias = norm_back(hat, inverse, vectors[0:1, :model], grad_in[...])
        grad_out[...] = (grad_base[...] + back).astype(BF)
        qkv = jnp.concatenate([sums[t : t + 1] for t in (1, 2, 3)], axis=1)
        whole = [
            grad_gain, grad_bias, sums_two[0:1], sums_two[1:2], sums_two[2:3], qkv, grad_b[0:1],
            grad_b[1:2],
        ]
        lines[...] = jnp.zeros_like(lines)
        for index, line in enumerate(whole):
            size = line.shape[1] // shards
            for f in range(shards):
                lines[f // 2, f % 2, index : index + 1, :size] = line[:, f * size : (f + 1) * size]
        for z in range(shards // 2):
            line_own[z] = lines[z, at[1]]
            line_other[z] = lines[z, at[1] ^ 1]


def finish(n, me, core, answers, tokens, cot, vectors, base, grad_base, w, sums_two, grad_b, shards, used):
    rows, model = tokens.shape
    block_len, width = answers[0].shape[1:]
    whole = pl.BlockSpec((rows, model), lambda kind, at: (0, 0))
    own_rows = model // shards

    def unit(kind, at):
        return lax.rem(kind + 3, 4)

    half = pl.BlockSpec(
        (1, shards // 2, own_rows, model), lambda kind, at: (unit(kind, at), 0, 0, 0)
    )
    half_shape = jax.ShapeDtypeStruct((4, shards // 2, own_rows, model), BF)
    half_lines = pl.BlockSpec((shards // 2, 8, model), lambda kind, at: (0, 0, 0))
    half_lines_shape = jax.ShapeDtypeStruct((shards // 2, 8, model), F32)
    return pl.pallas_call(
        functools.partial(finish_kernel, n, block_len, used, shards),
        grid_spec=pltpu.PrefetchScalarGridSpec(
            num_scalar_prefetch=1,
            grid=(4,),
            in_specs=[pl.BlockSpec((1, block_len, width), lambda kind, at: (kind, 0, 0))] * n
            + [
                whole,
                whole,
                pl.BlockSpec(vectors.shape, lambda kind, at: (0, 0)),
                whole,
                whole,
                pl.BlockSpec((1, model, model), lambda kind, at: (unit(kind, at), 0, 0)),
                pl.BlockSpec((8, model), lambda kind, at: (0, 0)),
                pl.BlockSpec(grad_b.shape, lambda kind, at: (0, 0)),
            ],
            out_specs=[whole, whole, half, half, half_lines, half_lines],
            scratch_shapes=[
                pltpu.VMEM((rows, model), BF),
                pltpu.VMEM((model, rows), BF),
                pltpu.VMEM((shards // 2, 2, own_rows, model), BF),
                pltpu.VMEM((rows, model), F32),
                pltpu.VMEM((8, model), F32),
                pltpu.VMEM((shards // 2, 2, 8, model), F32),
            ],
        ),
        out_shape=[
            jax.ShapeDtypeStruct((rows, model), BF),
            jax.ShapeDtypeStruct((rows, model), BF),
            half_shape,
            half_shape,
            half_lines_shape,
            half_lines_shape,
        ],
        compiler_params=pltpu.CompilerParams(vmem_limit_bytes=VMEM),
        cost_estimate=pl.CostEstimate(
            flops=16 * rows * model * model, bytes_accessed=40 * rows * model, transcendentals=0
        ),
        name="finish",
    )(
        jnp.stack([me, core]).astype(jnp.int32),
        *answers, tokens, cot, vectors, base, grad_base, w, sums_two, grad_b,
    )


def swap(value, shift, n):
    return lax.ppermute(value, "ctx", [(i, i ^ shift) for i in range(n)])


def swap_shard(value, shift, m):
    return lax.ppermute(value, "fsdp", [(i, i ^ shift) for i in range(m)])


def pack_kernel(q, qkv, out_w, *refs):
    out = refs[-1]
    rows = out_w.shape[0]
    out[:rows] = jnp.where(q[0] < 3, qkv[...].astype(F32), out_w[...].astype(F32)).astype(BF)
    lines = []
    for ref in refs[:-1]:
        line = ref[...].astype(F32).reshape(1, -1)
        lines.append(jnp.concatenate([line, jnp.zeros((1, out.shape[1] - line.shape[1]), F32)], axis=1))
    lines.append(jnp.zeros((out.shape[0] - rows - len(lines), out.shape[1]), F32))
    out[rows:] = jnp.concatenate(lines, axis=0).astype(BF)


def pack(q, qkv, out_w, vectors):
    rows, model = out_w.shape
    lines = [v.reshape(1, -1) if v.shape[0] < LANES else v for v in vectors]
    return pl.pallas_call(
        pack_kernel,
        grid_spec=pltpu.PrefetchScalarGridSpec(
            num_scalar_prefetch=1,
            grid=(1,),
            in_specs=[
                pl.BlockSpec((rows, model), lambda i, at: (0, jnp.minimum(at[0], 2))),
                pl.BlockSpec((rows, model), lambda i, at: (0, 0)),
            ]
            + [pl.BlockSpec(v.shape, lambda i, at, r=v.ndim: (0,) * r) for v in lines],
            out_specs=pl.BlockSpec((rows + 16, model), lambda i, at: (0, 0)),
        ),
        out_shape=jax.ShapeDtypeStruct((rows + 16, model), BF),
        name="pack",
    )(q.astype(jnp.int32).reshape(1), qkv, out_w, *lines)


def unpack_kernel(sizes, half, at, own, other, out):
    chips = own.shape[0]
    out[...] = jnp.zeros_like(out)
    rows = []
    for f in range(2 * chips):
        rel = f ^ at[0]
        both = jnp.where(rel % 2 == 0, own[rel // 2].astype(F32), other[rel // 2].astype(F32))
        rows.append(both)
    for index, size in enumerate(sizes):
        if index == half + 1:
            continue
        if index == half:
            cut = size // 2
            for h in range(2):
                line = [r[index : index + 1, h * cut : (h + 1) * cut] for r in rows]
                out[index + h : index + h + 1, : len(rows) * cut] = jnp.concatenate(line, axis=1)
        else:
            line = [r[index : index + 1, :size] for r in rows]
            out[index : index + 1, : len(rows) * size] = jnp.concatenate(line, axis=1)


def unpack(f, own, other, sizes, half):
    width = 2 * own.shape[0] * max(sizes[:half] + [sizes[half] // 2])
    full = pl.BlockSpec(own.shape, lambda i, at: (0, 0, 0))
    return pl.pallas_call(
        functools.partial(unpack_kernel, sizes, half),
        grid_spec=pltpu.PrefetchScalarGridSpec(
            num_scalar_prefetch=1,
            grid=(1,),
            in_specs=[full, full],
            out_specs=pl.BlockSpec((16, width), lambda i, at: (0, 0)),
        ),
        out_shape=jax.ShapeDtypeStruct((16, width), F32),
        name="unpack",
    )(f.astype(jnp.int32).reshape(1), own, other)


def along_z(mine, m):
    return [swap_shard(mine, step, m) for step in range(2, m, 2)]


def between_columns(along, n):
    return [along] + [swap(along, shift, n) for shift in range(1, n)]


def assemble_kernel(where, at, *refs):
    out = refs[-1]
    for piece, index, place in where:
        unit, shard = place(at)
        out[shard, unit] = refs[piece][index]


def assemble(at, pieces, n, m):
    where = []
    for unit in range(n):
        where.append((0, unit, lambda at, unit=unit: (unit, at[1])))
        where.append((1, unit, lambda at, unit=unit: (unit, at[1] ^ 1)))
    for core in range(2):
        for shift in range(n):
            for index in range(m // 2 - 1):
                where.append(
                    (
                        2 + core * n + shift,
                        index,
                        lambda at, shift=shift, flip=2 * (index + 1) ^ core: (at[0] ^ shift, at[1] ^ flip),
                    )
                )
    full = (m, n) + pieces[0].shape[1:]
    return pl.pallas_call(
        functools.partial(assemble_kernel, where),
        grid_spec=pltpu.PrefetchScalarGridSpec(
            num_scalar_prefetch=1,
            grid=(1,),
            in_specs=[pl.BlockSpec(p.shape, lambda i, at: (0, 0, 0)) for p in pieces],
            out_specs=pl.BlockSpec(full, lambda i, at: (0, 0, 0, 0)),
        ),
        out_shape=jax.ShapeDtypeStruct(full, pieces[0].dtype),
        compiler_params=pltpu.CompilerParams(vmem_limit_bytes=VMEM),
        name="assemble",
    )(at, *pieces)


def add_up(*pieces):
    return sum(p.astype(F32) for p in pieces).astype(BF)


def pick(value, at, axis=0):
    return lax.dynamic_index_in_dim(value, at, axis, keepdims=False)


def swapped(value, n):
    return [value] + [swap(value, s, n) for s in range(1, n)]


def ctx_step(halves, i, n):
    steps = [2**i for i in range(n.bit_length() - 1)]
    return [(value, swap(value, steps[(i + j) % len(steps)], n)) for j, value in enumerate(halves)]


def ctx_sum(halves, begin, n):
    terms = halves
    for i in range(begin, n.bit_length() - 1):
        terms = ctx_step([add_up(*t) for t in terms] if i else terms, i, n)
    return [term for half in terms for term in half]


def lay_kernel(shards, *refs):
    up, down = refs[8:]
    model = up.shape[1] // 4
    size = up.shape[1] // shards // 2
    ups = []
    for h in range(2):
        terms = refs[4 * h : 4 * h + 4]
        total = terms[0][...].astype(F32) + terms[1][...].astype(F32)
        ups.append(jnp.concatenate([total[0], total[1]], axis=1))
        rows = down.shape[0] // 4
        for unit in range(2):
            at = (2 * h + unit) * rows
            down[at : at + rows] = terms[2][unit].astype(F32) + terms[3][unit].astype(F32)
    for f in range(shards):
        line = [ups[h][:, f * size : (f + 1) * size] for h in range(2)]
        up[:, 2 * f * size : 2 * (f + 1) * size] = jnp.concatenate(line, axis=1)


def lay(first, second, shards, up_shape, down_shape):
    return pl.pallas_call(
        functools.partial(lay_kernel, shards),
        out_shape=[jax.ShapeDtypeStruct(up_shape, F32), jax.ShapeDtypeStruct(down_shape, F32)],
        compiler_params=pltpu.CompilerParams(vmem_limit_bytes=VMEM),
        name="lay",
    )(*first, *second)


def in_order(pieces, at):
    stacked = jnp.stack(pieces)
    return jnp.stack([pick(stacked, at ^ place) for place in range(len(pieces))])


def body(
    tokens,
    norm1_gain,
    norm1_bias,
    norm2_gain,
    norm2_bias,
    qkv_weight,
    qkv_bias,
    out_weight,
    out_bias,
    up_weight,
    up_bias,
    down_weight,
    down_bias,
    cotangent,
):
    block_len, seq_count, model = tokens.shape
    n = lax.axis_size("ctx")
    shards = lax.axis_size("fsdp")
    rows = block_len * seq_count
    hidden = up_weight.shape[1]
    me = lax.axis_index("ctx")
    me_arr = me.astype(jnp.int32).reshape(1)
    width = -(-seq_count * model // (n * LANES)) * LANES
    used = seq_count * model // width
    per = model // width

    parts = n // 4
    own_rows = out_weight.shape[0]

    vectors = (
        norm1_gain, norm1_bias, norm2_gain, norm2_bias, qkv_bias, out_bias, up_bias, out_bias,
        down_bias,
    )
    sizes = [v.shape[0] for v in vectors]
    per_shard = hidden // shards // 2

    def half_weights(h):
        up = up_weight.reshape(own_rows, shards, 2, per_shard)[:, :, h].reshape(own_rows, -1, model)
        down = down_weight[h * per_shard : (h + 1) * per_shard].reshape(-1, own_rows, model)
        return jnp.concatenate([up.transpose(1, 0, 2), down], axis=0)

    units = jnp.concatenate(
        [qkv_weight[None, :, t * model : (t + 1) * model] for t in range(3)] + [out_weight[None]]
    ).reshape(n, own_rows // parts, model)
    if n == 4:
        mine = pack(me, qkv_weight, out_weight, vectors)
    else:
        lines = [jnp.pad(v, (0, model - v.shape[0])) for v in vectors]
        lines = jnp.pad(jnp.stack(lines), ((0, 16 - len(vectors)), (0, 0)))
        mine = jnp.concatenate([pick(units, me), lines], axis=0)
    mine_rows = units.shape[1]
    came = along_z(mine, shards)
    along_units = jnp.stack([c[:mine_rows] for c in came])
    chips = jnp.stack([c[mine_rows:] for c in [mine] + came])
    first_half, _ = lax.optimization_barrier((half_weights(0), along_units))
    w_first = lax.all_gather(first_half, "fsdp", axis=0, tiled=False)
    unit_columns = between_columns(along_units, n)
    vectors = unpack(
        lax.axis_index("fsdp"), chips, swap_shard(chips, 1, shards), sizes, 6
    )
    inputs = tokens.transpose(1, 0, 2).reshape(rows, model)
    cot = cotangent.transpose(1, 0, 2).reshape(rows, model)
    vectors, inputs, cot, unit_columns = lax.optimization_barrier((vectors, inputs, cot, unit_columns))
    crossed = [swap_shard(held, 1, shards) for held in unit_columns]
    unit_pieces = [units, swap_shard(units, 1, shards)] + unit_columns + crossed

    tables = rotary_tables(n * block_len)
    def shard_sum(value):
        return lax.psum_scatter(value, "fsdp", scatter_dimension=0, tiled=False)

    at = jnp.stack([me, lax.axis_index("fsdp")]).astype(jnp.int32)
    *sent, w_units = project(
        n, shards, at, inputs, cot, vectors, unit_pieces, tables, block_len, width, used
    )
    pieces = [sent[0]] + [swap(sent[shift], shift, n) for shift in range(1, n)]
    mlp_inputs, second_half, _ = lax.optimization_barrier(
        (inputs, half_weights(1), (sent, w_first))
    )
    second_units = second_half.reshape(n, -1, model)
    along_second = along_z(pick(second_units, me), shards)
    base, grad_base, grad_up, grad_down, grad_b_first = mlp(
        mlp_inputs, cot, vectors, w_first
    )
    first_grads, pieces = lax.optimization_barrier(
        (jnp.concatenate([grad_up, grad_down], axis=1), pieces)
    )
    first_shard = shard_sum(first_grads)
    second_columns = between_columns(jnp.stack(along_second), n)
    made = attend(n, me_arr, pieces, tables)
    mlp_inputs, second_columns, second_units, _ = lax.optimization_barrier(
        (inputs, second_columns, second_units, made)
    )
    second_pieces = [second_units, swap_shard(second_units, 1, shards)] + second_columns
    second_pieces += [swap_shard(held, 1, shards) for held in second_columns]
    w_second = assemble(at, second_pieces, n, shards).reshape(shards, 4, own_rows, model)
    answers = [made[0]] + [swap(made[shift], shift, n) for shift in range(1, n)]
    base, grad_base, grad_up, grad_down, grad_b_second, sums_two = mlp(
        mlp_inputs, cot, vectors, w_second, start=(base, grad_base)
    )
    second_grads, answers = lax.optimization_barrier(
        (jnp.concatenate([grad_up, grad_down], axis=1), answers)
    )
    second_shard = shard_sum(second_grads)
    core = lax.axis_index("fsdp") % 2
    layer_out, tokens_grad, own, other, line_own, line_other = finish(
        n, me, core, answers, inputs, cot, vectors, base, grad_base, w_units, sums_two,
        jnp.concatenate([grad_b_first, grad_b_second]), shards, used,
    )

    def placed(value):
        return value.reshape(seq_count, block_len, model).transpose(1, 0, 2)

    z = lax.axis_index("fsdp") // 2
    chip = add_up(own, swap_shard(other, 1, shards))
    line_chip = add_up(line_own, swap_shard(line_other, 1, shards))
    chip = jnp.concatenate([chip, jnp.pad(line_chip[None], ((0, 3), (0, 0), (0, 0), (0, 0)))], axis=2)
    chip = (
        chip.reshape(4, shards // 2, parts, -1, model)
        .transpose(0, 2, 1, 3, 4)
        .reshape(n, shards // 2, -1, model)
    )
    unit = add_up(pick(chip, me), *[swap(pick(chip, me ^ s), s, n) for s in range(1, n)])
    unit, first_shard, second_shard = lax.optimization_barrier((unit, first_shard, second_shard))
    first_sum = ctx_sum([first_shard[:2], first_shard[2:]], 0, n)
    second_sum = ctx_sum([second_shard[:2], second_shard[2:]], 0, n)
    mine = add_up(
        pick(unit, z),
        *[swap_shard(pick(unit, z ^ s), 2 * s, shards) for s in range(1, shards // 2)],
    )
    unit_all = swapped(mine, n)
    part_units = in_order(unit_all, me).reshape(4, -1, model).astype(F32)
    line_sums = part_units[0, own_rows:]
    part_units = part_units[:, :own_rows]
    part_qkv = jnp.concatenate([part_units[t] for t in range(3)], axis=1)
    part_up, part_down = lay(first_sum, second_sum, shards, up_weight.shape, down_weight.shape)
    sizes = [own_rows] * 5 + [3 * own_rows, per_shard, per_shard]
    gain1, bias1, gain2, bias2, columns, qkv_b, *up_b = [
        line_sums[index, :size] for index, size in enumerate(sizes)
    ]
    return (
        placed(layer_out), placed(tokens_grad), gain1, bias1, gain2, bias2, part_qkv, qkv_b,
        part_units[3], columns, part_up, jnp.concatenate(up_b), part_down, columns,
    )


def solution(mesh):
    blocks = P("ctx", "fsdp", None)
    line, matrix = P("fsdp"), P("fsdp", None)
    return jax.shard_map(
        body,
        mesh=mesh,
        in_specs=(
            blocks, line, line, line, line, matrix, line, matrix, line, matrix, line, matrix, line,
            blocks,
        ),
        out_specs=(
            blocks, blocks, line, line, line, line, matrix, line, matrix, line, matrix, line,
            matrix, line,
        ),
        check_vma=False,
    )
```

```python
import functools

import jax
import jax.numpy as jnp
import numpy as np
from jax import lax
from jax.experimental import pallas as pl
from jax.experimental.pallas import tpu as pltpu
from jax.sharding import PartitionSpec as P

H = 12
HD = 64
ROT = 16
LANES = 128
EPS = 1e-05
MASKED = -1e30
VMEM = 56 * 1024 * 1024
BF = jnp.bfloat16
F32 = jnp.float32


def dot(left, right, dims=((1,), (0,))):
    return lax.dot_general(left, right, (dims, ((), ())), preferred_element_type=F32)


def back_dot(left, right):
    return dot(left, right, ((1,), (1,)))


def outer_sum(left, right):
    return dot(left, right, ((0,), (0,)))


def normalized(values):
    center = values - jnp.mean(values, axis=-1, keepdims=True)
    spread = jnp.mean(center * center, axis=-1, keepdims=True)
    inverse = lax.rsqrt(spread + EPS)
    return center * inverse, inverse


def norm_back(hat, inverse, gain, grad):
    scaled = grad * gain
    first = jnp.mean(scaled, axis=-1, keepdims=True)
    second = jnp.mean(scaled * hat, axis=-1, keepdims=True)
    return (
        inverse * (scaled - first - hat * second),
        jnp.sum(grad * hat, axis=0, keepdims=True),
        jnp.sum(grad, axis=0, keepdims=True),
    )


def rotary_tables(length):
    half = ROT // 2
    inverse = np.float32(10000.0) ** (-np.arange(0, ROT, 2, dtype=np.float32) / np.float32(ROT))
    phase = np.arange(length, dtype=np.float32)[:, None] * inverse[None, :].astype(np.float32)
    cosine, sine = np.cos(phase), np.sin(phase)
    c = np.ones((length, HD), np.float32)
    s1 = np.zeros((length, HD), np.float32)
    s2 = np.zeros((length, HD), np.float32)
    c[:, :half] = cosine
    c[:, half:ROT] = cosine
    s1[:, :half] = -sine
    s2[:, half:ROT] = sine
    return tuple(np.concatenate([t, t], axis=1) for t in (c, s1, s2))


def turn(values, c, s1, s2):
    half = ROT // 2
    return (
        values * c
        + pltpu.roll(values, LANES - half, 1) * s1
        + pltpu.roll(values, half, 1) * s2
    )


def project_kernel(
    n, block_len, used, me, tokens, cot, vectors, c_ref, s1_ref, s2_ref, *rest
):
    own, other = rest[:2]
    columns, crossed = rest[2 : 2 + n], rest[2 + n : 2 + 2 * n]
    outs = rest[2 + 2 * n : 2 + 3 * n]
    w, normed, b, laid = rest[2 + 3 * n :]
    kind = pl.program_id(0)
    model = tokens.shape[1]
    parts = n // 4
    f = me[1]

    for part in range(parts):
        unit = kind * parts + part
        laid[f, part] = own[unit]
        laid[f ^ 1, part] = other[unit]
        for shift in range(n):

            @pl.when((unit ^ me[0]) == shift)
            def _(shift=shift, part=part):
                for index in range(columns[shift].shape[0]):
                    step = 2 * (index + 1)
                    laid[f ^ step, part] = columns[shift][index]
                    laid[f ^ step ^ 1, part] = crossed[shift][index]

    w[0] = laid[...].reshape(model, model)

    @pl.when(kind == 0)
    def _():
        hat, _inverse = normalized(tokens[...].astype(F32))
        normed[...] = (hat * vectors[0:1, :model] + vectors[1:2, :model]).astype(BF)

    for t in range(3):

        @pl.when(kind == t)
        def _(t=t):
            b[...] = vectors[4:5, t * model : (t + 1) * model]

    width = outs[0].shape[-1]
    per = w.shape[-1] // width

    def operands(shift, left):
        group = jnp.minimum(me[0] ^ shift, used - 1)
        rows = pl.multiple_of((group // per) * block_len, block_len)
        cols = pl.multiple_of((group % per) * width, LANES)
        return left[pl.ds(rows, block_len)], pl.ds(cols, width)

    @pl.when(kind < 2)
    def _():
        c, s1, s2 = c_ref[...], s1_ref[...], s2_ref[...]
        for shift in range(n):
            left, cols = operands(shift, normed)
            full = dot(left, w[0, :, cols]) + b[:, cols]
            for j in range(width // LANES):
                at = slice(j * LANES, (j + 1) * LANES)
                outs[shift][0, :, at] = turn(full[:, at], c, s1, s2).astype(BF)

    @pl.when(kind == 2)
    def _():
        for shift in range(n):
            left, cols = operands(shift, normed)
            outs[shift][0] = (dot(left, w[0, :, cols]) + b[:, cols]).astype(BF)

    @pl.when(kind == 3)
    def _():
        for shift in range(n):
            left, cols = operands(shift, cot)
            outs[shift][0] = back_dot(left, w[0, cols]).astype(BF)


def project(n, m, at, tokens, cot, vectors, pieces, tables, block_len, width, used):
    rows, model = tokens.shape
    parts = n // 4
    whole = pl.BlockSpec((rows, model), lambda kind, me_ref: (0, 0))
    own = pl.BlockSpec((block_len, LANES), lambda kind, me_ref: (me_ref[0], 0))
    return pl.pallas_call(
        functools.partial(project_kernel, n, block_len, used),
        grid_spec=pltpu.PrefetchScalarGridSpec(
            num_scalar_prefetch=1,
            grid=(4,),
            in_specs=[
                whole,
                whole,
                pl.BlockSpec(vectors.shape, lambda kind, me_ref: (0, 0)),
                own,
                own,
                own,
            ]
            + [pl.BlockSpec(p.shape, lambda kind, me_ref: (0, 0, 0)) for p in pieces],
            out_specs=[pl.BlockSpec((1, block_len, width), lambda kind, me_ref: (kind, 0, 0))] * n
            + [pl.BlockSpec((1, model, model), lambda kind, me_ref: (kind, 0, 0))],
            scratch_shapes=[
                pltpu.VMEM((rows, model), BF),
                pltpu.VMEM((1, model), F32),
                pltpu.VMEM((m, parts, model // m // parts, model), BF),
            ],
        ),
        out_shape=[jax.ShapeDtypeStruct((4, block_len, width), BF)] * n
        + [jax.ShapeDtypeStruct((4, model, model), BF)],
        compiler_params=pltpu.CompilerParams(vmem_limit_bytes=VMEM),
        cost_estimate=pl.CostEstimate(
            flops=8 * rows * model * model,
            bytes_accessed=2 * (4 * model * model + 6 * rows * model),
            transcendentals=0,
        ),
        name="project",
    )(at, tokens, cot, vectors, *(jnp.asarray(t) for t in tables), *pieces)


def attend_kernel(n, block, me, *refs):
    ins = refs[:n]
    c_ref, s1_ref, s2_ref = refs[n : n + 3]
    outs = refs[n + 3 : 2 * n + 3]
    (q_s, k_s, v_s, g_s, qt_s, kt_s, vt_s, gt_s, sc, pb, dk, dv, o_s, dq_s) = refs[2 * n + 3 :]
    two = 2 * block
    scale = HD**-0.5

    for shift in range(n):
        at = ins[shift]
        place = me[0] ^ shift
        for kind, plain, flipped in ((0, q_s, qt_s), (1, k_s, kt_s), (2, v_s, vt_s), (3, g_s, gt_s)):
            piece = at[kind].astype(F32)
            if kind == 0:
                piece = piece * scale
            plain[place] = piece.astype(BF)
            flipped[place] = piece.T.astype(BF)

    lane = lax.broadcasted_iota(jnp.int32, (block, LANES), 1) < HD
    row = lax.broadcasted_iota(jnp.int32, (LANES, block), 0) < HD
    key_at = lax.broadcasted_iota(jnp.int32, (block, two), 0)
    query_at = lax.broadcasted_iota(jnp.int32, (block, two), 1)
    query_at = jnp.where(query_at >= block, query_at - block, query_at)
    allowed = key_at <= query_at

    def beside(flipped):
        zero = jnp.zeros_like(flipped)
        return jnp.concatenate([jnp.where(row, flipped, zero), jnp.where(row, zero, flipped)], axis=1)

    def below(plain):
        zero = jnp.zeros_like(plain)
        return jnp.concatenate([jnp.where(lane, plain, zero), jnp.where(lane, zero, plain)], axis=0)

    def loop(upto, body, init):
        if isinstance(upto, int):
            for j in range(upto):
                init = body(j, init)
            return init
        return lax.fori_loop(0, upto, body, init)

    def query_block(i, _):
        queries_t = beside(qt_s[i].astype(F32)).astype(BF)
        grads_t = beside(gt_s[i].astype(F32)).astype(BF)
        queries = below(q_s[i].astype(F32)).astype(BF)
        grads = below(g_s[i].astype(F32)).astype(BF)

        def score(j, top):
            found = dot(k_s[j], queries_t)
            sc[j] = found
            return jnp.maximum(top, jnp.max(found, axis=0, keepdims=True))

        diagonal = jnp.where(allowed, dot(k_s[i], queries_t), MASKED)
        sc[i] = diagonal
        top = loop(i, score, jnp.max(diagonal, axis=0, keepdims=True))

        def weigh(j, total):
            exps = jnp.exp(sc[j] - top)
            sc[j] = exps
            return total + jnp.sum(exps, axis=0, keepdims=True)

        total = loop(i + 1, weigh, jnp.zeros((1, two), F32))
        inverse = 1.0 / total

        def mix(j, heads):
            probs = sc[j] * inverse
            sc[j] = probs
            low = probs.astype(BF)
            pb[j] = low
            return tuple(
                heads[h] + dot(vt_s[j, h * HD : (h + 1) * HD], low[:, h * block : (h + 1) * block])
                for h in range(2)
            )

        none = jnp.zeros((HD, block), F32)
        heads = loop(i + 1, mix, (none, none))
        delta = jnp.concatenate(
            [
                jnp.sum(heads[h] * gt_s[i, h * HD : (h + 1) * HD].astype(F32), axis=0, keepdims=True)
                for h in range(2)
            ],
            axis=1,
        )
        o_s[i] = jnp.concatenate(heads, axis=0).T.astype(BF)

        def back(j, found, first):
            grad_scores = (sc[j] * (dot(v_s[j], grads_t) - delta)).astype(BF)
            key_part = dot(grad_scores, queries)
            value_part = dot(pb[j], grads)
            if first:
                dk[j] = key_part
                dv[j] = value_part
            else:
                dk[j] = dk[j] + key_part
                dv[j] = dv[j] + value_part
            return tuple(
                found[h]
                + dot(kt_s[j, h * HD : (h + 1) * HD], grad_scores[:, h * block : (h + 1) * block])
                for h in range(2)
            )

        found = back(i, (none, none), True)
        found = loop(i, lambda j, kept: back(j, kept, False), found)
        grad_query = jnp.concatenate(found, axis=0).T * scale
        dq_s[i] = turn(grad_query, c_ref[i], -s1_ref[i], -s2_ref[i]).astype(BF)
        return 0

    if n <= 4:
        for i in range(n):
            query_block(i, 0)
    else:
        lax.fori_loop(0, n, query_block, 0)

    for shift in range(n):
        place = me[0] ^ shift
        c, s1, s2 = c_ref[place], -s1_ref[place], -s2_ref[place]
        outs[shift][0] = o_s[place]
        outs[shift][1] = dq_s[place]
        outs[shift][2] = turn(dk[place], c, s1, s2).astype(BF)
        outs[shift][3] = dv[place].astype(BF)


def attend(n, me, pieces, tables):
    _, block, width = pieces[0].shape
    length = n * block
    spec = pl.BlockSpec((4, block, LANES), lambda j, me_ref: (0, 0, j))
    table_spec = pl.BlockSpec((n, block, LANES), lambda j, me_ref: (0, 0, 0))
    plain = pltpu.VMEM((n, block, LANES), BF)
    flipped = pltpu.VMEM((n, LANES, block), BF)
    total = pltpu.VMEM((n, block, LANES), F32)
    work = width // HD * length * (length + block) // 2
    return pl.pallas_call(
        functools.partial(attend_kernel, n, block),
        grid_spec=pltpu.PrefetchScalarGridSpec(
            num_scalar_prefetch=1,
            grid=(width // LANES,),
            in_specs=[spec] * n + [table_spec] * 3,
            out_specs=[spec] * n,
            scratch_shapes=[
                plain, plain, plain, plain,
                flipped, flipped, flipped, flipped,
                pltpu.VMEM((n, block, 2 * block), F32),
                pltpu.VMEM((n, block, 2 * block), BF),
                total, total, plain, plain,
            ],
        ),
        out_shape=[jax.ShapeDtypeStruct((4, block, width), BF)] * n,
        compiler_params=pltpu.CompilerParams(vmem_limit_bytes=VMEM),
        cost_estimate=pl.CostEstimate(
            flops=12 * work * 4 * HD * 10, bytes_accessed=2 * 8 * length * width, transcendentals=work
        ),
        name="attend",
    )(me, *pieces, *(jnp.asarray(t).reshape(n, block, LANES) for t in tables))


def mlp_kernel(last, *refs):
    tokens, cot, vectors, w_up, b_up, w_down = refs[:6]
    model = tokens.shape[1]
    if last:
        start_out, start_grad, out, grad_in, grad_up, grad_down, grad_b, sums, normed, flipped = refs[6:]
    else:
        out, grad_in, grad_up, grad_down, grad_b, normed, flipped = refs[6:]
    step = pl.program_id(0)
    row = 7 if last else 6
    gain, bias = vectors[2:3, :model], vectors[3:4, :model]

    @pl.when(step == 0)
    def _():
        values = tokens[...].astype(F32)
        hat, _inverse = normalized(values)
        rounded = hat * gain + bias
        normed[...] = rounded.astype(BF)
        flipped[...] = rounded.T.astype(BF)
        if last:
            out[...] = start_out[...]
            grad_in[...] = start_grad[...]
        else:
            out[...] = values + (vectors[5:6, :model] + vectors[8:9, :model])
            grad_in[...] = jnp.zeros_like(grad_in)

    up = w_up[...].reshape(model, -1)
    down = w_down[...].reshape(-1, model)
    hidden = dot(normed[...], up) + b_up[row : row + 1]
    share = 0.5 + 0.5 * lax.erf(hidden * (0.5**0.5))
    slope = share + hidden * (jnp.exp(-0.5 * hidden * hidden) * ((2.0 * np.pi) ** -0.5))
    active = (hidden * share).astype(BF)
    grad_hidden = (back_dot(cot[...], down) * slope).astype(BF)
    grad_b[...] = jnp.sum(grad_hidden.astype(F32), axis=0, keepdims=True)
    out[...] = out[...] + dot(active, down)
    grad_in[...] = grad_in[...] + back_dot(grad_hidden, up)
    grad_down[...] = outer_sum(active, cot[...]).astype(BF).reshape(grad_down.shape)
    grad_up[...] = dot(flipped[...], grad_hidden).astype(BF).reshape(grad_up.shape)

    if last:

        @pl.when(step == pl.num_programs(0) - 1)
        def _():
            hat, inverse = normalized(tokens[...].astype(F32))
            upstream = cot[...].astype(F32)
            back, grad_gain, grad_bias = norm_back(hat, inverse, gain, grad_in[...])
            grad_in[...] = upstream + back
            sums[0:1] = grad_gain
            sums[1:2] = grad_bias
            sums[2:3] = jnp.sum(upstream, axis=0, keepdims=True)
            sums[3:8] = jnp.zeros((5, sums.shape[1]), F32)


def mlp(tokens, cot, vectors, weights, start=None):
    rows, model = tokens.shape
    shards, units, shard_rows, _ = weights.shape
    half = units // 2 * model
    chunk = model // 2
    group = chunk * shards // half
    last = start is not None
    whole = pl.BlockSpec((rows, model), lambda j: (0, 0))
    line = pl.BlockSpec((1, chunk), lambda j: (0, j))
    tall = (shards, 1, shard_rows, chunk)
    flat = (group, units // 2, shard_rows, model)
    total = jax.ShapeDtypeStruct((rows, model), F32)
    grads = jax.ShapeDtypeStruct((shards, units // 2, shard_rows, model), BF)
    return pl.pallas_call(
        functools.partial(mlp_kernel, last),
        grid=(half // chunk,),
        in_specs=[
            whole,
            whole,
            pl.BlockSpec(vectors.shape, lambda j: (0, 0)),
            pl.BlockSpec(tall, lambda j: (0, j // 2, 0, j % 2)),
            pl.BlockSpec((16, chunk), lambda j: (0, j)),
            pl.BlockSpec(flat, lambda j: (j, 1, 0, 0)),
        ]
        + [whole] * (2 * last),
        out_specs=[
            whole,
            whole,
            pl.BlockSpec(tall, lambda j: (0, j // 2, 0, j % 2)),
            pl.BlockSpec(flat, lambda j: (j, 0, 0, 0)),
            line,
        ]
        + ([pl.BlockSpec((8, model), lambda j: (0, 0))] if last else []),
        out_shape=[total, total, grads, grads, jax.ShapeDtypeStruct((1, half), F32)]
        + ([jax.ShapeDtypeStruct((8, model), F32)] if last else []),
        scratch_shapes=[pltpu.VMEM((rows, model), BF), pltpu.VMEM((model, rows), BF)],
        compiler_params=pltpu.CompilerParams(vmem_limit_bytes=VMEM),
        cost_estimate=pl.CostEstimate(
            flops=12 * rows * model * half,
            bytes_accessed=8 * model * half + 12 * rows * model,
            transcendentals=2 * rows * half,
        ),
        name="mlp",
    )(tokens, cot, vectors, weights, vectors, weights, *(start or ()))


def finish_kernel(n, block_len, used, shards, at, *refs):
    answers = refs[:n]
    tokens, cot, vectors, base, grad_base, w, sums_two, grad_b = refs[n : n + 8]
    out, grad_out, own, other, line_own, line_other = refs[n + 8 : n + 14]
    held, normed, grads, grad_in, sums, lines = refs[n + 14 :]
    kind = pl.program_id(0)
    model = tokens.shape[1]
    width = answers[0].shape[-1]
    per = model // width

    for shift in range(n):
        group = jnp.minimum(at[0] ^ shift, used - 1)
        rows = pl.multiple_of((group // per) * block_len, block_len)
        cols = pl.multiple_of((group % per) * width, LANES)
        if used == n:
            held[pl.ds(rows, block_len), pl.ds(cols, width)] = answers[shift][0]
        else:

            @pl.when((at[0] ^ shift) < used)
            def _(rows=rows, cols=cols, shift=shift):
                held[pl.ds(rows, block_len), pl.ds(cols, width)] = answers[shift][0]

    @pl.when(kind == 0)
    def _():
        hat, _inverse = normalized(tokens[...].astype(F32))
        normed[...] = (hat * vectors[0:1, :model] + vectors[1:2, :model]).T.astype(BF)
        grad_in[...] = jnp.zeros_like(grad_in)
        out[...] = (base[...] + dot(held[...], w[0])).astype(BF)
        grads[...] = outer_sum(held[...], cot[...]).astype(BF).reshape(grads.shape)

    @pl.when(kind > 0)
    def _():
        grads[...] = dot(normed[...], held[...]).astype(BF).reshape(grads.shape)
        grad_in[...] = grad_in[...] + back_dot(held[...], w[0])
        sums[pl.ds(kind, 1)] = jnp.sum(held[...].astype(F32), axis=0, keepdims=True)

    for z in range(shards // 2):
        own[0, z] = grads[z, at[1]]
        other[0, z] = grads[z, at[1] ^ 1]

    @pl.when(kind == 3)
    def _():
        hat, inverse = normalized(tokens[...].astype(F32))
        back, grad_gain, grad_bias = norm_back(hat, inverse, vectors[0:1, :model], grad_in[...])
        grad_out[...] = (grad_base[...] + back).astype(BF)
        qkv = jnp.concatenate([sums[t : t + 1] for t in (1, 2, 3)], axis=1)
        whole = [
            grad_gain, grad_bias, sums_two[0:1], sums_two[1:2], sums_two[2:3], qkv, grad_b[0:1],
            grad_b[1:2],
        ]
        lines[...] = jnp.zeros_like(lines)
        for index, line in enumerate(whole):
            size = line.shape[1] // shards
            for f in range(shards):
                lines[f // 2, f % 2, index : index + 1, :size] = line[:, f * size : (f + 1) * size]
        for z in range(shards // 2):
            line_own[z] = lines[z, at[1]]
            line_other[z] = lines[z, at[1] ^ 1]


def finish(n, me, core, answers, tokens, cot, vectors, base, grad_base, w, sums_two, grad_b, shards, used):
    rows, model = tokens.shape
    block_len, width = answers[0].shape[1:]
    whole = pl.BlockSpec((rows, model), lambda kind, at: (0, 0))
    own_rows = model // shards

    def unit(kind, at):
        return lax.rem(kind + 3, 4)

    half = pl.BlockSpec(
        (1, shards // 2, own_rows, model), lambda kind, at: (unit(kind, at), 0, 0, 0)
    )
    half_shape = jax.ShapeDtypeStruct((4, shards // 2, own_rows, model), BF)
    half_lines = pl.BlockSpec((shards // 2, 8, model), lambda kind, at: (0, 0, 0))
    half_lines_shape = jax.ShapeDtypeStruct((shards // 2, 8, model), F32)
    return pl.pallas_call(
        functools.partial(finish_kernel, n, block_len, used, shards),
        grid_spec=pltpu.PrefetchScalarGridSpec(
            num_scalar_prefetch=1,
            grid=(4,),
            in_specs=[pl.BlockSpec((1, block_len, width), lambda kind, at: (kind, 0, 0))] * n
            + [
                whole,
                whole,
                pl.BlockSpec(vectors.shape, lambda kind, at: (0, 0)),
                whole,
                whole,
                pl.BlockSpec((1, model, model), lambda kind, at: (unit(kind, at), 0, 0)),
                pl.BlockSpec((8, model), lambda kind, at: (0, 0)),
                pl.BlockSpec(grad_b.shape, lambda kind, at: (0, 0)),
            ],
            out_specs=[whole, whole, half, half, half_lines, half_lines],
            scratch_shapes=[
                pltpu.VMEM((rows, model), BF),
                pltpu.VMEM((model, rows), BF),
                pltpu.VMEM((shards // 2, 2, own_rows, model), BF),
                pltpu.VMEM((rows, model), F32),
                pltpu.VMEM((8, model), F32),
                pltpu.VMEM((shards // 2, 2, 8, model), F32),
            ],
        ),
        out_shape=[
            jax.ShapeDtypeStruct((rows, model), BF),
            jax.ShapeDtypeStruct((rows, model), BF),
            half_shape,
            half_shape,
            half_lines_shape,
            half_lines_shape,
        ],
        compiler_params=pltpu.CompilerParams(vmem_limit_bytes=VMEM),
        cost_estimate=pl.CostEstimate(
            flops=16 * rows * model * model, bytes_accessed=40 * rows * model, transcendentals=0
        ),
        name="finish",
    )(
        jnp.stack([me, core]).astype(jnp.int32),
        *answers, tokens, cot, vectors, base, grad_base, w, sums_two, grad_b,
    )


def swap(value, shift, n):
    return lax.ppermute(value, "ctx", [(i, i ^ shift) for i in range(n)])


def swap_shard(value, shift, m):
    return lax.ppermute(value, "fsdp", [(i, i ^ shift) for i in range(m)])


def pack_kernel(q, qkv, out_w, *refs):
    out = refs[-1]
    rows = out_w.shape[0]
    out[:rows] = jnp.where(q[0] < 3, qkv[...].astype(F32), out_w[...].astype(F32)).astype(BF)
    lines = []
    for ref in refs[:-1]:
        line = ref[...].astype(F32).reshape(1, -1)
        lines.append(jnp.concatenate([line, jnp.zeros((1, out.shape[1] - line.shape[1]), F32)], axis=1))
    lines.append(jnp.zeros((out.shape[0] - rows - len(lines), out.shape[1]), F32))
    out[rows:] = jnp.concatenate(lines, axis=0).astype(BF)


def pack(q, qkv, out_w, vectors):
    rows, model = out_w.shape
    lines = [v.reshape(1, -1) if v.shape[0] < LANES else v for v in vectors]
    return pl.pallas_call(
        pack_kernel,
        grid_spec=pltpu.PrefetchScalarGridSpec(
            num_scalar_prefetch=1,
            grid=(1,),
            in_specs=[
                pl.BlockSpec((rows, model), lambda i, at: (0, jnp.minimum(at[0], 2))),
                pl.BlockSpec((rows, model), lambda i, at: (0, 0)),
            ]
            + [pl.BlockSpec(v.shape, lambda i, at, r=v.ndim: (0,) * r) for v in lines],
            out_specs=pl.BlockSpec((rows + 16, model), lambda i, at: (0, 0)),
        ),
        out_shape=jax.ShapeDtypeStruct((rows + 16, model), BF),
        name="pack",
    )(q.astype(jnp.int32).reshape(1), qkv, out_w, *lines)


def unpack_kernel(sizes, half, at, own, other, out):
    chips = own.shape[0]
    out[...] = jnp.zeros_like(out)
    rows = []
    for f in range(2 * chips):
        rel = f ^ at[0]
        both = jnp.where(rel % 2 == 0, own[rel // 2].astype(F32), other[rel // 2].astype(F32))
        rows.append(both)
    for index, size in enumerate(sizes):
        if index == half + 1:
            continue
        if index == half:
            cut = size // 2
            for h in range(2):
                line = [r[index : index + 1, h * cut : (h + 1) * cut] for r in rows]
                out[index + h : index + h + 1, : len(rows) * cut] = jnp.concatenate(line, axis=1)
        else:
            line = [r[index : index + 1, :size] for r in rows]
            out[index : index + 1, : len(rows) * size] = jnp.concatenate(line, axis=1)


def unpack(f, own, other, sizes, half):
    width = 2 * own.shape[0] * max(sizes[:half] + [sizes[half] // 2])
    full = pl.BlockSpec(own.shape, lambda i, at: (0, 0, 0))
    return pl.pallas_call(
        functools.partial(unpack_kernel, sizes, half),
        grid_spec=pltpu.PrefetchScalarGridSpec(
            num_scalar_prefetch=1,
            grid=(1,),
            in_specs=[full, full],
            out_specs=pl.BlockSpec((16, width), lambda i, at: (0, 0)),
        ),
        out_shape=jax.ShapeDtypeStruct((16, width), F32),
        name="unpack",
    )(f.astype(jnp.int32).reshape(1), own, other)


def along_z(mine, m):
    return [swap_shard(mine, step, m) for step in range(2, m, 2)]


def between_columns(along, n):
    return [along] + [swap(along, shift, n) for shift in range(1, n)]


def assemble_kernel(where, at, *refs):
    out = refs[-1]
    for piece, index, place in where:
        unit, shard = place(at)
        out[shard, unit] = refs[piece][index]


def assemble(at, pieces, n, m):
    where = []
    for unit in range(n):
        where.append((0, unit, lambda at, unit=unit: (unit, at[1])))
        where.append((1, unit, lambda at, unit=unit: (unit, at[1] ^ 1)))
    for core in range(2):
        for shift in range(n):
            for index in range(m // 2 - 1):
                where.append(
                    (
                        2 + core * n + shift,
                        index,
                        lambda at, shift=shift, flip=2 * (index + 1) ^ core: (at[0] ^ shift, at[1] ^ flip),
                    )
                )
    full = (m, n) + pieces[0].shape[1:]
    return pl.pallas_call(
        functools.partial(assemble_kernel, where),
        grid_spec=pltpu.PrefetchScalarGridSpec(
            num_scalar_prefetch=1,
            grid=(1,),
            in_specs=[pl.BlockSpec(p.shape, lambda i, at: (0, 0, 0)) for p in pieces],
            out_specs=pl.BlockSpec(full, lambda i, at: (0, 0, 0, 0)),
        ),
        out_shape=jax.ShapeDtypeStruct(full, pieces[0].dtype),
        compiler_params=pltpu.CompilerParams(vmem_limit_bytes=VMEM),
        name="assemble",
    )(at, *pieces)


def add_up(*pieces):
    return sum(p.astype(F32) for p in pieces).astype(BF)


def pick(value, at, axis=0):
    return lax.dynamic_index_in_dim(value, at, axis, keepdims=False)


def swapped(value, n):
    return [value] + [swap(value, s, n) for s in range(1, n)]


def ctx_step(halves, i, n):
    steps = [2**i for i in range(n.bit_length() - 1)]
    return [(value, swap(value, steps[(i + j) % len(steps)], n)) for j, value in enumerate(halves)]


def ctx_sum(halves, begin, n):
    terms = halves
    for i in range(begin, n.bit_length() - 1):
        terms = ctx_step([add_up(*t) for t in terms] if i else terms, i, n)
    return [term for half in terms for term in half]


def lay_kernel(shards, *refs):
    up, down = refs[8:]
    model = up.shape[1] // 4
    size = up.shape[1] // shards // 2
    ups = []
    for h in range(2):
        terms = refs[4 * h : 4 * h + 4]
        total = terms[0][...].astype(F32) + terms[1][...].astype(F32)
        ups.append(jnp.concatenate([total[0], total[1]], axis=1))
        rows = down.shape[0] // 4
        for unit in range(2):
            at = (2 * h + unit) * rows
            down[at : at + rows] = terms[2][unit].astype(F32) + terms[3][unit].astype(F32)
    for f in range(shards):
        line = [ups[h][:, f * size : (f + 1) * size] for h in range(2)]
        up[:, 2 * f * size : 2 * (f + 1) * size] = jnp.concatenate(line, axis=1)


def lay(first, second, shards, up_shape, down_shape):
    return pl.pallas_call(
        functools.partial(lay_kernel, shards),
        out_shape=[jax.ShapeDtypeStruct(up_shape, F32), jax.ShapeDtypeStruct(down_shape, F32)],
        compiler_params=pltpu.CompilerParams(vmem_limit_bytes=VMEM),
        name="lay",
    )(*first, *second)


def in_order(pieces, at):
    stacked = jnp.stack(pieces)
    return jnp.stack([pick(stacked, at ^ place) for place in range(len(pieces))])


def body(
    tokens,
    norm1_gain,
    norm1_bias,
    norm2_gain,
    norm2_bias,
    qkv_weight,
    qkv_bias,
    out_weight,
    out_bias,
    up_weight,
    up_bias,
    down_weight,
    down_bias,
    cotangent,
):
    block_len, seq_count, model = tokens.shape
    n = lax.axis_size("ctx")
    shards = lax.axis_size("fsdp")
    rows = block_len * seq_count
    hidden = up_weight.shape[1]
    me = lax.axis_index("ctx")
    me_arr = me.astype(jnp.int32).reshape(1)
    width = -(-seq_count * model // (n * LANES)) * LANES
    used = seq_count * model // width
    per = model // width

    parts = n // 4
    own_rows = out_weight.shape[0]

    vectors = (
        norm1_gain, norm1_bias, norm2_gain, norm2_bias, qkv_bias, out_bias, up_bias, out_bias,
        down_bias,
    )
    sizes = [v.shape[0] for v in vectors]
    per_shard = hidden // shards // 2

    def half_weights(h):
        up = up_weight.reshape(own_rows, shards, 2, per_shard)[:, :, h].reshape(own_rows, -1, model)
        down = down_weight[h * per_shard : (h + 1) * per_shard].reshape(-1, own_rows, model)
        return jnp.concatenate([up.transpose(1, 0, 2), down], axis=0)

    units = jnp.concatenate(
        [qkv_weight[None, :, t * model : (t + 1) * model] for t in range(3)] + [out_weight[None]]
    ).reshape(n, own_rows // parts, model)
    if n == 4:
        mine = pack(me, qkv_weight, out_weight, vectors)
    else:
        lines = [jnp.pad(v, (0, model - v.shape[0])) for v in vectors]
        lines = jnp.pad(jnp.stack(lines), ((0, 16 - len(vectors)), (0, 0)))
        mine = jnp.concatenate([pick(units, me), lines], axis=0)
    mine_rows = units.shape[1]
    came = along_z(mine, shards)
    along_units = jnp.stack([c[:mine_rows] for c in came])
    chips = jnp.stack([c[mine_rows:] for c in [mine] + came])
    first_half, _ = lax.optimization_barrier((half_weights(0), along_units))
    w_first = lax.all_gather(first_half, "fsdp", axis=0, tiled=False)
    unit_columns = between_columns(along_units, n)
    vectors = unpack(
        lax.axis_index("fsdp"), chips, swap_shard(chips, 1, shards), sizes, 6
    )
    inputs = tokens.transpose(1, 0, 2).reshape(rows, model)
    cot = cotangent.transpose(1, 0, 2).reshape(rows, model)
    vectors, inputs, cot, unit_columns = lax.optimization_barrier((vectors, inputs, cot, unit_columns))
    crossed = [swap_shard(held, 1, shards) for held in unit_columns]
    unit_pieces = [units, swap_shard(units, 1, shards)] + unit_columns + crossed

    tables = rotary_tables(n * block_len)
    def shard_sum(value):
        return lax.psum_scatter(value, "fsdp", scatter_dimension=0, tiled=False)

    at = jnp.stack([me, lax.axis_index("fsdp")]).astype(jnp.int32)
    *sent, w_units = project(
        n, shards, at, inputs, cot, vectors, unit_pieces, tables, block_len, width, used
    )
    pieces = [sent[0]] + [swap(sent[shift], shift, n) for shift in range(1, n)]
    mlp_inputs, second_half, _ = lax.optimization_barrier(
        (inputs, half_weights(1), (sent, w_first))
    )
    second_units = second_half.reshape(n, -1, model)
    along_second = along_z(pick(second_units, me), shards)
    base, grad_base, grad_up, grad_down, grad_b_first = mlp(
        mlp_inputs, cot, vectors, w_first
    )
    first_grads, pieces = lax.optimization_barrier(
        (jnp.concatenate([grad_up, grad_down], axis=1), pieces)
    )
    first_shard = shard_sum(first_grads)
    second_columns = between_columns(jnp.stack(along_second), n)
    made = attend(n, me_arr, pieces, tables)
    mlp_inputs, second_columns, second_units, _ = lax.optimization_barrier(
        (inputs, second_columns, second_units, made)
    )
    second_pieces = [second_units, swap_shard(second_units, 1, shards)] + second_columns
    second_pieces += [swap_shard(held, 1, shards) for held in second_columns]
    w_second = assemble(at, second_pieces, n, shards).reshape(shards, 4, own_rows, model)
    answers = [made[0]] + [swap(made[shift], shift, n) for shift in range(1, n)]
    base, grad_base, grad_up, grad_down, grad_b_second, sums_two = mlp(
        mlp_inputs, cot, vectors, w_second, start=(base, grad_base)
    )
    second_grads, answers = lax.optimization_barrier(
        (jnp.concatenate([grad_up, grad_down], axis=1), answers)
    )
    second_shard = shard_sum(second_grads)
    core = lax.axis_index("fsdp") % 2
    layer_out, tokens_grad, own, other, line_own, line_other = finish(
        n, me, core, answers, inputs, cot, vectors, base, grad_base, w_units, sums_two,
        jnp.concatenate([grad_b_first, grad_b_second]), shards, used,
    )

    def placed(value):
        return value.reshape(seq_count, block_len, model).transpose(1, 0, 2)

    z = lax.axis_index("fsdp") // 2
    chip = add_up(own, swap_shard(other, 1, shards))
    line_chip = add_up(line_own, swap_shard(line_other, 1, shards))
    chip = jnp.concatenate([chip, jnp.pad(line_chip[None], ((0, 3), (0, 0), (0, 0), (0, 0)))], axis=2)
    chip = (
        chip.reshape(4, shards // 2, parts, -1, model)
        .transpose(0, 2, 1, 3, 4)
        .reshape(n, shards // 2, -1, model)
    )
    unit = add_up(pick(chip, me), *[swap(pick(chip, me ^ s), s, n) for s in range(1, n)])
    unit, first_shard, second_shard = lax.optimization_barrier((unit, first_shard, second_shard))
    first_sum = ctx_sum([first_shard[:2], first_shard[2:]], 0, n)
    second_sum = ctx_sum([second_shard[:2], second_shard[2:]], 0, n)
    mine = add_up(
        pick(unit, z),
        *[swap_shard(pick(unit, z ^ s), 2 * s, shards) for s in range(1, shards // 2)],
    )
    unit_all = swapped(mine, n)
    part_units = in_order(unit_all, me).reshape(4, -1, model).astype(F32)
    line_sums = part_units[0, own_rows:]
    part_units = part_units[:, :own_rows]
    part_qkv = jnp.concatenate([part_units[t] for t in range(3)], axis=1)
    part_up, part_down = lay(first_sum, second_sum, shards, up_weight.shape, down_weight.shape)
    sizes = [own_rows] * 5 + [3 * own_rows, per_shard, per_shard]
    gain1, bias1, gain2, bias2, columns, qkv_b, *up_b = [
        line_sums[index, :size] for index, size in enumerate(sizes)
    ]
    return (
        placed(layer_out), placed(tokens_grad), gain1, bias1, gain2, bias2, part_qkv, qkv_b,
        part_units[3], columns, part_up, jnp.concatenate(up_b), part_down, columns,
    )


def solution(mesh):
    blocks = P("ctx", "fsdp", None)
    line, matrix = P("fsdp"), P("fsdp", None)
    return jax.shard_map(
        body,
        mesh=mesh,
        in_specs=(
            blocks, line, line, line, line, matrix, line, matrix, line, matrix, line, matrix, line,
            blocks,
        ),
        out_specs=(
            blocks, blocks, line, line, line, line, matrix, line, matrix, line, matrix, line,
            matrix, line,
        ),
        check_vma=False,
    )
```
